128 devices in a mesh: gx: 16 (over x, z), gy: 8 (over y, core).
Axes of the slice: x: 4, y: 4, z: 4, core: 2. Of those that a mesh axis runs over, the one named last changes fastest.
Arguments:
- tracers: float32 [2, 16, 2048, 1024], P(None, None, 'gx', 'gy'), may hold values from -6 to 6
- east_flow: bfloat16 [16, 2048, 1024], P(None, 'gx', 'gy'), may hold values from -0.14941406 to 0.14941406
- north_flow: bfloat16 [16, 2048, 1024], P(None, 'gx', 'gy'), may hold values from -0.14941406 to 0.14941406
- levels: int32 [2048, 1024], P('gx', 'gy'), may hold values from 0 to 16, as said below
Outputs:
- new_tracers: float32 [2, 16, 2048, 1024], P(None, None, 'gx', 'gy')
- pressure: float32 [2048, 1024], P('gx', 'gy')
The draws below stay inside these ranges and needn't reach their ends.
Inputs may be any that keep to these rules, and one draw needn't show every extreme that they name: Land (0) comes in patches, more of it to the east; every ocean column has 1 to 16 levels.
All inputs are finite; a program needn't handle non-finite values.
Results may differ from the reference program's by a relative error of at most 0.0003.
Values may be sent and summed in bfloat16 or wider, within the bound.
No kernel may reach another device: no remote copies, remote signals or barrier semaphores. Data moves between devices by JAX's collectives and lax.ppermute only.
A program may use at most 128 MiB of HBM per device.

```python
import jax
import jax.numpy as jnp
from jax import lax

KL = 16
NSTEP = 2
ITERS = 3
NX = 2048
NY = 1024


def draw_levels(key, part):
    key = jax.random.fold_in(key, 11)
    coarse_key, depth_key = jax.random.split(key)
    coarse_x = NX // 8
    coarse_y = NY // 8
    column_index = jnp.arange(coarse_x, dtype=jnp.int32)[:, None]
    threshold = 1 + 6 * column_index // coarse_x
    coarse = jax.random.randint(coarse_key, (coarse_x, coarse_y), 0, 8, dtype=jnp.int32)
    land = coarse < threshold
    land = jnp.repeat(jnp.repeat(land, 8, axis=0), 8, axis=1)
    depth = jax.random.randint(depth_key, (NX, NY), 1, KL + 1, dtype=jnp.int32)
    return jnp.where(land, 0, depth).astype(jnp.int32)


def block_levels(own_key, shape, pieces, low, top_value):
    def one(dim, parts):
        steps = jax.random.uniform(jax.random.fold_in(jax.random.fold_in(own_key, 6), dim), (parts,), jnp.float32, low / len(pieces), top_value / len(pieces))
        return jnp.repeat(jnp.exp(steps), shape[dim] // parts).reshape((-1,) + (1,) * (len(shape) - dim - 1))

    level = one(*pieces[0])
    for cut in pieces[1:]:
        level = level * one(*cut)
    return level


def normal_values(own_key, extent, spread, limit, shards=(), kind=jnp.bfloat16):
    array = spread * jax.random.normal(own_key, extent, jnp.float32)
    if shards:
        array = array * block_levels(own_key, extent, shards, -0.22, 0.18)
    return jnp.clip(array, -limit, limit).astype(kind)


def setup_inputs(seed: int = 0) -> dict:
    key_of = jax.random.split(jax.random.key(seed), 5)
    tracers = normal_values(key_of[0], (2, KL, NX, NY), 1.0, 6.0, ((2, 16), (3, 8)), jnp.float32)
    east_flow = jnp.clip(jax.random.uniform(key_of[1], (KL, NX, NY), jnp.float32, -0.14941406, 0.14941406) * block_levels(key_of[1], (KL, NX, NY), ((1, 16), (2, 8)), -0.4, 0.0), -0.14941406, 0.14941406).astype(jnp.bfloat16)
    north_flow = jnp.clip(jax.random.uniform(key_of[2], (KL, NX, NY), jnp.float32, -0.14941406, 0.14941406) * block_levels(key_of[2], (KL, NX, NY), ((1, 16), (2, 8)), -0.4, 0.0), -0.14941406, 0.14941406).astype(jnp.bfloat16)
    levels = draw_levels(jax.random.fold_in(key_of[4], 71), 0)
    return {"tracers": tracers, "east_flow": east_flow, "north_flow": north_flow, "levels": levels}


KAPPA = 0.08
ALPHA = 0.05


def shift_north(field):
    return jnp.concatenate([field[..., 1:], jnp.zeros_like(field[..., :1])], axis=-1)


def shift_south(field):
    return jnp.concatenate([jnp.zeros_like(field[..., :1]), field[..., :-1]], axis=-1)


def level_update(level_index, tracers, east_flow, north_flow, levels):
    column = lax.dynamic_index_in_dim(tracers, level_index, axis=1, keepdims=False)
    east_speed = lax.dynamic_index_in_dim(east_flow, level_index, axis=0, keepdims=False).astype(jnp.float32)
    north_speed = lax.dynamic_index_in_dim(north_flow, level_index, axis=0, keepdims=False).astype(jnp.float32)
    wet = (level_index < levels).astype(jnp.float32)
    open_east = wet * jnp.roll(wet, -1, axis=0)
    open_north = wet * shift_north(wet)
    east_face = east_speed * open_east
    north_face = north_speed * open_north
    for step_index in range(NSTEP):
        east_value = jnp.roll(column, -1, axis=1)
        north_value = shift_north(column)
        east_flux = jnp.maximum(east_face, 0.0) * column + jnp.minimum(east_face, 0.0) * east_value - KAPPA * open_east * (east_value - column)
        north_flux = jnp.maximum(north_face, 0.0) * column + jnp.minimum(north_face, 0.0) * north_value - KAPPA * open_north * (north_value - column)
        column = (column - (east_flux - jnp.roll(east_flux, 1, axis=1)) - (north_flux - shift_south(north_flux))) * wet
    forcing_term = wet * (column[0] - 0.8 * column[1])
    return column, forcing_term


def reference(tracers, east_flow, north_flow, levels):
    def one_level(level_index):
        return level_update(level_index, tracers, east_flow, north_flow, levels)

    columns, terms = lax.map(one_level, jnp.arange(KL, dtype=jnp.int32))
    new_tracers = jnp.moveaxis(columns, 0, 1)
    forcing = 0.25 * jnp.sum(terms, axis=0)
    depth = levels.astype(jnp.float32) / KL
    ocean = (levels > 0).astype(jnp.float32)
    east_coef = jnp.minimum(depth, jnp.roll(depth, -1, axis=0))
    west_coef = jnp.roll(east_coef, 1, axis=0)
    north_coef = jnp.minimum(depth, shift_north(depth))
    south_coef = shift_south(north_coef)
    diagonal = ALPHA * depth + (1.0 - ocean) + east_coef + west_coef + north_coef + south_coef

    def operate(field):
        return diagonal * field - east_coef * jnp.roll(field, -1, axis=0) - west_coef * jnp.roll(field, 1, axis=0) - north_coef * shift_north(field) - south_coef * shift_south(field)

    solution = jnp.zeros_like(forcing)
    residual = forcing
    precond = residual / diagonal
    direction = precond
    rz_now = jnp.sum(residual * precond)
    for step_index in range(ITERS):
        image = operate(direction)
        alpha = rz_now / jnp.sum(direction * image)
        solution = solution + alpha * direction
        residual = residual - alpha * image
        precond = residual / diagonal
        rz_next = jnp.sum(residual * precond)
        direction = precond + (rz_next / rz_now) * direction
        rz_now = rz_next
    return new_tracers, solution
```

```python
import functools

import jax
import jax.numpy as jnp
from jax import lax
from jax.experimental import pallas as pl
from jax.experimental.pallas import tpu as pltpu
from jax.sharding import PartitionSpec as P

KAPPA = 0.08
ALPHA = 0.05
F32 = jnp.float32

SX = 128
SY = 128
KL = 16
EDGE = 8
PAD = 16
ROWS = SX + 2 * PAD
WIDE = SX + 2 * EDGE
LOW = PAD - EDGE
ARRAYS = 2 * KL + 2 * KL + 1
VMEM = 48 * 1024 * 1024


def lanes(shape=(8, 128)):
    return lax.broadcasted_iota(jnp.int32, shape, len(shape) - 1)


def edges_kernel(t_lo, t_hi, e_lo, e_hi, n_lo, n_hi, d_lo, d_hi, out_lo, out_hi):
    for t, e, n, d, out, at in (
        (t_lo, e_lo, n_lo, d_lo, out_lo, 0),
        (t_hi, e_hi, n_hi, d_hi, out_hi, 8),
    ):
        for k in range(KL):
            out[k] = t[0, k]
            out[KL + k] = t[1, k]
            out[2 * KL + k] = e[k].astype(F32)[at : at + 8]
            out[3 * KL + k] = n[k].astype(F32)[at : at + 8]
        out[4 * KL] = d[...].astype(F32)


def edges(tracers, east, north, levels):
    def spec(shape, at, dim):
        index = [0] * len(shape)
        index[dim] = at
        return pl.BlockSpec(shape, lambda i, index=tuple(index): index)

    t = (2, KL, 8, SY)
    f = (KL, 16, SY)
    d = (8, SY)
    out = jax.ShapeDtypeStruct((ARRAYS, 8, SY), F32)
    whole = pl.BlockSpec((ARRAYS, 8, SY), lambda i: (0, 0, 0))
    return pl.pallas_call(
        edges_kernel,
        grid=(1,),
        in_specs=[
            spec(t, 0, 2),
            spec(t, SX // 8 - 1, 2),
            spec(f, 0, 1),
            spec(f, SX // 16 - 1, 1),
            spec(f, 0, 1),
            spec(f, SX // 16 - 1, 1),
            spec(d, 0, 0),
            spec(d, SX // 8 - 1, 0),
        ],
        out_specs=[whole, whole],
        out_shape=[out, out],
        compiler_params=pltpu.CompilerParams(vmem_limit_bytes=VMEM),
        name="edges",
    )(tracers, tracers, east, east, north, north, levels, levels)


def pack(slices, rows):
    group = lanes((rows, 128)) // 8
    one = jnp.zeros((rows, 128), F32)
    two = jnp.zeros((rows, 128), F32)
    for k in range(KL):
        value = slices(k)
        here = group == k
        one = jnp.where(here, pltpu.roll(value, (8 * k - 123) % 128, 1), one)
        two = jnp.where(here, pltpu.roll(value, (8 * k - 125) % 128, 1), two)
    return one, two


def pack_kernel(t, e, n, d, one, two):
    chunk = 16

    def body(i, carry):
        rows = pl.ds(pl.multiple_of(i * chunk, chunk), chunk)
        out = pl.ds(pl.multiple_of(i * chunk + EDGE, 8), chunk)
        sources = (
            lambda k: t[0, k, rows, :],
            lambda k: t[1, k, rows, :],
            lambda k: e[k, rows, :].astype(F32),
            lambda k: n[k, rows, :].astype(F32),
            lambda k: d[rows, :].astype(F32),
        )
        for a, source in enumerate(sources):
            one[a, out, :], two[a, out, :] = pack(source, chunk)
        return carry

    lax.fori_loop(0, SX // chunk, body, 0)
    for ref in (one, two):
        ref[:, 0:EDGE, :] = jnp.zeros((5, EDGE, 128), F32)
        ref[:, WIDE - EDGE : WIDE, :] = jnp.zeros((5, EDGE, 128), F32)


def pack_rows(tracers, east, north, levels):
    out = jax.ShapeDtypeStruct((5, WIDE, 128), F32)
    return pl.pallas_call(
        pack_kernel,
        out_shape=[out, out],
        compiler_params=pltpu.CompilerParams(vmem_limit_bytes=VMEM),
        name="pack_rows",
    )(tracers, east, north, levels)


def pack_edges_kernel(low, high, one_in, two_in, one, two):
    one[:, EDGE : WIDE - EDGE, :] = one_in[:, EDGE : WIDE - EDGE, :]
    two[:, EDGE : WIDE - EDGE, :] = two_in[:, EDGE : WIDE - EDGE, :]
    for ref, at in ((low, 0), (high, WIDE - EDGE)):
        for a in range(5):
            base = KL * a
            source = (lambda k: ref[base + k]) if a < 4 else (lambda k: ref[base])
            one[a, at : at + 8, :], two[a, at : at + 8, :] = pack(source, 8)


def pack_edges(low, high, one, two):
    out = jax.ShapeDtypeStruct((5, WIDE, 128), F32)
    return pl.pallas_call(
        pack_edges_kernel,
        out_shape=[out, out],
        compiler_params=pltpu.CompilerParams(vmem_limit_bytes=VMEM),
        name="pack_edges",
    )(low, high, one, two)


GROUPS = tuple(range(LOW, LOW + WIDE, 8))


def rows_at(row):
    return slice(row, row + 8)


def ocean_kernel(
    tracers, east, north, levels, low, high, one, two, one_in, two_in, count,
    new, w0_out, w1_out, w2_out, sums_out,
    depth, low_east, low_north, strip_q, strip_depth, strip_flow, edge_q, edge_a, edge_b,
    q0, q1, flow, coef, total, strip_total, field, grid,
):
    lane = lanes()
    member = lane % 8
    strip_level = (lane // 8).astype(F32)
    first = lax.axis_index("gy") == 0
    last = lax.axis_index("gy") == count - 1

    for g in GROUPS:
        r = g - LOW
        if r < EDGE:
            value = low[4 * KL]
        elif r >= WIDE - EDGE:
            value = high[4 * KL]
        else:
            value = levels[rows_at(r - EDGE), :].astype(F32)
        depth[rows_at(g), :] = value
        rows = rows_at(r)
        for a in range(5):
            from_low = one_in[a, rows, :]
            from_high = two_in[a, rows, :]
            if a == 4:
                from_low = jnp.where(first, 0.0, from_low)
                from_high = jnp.where(last, 0.0, from_high)
            low_strip = jnp.where(member < 5, from_low, one[a, rows, :])
            high_strip = jnp.where(member >= 3, from_high, two[a, rows, :])
            for side, value in enumerate((low_strip, high_strip)):
                if a < 2:
                    strip_q[side, a, 0, rows_at(g), :] = value
                elif a < 4:
                    strip_flow[side, a - 2, rows_at(g), :] = value
                else:
                    strip_depth[side, rows_at(g), :] = value
    blank = jnp.zeros((8, 128), F32)
    for outside in (LOW - 8, LOW + WIDE):
        depth[rows_at(outside), :] = blank
        strip_depth[0, rows_at(outside), :] = blank
        strip_depth[1, rows_at(outside), :] = blank

    def merge(low_value, high_value):
        return jnp.where(member == 4, low_value, high_value)

    def face_weights(face, flow_value, threshold):
        is_open = face > threshold
        ahead = jnp.where(is_open, KAPPA + jnp.maximum(flow_value, 0.0), 0.0)
        back = jnp.where(is_open, KAPPA - jnp.minimum(flow_value, 0.0), 0.0)
        return ahead, back

    def weights(depth_ref, face_east, face_north, flow_ref, coef_ref, threshold, south_edge):
        for g in GROUPS:
            rows = rows_at(g)
            a_east, b_east = face_weights(face_east(g), flow_ref[0, rows, :], threshold)
            a_north, b_north = face_weights(face_north(g), flow_ref[1, rows, :], threshold)
            coef_ref[0, rows, :] = a_east
            coef_ref[1, rows, :] = b_east
            coef_ref[2, rows, :] = b_north
            a_south, b_south = south_edge(g, a_north, b_north)
            coef_ref[3, rows, :] = a_south
            leaving = a_east + a_north + coef_ref[1, rows_at(g - 1), :] + b_south
            coef_ref[4, rows, :] = jnp.where(depth_ref[rows, :] > threshold, 1.0 - leaving, 0.0)

    def update(source, coef_ref, g, north_value, south_value):
        rows = rows_at(g)
        value = source[rows, :]
        return (
            coef_ref[4, rows, :] * value
            + coef_ref[1, rows, :] * source[rows_at(g + 1), :]
            + coef_ref[0, rows_at(g - 1), :] * source[rows_at(g - 1), :]
            + coef_ref[2, rows, :] * north_value(value)
            + coef_ref[3, rows, :] * south_value(value)
        )

    def ahead_one(value):
        return pltpu.roll(value, 127, 1)

    def back_one(value):
        return pltpu.roll(value, 1, 1)

    for side in range(2):
        sd = strip_depth.at[side]

        def face_east(g, sd=sd):
            return jnp.minimum(sd[rows_at(g), :], sd[rows_at(g + 1), :])

        def face_north(g, sd=sd):
            value = sd[rows_at(g), :]
            return jnp.minimum(value, ahead_one(value))

        def south_edge(g, a_north, b_north, side=side):
            if side == 0:
                edge_a[rows_at(g), :] = a_north
                edge_b[rows_at(g), :] = b_north
            return back_one(a_north), back_one(b_north)

        coef[1, rows_at(LOW - 8), :] = blank
        weights(sd, face_east, face_north, strip_flow.at[side], coef, strip_level, south_edge)
        for tracer in range(2):
            for g in GROUPS:
                strip_q[side, tracer, 1, rows_at(g), :] = update(
                    strip_q.at[side, tracer, 0], coef, g, ahead_one, back_one
                )
        for g in GROUPS:
            temperature, salinity = (
                update(strip_q.at[side, tracer, 1], coef, g, ahead_one, back_one) for tracer in range(2)
            )
            value = temperature - 0.8 * salinity
            for shift in (8, 16, 32, 64):
                value = value + pltpu.roll(value, shift, 1)
            strip_total[side, rows_at(g), :] = value
    for tracer in range(2):
        for step in range(2):
            for g in GROUPS:
                rows = rows_at(g)
                edge_q[tracer, step, rows, :] = merge(
                    strip_q[0, tracer, step, rows, :], strip_q[1, tracer, step, rows, :]
                )

    def beside(low_value, high_value):
        return jnp.where(lane >= 64, pltpu.roll(low_value, 3, 1), pltpu.roll(high_value, 125, 1))

    def northward(main, side):
        a, b = ahead_one(main), ahead_one(side)
        return jnp.where(lane == 127, b, a), jnp.where(lane == 127, a, b)

    def southward(main, side):
        a, b = back_one(main), back_one(side)
        return jnp.where(lane == 0, b, a), jnp.where(lane == 0, a, b)

    for g in GROUPS + (LOW - 8, LOW + WIDE):
        rows = rows_at(g)
        grid[0, 0, rows, :] = depth[rows, :]
        grid[0, 1, rows, :] = beside(strip_depth[0, rows, :], strip_depth[1, rows, :])
    for g in GROUPS:
        rows = rows_at(g)
        both = grid[0, 0, rows, :], grid[0, 1, rows, :]
        further = northward(*both)
        for part in range(2):
            grid[1, part, rows, :] = jnp.minimum(both[part], grid[0, part, rows_at(g + 1), :])
            grid[2, part, rows, :] = jnp.minimum(both[part], further[part])
        total[rows, :] = blank
    for part in range(2):
        grid[1, part, rows_at(LOW - 8), :] = blank

    def level(k, carry):
        threshold = k.astype(F32)
        turn = (120 + 4 - 8 * k) % 128
        turn = lax.rem(252 - 8 * k, 128)
        for g in GROUPS:
            r = g - LOW
            rows = rows_at(g)
            if r < EDGE or r >= WIDE - EDGE:
                ref = low if r < EDGE else high
                q0[0, rows, :] = ref[k]
                q0[1, rows, :] = ref[KL + k]
                flow[0, rows, :] = ref[2 * KL + k]
                flow[1, rows, :] = ref[3 * KL + k]
            else:
                q0[0, rows, :] = tracers[0, k, rows_at(r - EDGE), :]
                q0[1, rows, :] = tracers[1, k, rows_at(r - EDGE), :]
        flow[0, PAD : PAD + SX, :] = east[k].astype(F32)
        flow[1, PAD : PAD + SX, :] = north[k].astype(F32)

        def south_edge(g, a_north, b_north):
            a_edge = pltpu.roll(edge_a[rows_at(g), :], turn, 1)
            b_edge = pltpu.roll(edge_b[rows_at(g), :], turn, 1)
            return jnp.where(lane == 0, a_edge, back_one(a_north)), jnp.where(lane == 0, b_edge, back_one(b_north))

        weights(
            depth,
            lambda g: grid[1, 0, rows_at(g), :],
            lambda g: grid[2, 0, rows_at(g), :],
            flow,
            coef,
            threshold,
            south_edge,
        )

        def stepped(source, tracer, step, g):
            edge = pltpu.roll(edge_q[tracer, step, rows_at(g), :], turn, 1)
            return update(
                source,
                coef,
                g,
                lambda value: jnp.where(lane == 127, edge, ahead_one(value)),
                lambda value: jnp.where(lane == 0, edge, back_one(value)),
            )

        for tracer in range(2):
            for g in GROUPS:
                q1[tracer, rows_at(g), :] = stepped(q0.at[tracer], tracer, 0, g)
        for g in GROUPS:
            temperature = stepped(q1.at[0], 0, 1, g)
            salinity = stepped(q1.at[1], 1, 1, g)
            if PAD <= g < PAD + SX:
                new[0, k, rows_at(g - PAD), :] = temperature
                new[1, k, rows_at(g - PAD), :] = salinity
            total[rows_at(g), :] += temperature - 0.8 * salinity
        return carry

    lax.fori_loop(0, KL, level, 0)

    scale = 1.0 / KL
    for g in GROUPS:
        rows = rows_at(g)
        souths = southward(grid[2, 0, rows, :], grid[2, 1, rows, :])
        for part in range(2):
            here = grid[0, part, rows, :]
            own = ALPHA * scale * here + jnp.where(here == 0.0, 1.0, 0.0)
            faces = grid[1, part, rows, :] + grid[1, part, rows_at(g - 1), :] + grid[2, part, rows, :] + souths[part]
            diagonal = own + scale * faces
            grid[3, part, rows, :] = 1.0 / diagonal
            grid[4, part, rows, :] = own
            grid[5, part, rows, :] = diagonal
        forcing = 0.25 * total[rows, :]
        forcing_beside = 0.25 * beside(strip_total[0, rows, :], strip_total[1, rows, :])
        field[0, 0, rows, :] = forcing * grid[3, 0, rows, :]
        field[0, 1, rows, :] = forcing_beside * grid[3, 1, rows, :]
    for part in range(2):
        for outside in (LOW - 8, LOW + WIDE):
            for i in range(3):
                field[i, part, rows_at(outside), :] = blank

    moments = [blank] * 6
    for i in range(3):
        for g in GROUPS:
            rows = rows_at(g)
            both = field[i, 0, rows, :], field[i, 1, rows, :]
            norths = northward(*both)
            souths = southward(*both)
            south_faces = southward(grid[2, 0, rows, :], grid[2, 1, rows, :])
            for part in range(2):
                if i == 2 and part == 1:
                    continue
                here = both[part]
                east_gap = here - field[i, part, rows_at(g + 1), :]
                north_gap = here - norths[part]
                east_face = scale * grid[1, part, rows, :]
                north_face = scale * grid[2, part, rows, :]
                own = grid[4, part, rows, :]
                if part == 0 and PAD <= g < PAD + SX:
                    moments[2 * i] += grid[5, 0, rows, :] * here * here
                    moments[2 * i + 1] += (
                        own * here * here + east_face * east_gap * east_gap + north_face * north_gap * north_gap
                    )
                if i < 2:
                    image = (
                        own * here
                        + east_face * east_gap
                        + scale * grid[1, part, rows_at(g - 1), :] * (here - field[i, part, rows_at(g - 1), :])
                        + north_face * north_gap
                        + scale * south_faces[part] * (here - souths[part])
                    )
                    field[i + 1, part, rows, :] = image * grid[3, part, rows, :]
    row = jnp.zeros((8, 128), F32)
    for i in range(6):
        value = jnp.sum(jnp.sum(moments[i], axis=0, keepdims=True), axis=1, keepdims=True)
        row = jnp.where(lane == i, value, row)
    for g in range(0, 128, 8):
        sums_out[rows_at(g), :] = row
    for i, out in enumerate((w0_out, w1_out, w2_out)):
        out[...] = field[i, 0, PAD : PAD + SX, :]


def ocean(tracers, east, north, levels, low, high, one, two, one_in, two_in, count):
    tall = (ROWS, 128)
    plane = jax.ShapeDtypeStruct((SX, SY), F32)
    scratch = [
        tall,
        (8, 128),
        (8, 128),
        (2, 2, 2) + tall,
        (2,) + tall,
        (2, 2) + tall,
        (2, 2) + tall,
        tall,
        tall,
        (2,) + tall,
        (2,) + tall,
        (2,) + tall,
        (5,) + tall,
        tall,
        (2,) + tall,
        (3, 2) + tall,
        (6, 2) + tall,
    ]
    return pl.pallas_call(
        functools.partial(ocean_kernel_with, count),
        out_shape=[jax.ShapeDtypeStruct(tracers.shape, F32), plane, plane, plane, plane],
        scratch_shapes=[pltpu.VMEM(shape, F32) for shape in scratch],
        compiler_params=pltpu.CompilerParams(vmem_limit_bytes=VMEM),
        name="ocean",
    )(tracers, east, north, levels, low, high, one, two, one_in, two_in)


def ocean_kernel_with(count, *refs):
    return ocean_kernel(*refs[:10], count, *refs[10:])


def finish_kernel(sums, w0, w1, w2, out):
    value = sums[0:8, :]
    for g in range(8, 128, 8):
        value = value + sums[rows_at(g), :]
    value = jnp.sum(value, axis=0, keepdims=True)
    lane = lanes((1, 128))
    m0, m1, m2, m3, m4, m5 = (
        jnp.sum(jnp.where(lane == i, value, 0.0), axis=1, keepdims=True) for i in range(6)
    )
    floor = 4e-7
    l10 = m2 / m1
    l20 = m3 / m1
    d1 = m3 - l10 * m2
    t = m4 - l20 * m2
    has1 = d1 > floor * m3
    l21 = jnp.where(has1, t / d1, 0.0)
    d2 = m5 - l20 * m3 - l21 * t
    has2 = has1 & (d2 > floor * m5)
    y1 = m1 - l10 * m0
    y2 = m2 - l20 * m0 - l21 * y1
    c2 = jnp.where(has2, y2 / d2, 0.0)
    c1 = jnp.where(has1, y1 / d1, 0.0) - l21 * c2
    c0 = m0 / m1 - l10 * c1 - l20 * c2
    for g in range(0, SX, 8):
        rows = rows_at(g)
        out[rows, :] = c0 * w0[rows, :] + c1 * w1[rows, :] + c2 * w2[rows, :]


def finish(sums, w0, w1, w2):
    return pl.pallas_call(
        finish_kernel,
        out_shape=jax.ShapeDtypeStruct((SX, SY), F32),
        name="finish",
    )(sums, w0, w1, w2)


def shift(array, axis, step):
    count = lax.axis_size(axis)
    return lax.ppermute(array, axis, [(i, (i + step) % count) for i in range(count)])


def on_device(tracers, east, north, levels):
    first, final = edges(tracers, east, north, levels)
    high = shift(first, "gx", -1)
    low = shift(final, "gx", 1)
    one, two = pack_rows(tracers, east, north, levels)
    one, two = pack_edges(low, high, one, two)
    one_in = shift(one, "gy", 1)
    two_in = shift(two, "gy", -1)
    new, w0, w1, w2, sums = ocean(
        tracers, east, north, levels, low, high, one, two, one_in, two_in, lax.axis_size("gy")
    )
    sums = lax.all_to_all(sums, ("gx", "gy"), split_axis=0, concat_axis=0, tiled=True)
    return new, finish(sums, w0, w1, w2)


def solution(mesh):
    placed = (P(None, None, "gx", "gy"), P(None, "gx", "gy"), P(None, "gx", "gy"), P("gx", "gy"))
    return jax.shard_map(
        on_device,
        mesh=mesh,
        in_specs=placed,
        out_specs=(P(None, None, "gx", "gy"), P("gx", "gy")),
        check_vma=False,
    )
```

```python
import functools

import jax
import jax.numpy as jnp
from jax import lax
from jax.experimental import pallas as pl
from jax.experimental.pallas import tpu as pltpu
from jax.sharding import PartitionSpec as P

KAPPA = 0.08
ALPHA = 0.05
F32 = jnp.float32

SX = 128
SY = 128
KL = 16
EDGE = 8
PAD = 16
ROWS = SX + 2 * PAD
WIDE = SX + 2 * EDGE
LOW = PAD - EDGE
ARRAYS = 2 * KL + 2 * KL + 1
VMEM = 40 * 1024 * 1024
GROUPS = tuple(range(LOW, LOW + WIDE, 8))
OUTSIDE = (LOW - 8, LOW + WIDE)
SENT = 3


def params(limit=VMEM):
    return pltpu.CompilerParams(vmem_limit_bytes=limit)


def rows_at(row):
    return slice(row, row + 8)


def lanes(shape=(8, 128)):
    return lax.broadcasted_iota(jnp.int32, shape, len(shape) - 1)


def ahead_one(value):
    return pltpu.roll(value, 127, 1)


def back_one(value):
    return pltpu.roll(value, 1, 1)


def edges_kernel(t, e, n, d, out_lo, out_hi, flows, depths, sems):
    copies = []
    for side, (out, at) in enumerate(((out_lo, 0), (out_hi, SX - 8))):
        at16 = 0 if side == 0 else SX - 16
        copies += [
            (t.at[0, :, at : at + 8, :], out.at[0:KL]),
            (t.at[1, :, at : at + 8, :], out.at[KL : 2 * KL]),
            (e.at[:, at16 : at16 + 16, :], flows.at[side, 0]),
            (n.at[:, at16 : at16 + 16, :], flows.at[side, 1]),
            (d.at[at : at + 8, :], depths.at[side]),
        ]
    copies = [pltpu.make_async_copy(src, dst, sems.at[i]) for i, (src, dst) in enumerate(copies)]
    for copy in copies:
        copy.start()
    for side, out in enumerate((out_lo, out_hi)):
        for i in range(5):
            copies[5 * side + i].wait()
        for f in range(2):
            for k in range(KL):
                out[(2 + f) * KL + k] = flows[side, f, k].astype(F32)[8 * side : 8 * side + 8]
        out[4 * KL] = depths[side].astype(F32)


def edges(tracers, east, north, levels):
    out = jax.ShapeDtypeStruct((ARRAYS, 8, SY), F32)
    return pl.pallas_call(
        edges_kernel,
        in_specs=[pl.BlockSpec(memory_space=pltpu.HBM)] * 4,
        out_shape=[out, out],
        scratch_shapes=[
            pltpu.VMEM((2, 2, KL, 16, SY), jnp.bfloat16),
            pltpu.VMEM((2, 8, SY), jnp.int32),
            pltpu.SemaphoreType.DMA((10,)),
        ],
        compiler_params=params(62 * 1024 * 1024),
        name="edges",
    )(tracers, east, north, levels)


def pack(source, rows):
    group = lanes((rows, 128)) // 8
    one = jnp.zeros((rows, 128), F32)
    two = jnp.zeros((rows, 128), F32)
    for k in range(KL):
        value = source(k)
        here = group == k
        one = jnp.where(here, pltpu.roll(value, (8 * k - 124) % 128, 1), one)
        two = jnp.where(here, pltpu.roll(value, (8 * k - 125) % 128, 1), two)
    return one, two


def merge_one(t0, t1, e, n, d):
    member = lanes(t0.shape) % 8
    return (
        jnp.where(member < 4, t0, pltpu.roll(n, 4, 1)),
        jnp.where(member < 4, t1, pltpu.roll(e, 4, 1)),
        d,
    )


def split_one(a, b, c):
    return a, b, pltpu.roll(b, 124, 1), pltpu.roll(a, 124, 1), c


def merge_two(t0, t1, e, n, d):
    member = lanes(t0.shape) % 8
    return (
        jnp.where(member < 3, pltpu.roll(d, 125, 1), t0),
        jnp.where(member < 2, pltpu.roll(d, 122, 1), t1),
        jnp.where((member >= 3) & (member < 7), n, pltpu.roll(e, 4, 1)),
    )


def split_two(a, b, c):
    member = lanes(a.shape) % 8
    depth = jnp.where(member < 6, pltpu.roll(a, 3, 1), pltpu.roll(b, 6, 1))
    return a, b, pltpu.roll(c, 124, 1), c, depth


def pack_all(sources, rows, own, own_rows, sent_one, sent_two, sent_rows):
    packed = [pack(source, rows) for source in sources]
    for which in range(2):
        for a in range(5):
            own[which, a, own_rows, :] = packed[a][which]
    for sent, values in (
        (sent_one, merge_one(*(p[0] for p in packed))),
        (sent_two, merge_two(*(p[1] for p in packed))),
    ):
        for a in range(SENT):
            sent[a, sent_rows, :] = values[a]


def pack_rows_kernel(t, e, n, d, own, one, two):
    chunk = 16

    def body(i, carry):
        rows = pl.ds(pl.multiple_of(i * chunk, chunk), chunk)
        sources = (
            lambda k: t[0, k, rows, :],
            lambda k: t[1, k, rows, :],
            lambda k: e[k, rows, :].astype(F32),
            lambda k: n[k, rows, :].astype(F32),
            lambda k: d[rows, :].astype(F32),
        )
        pack_all(sources, chunk, own, rows, one, two, rows)
        return carry

    lax.fori_loop(0, SX // chunk, body, 0)


def pack_rows(tracers, east, north, levels):
    sent = jax.ShapeDtypeStruct((SENT, SX, 128), F32)
    return pl.pallas_call(
        pack_rows_kernel,
        out_shape=[jax.ShapeDtypeStruct((2, 5, SX, 128), F32), sent, sent],
        compiler_params=params(),
        name="pack_rows",
    )(tracers, east, north, levels)


def pack_edges_kernel(low, high, one_rows, two_rows, own, one, two):
    for g in range(0, SX, 8):
        for a in range(SENT):
            one[a, rows_at(g + EDGE), :] = one_rows[a, rows_at(g), :]
            two[a, rows_at(g + EDGE), :] = two_rows[a, rows_at(g), :]
    for ref, own_at, at in ((low, 0, 0), (high, 8, WIDE - EDGE)):
        sources = [(lambda k, a=a, ref=ref: ref[KL * a + k]) for a in range(4)]
        sources.append(lambda k, ref=ref: ref[4 * KL])
        pack_all(sources, 8, own, rows_at(own_at), one, two, rows_at(at))


def pack_edges(low, high, one, two):
    sent = jax.ShapeDtypeStruct((SENT, WIDE, 128), F32)
    return pl.pallas_call(
        pack_edges_kernel,
        out_shape=[jax.ShapeDtypeStruct((2, 5, 2 * EDGE, 128), F32), sent, sent],
        compiler_params=params(),
        name="pack_edges",
    )(low, high, one, two)


def face_weights(face, flow_value, threshold):
    is_open = face > threshold
    ahead = jnp.where(is_open, KAPPA + jnp.maximum(flow_value, 0.0), 0.0)
    back = jnp.where(is_open, KAPPA - jnp.minimum(flow_value, 0.0), 0.0)
    return ahead, back


def set_weights(depth_at, face_east, face_north, flow, coef, threshold, south):
    coef[1, rows_at(LOW - 8), :] = jnp.zeros((8, 128), F32)
    for g in GROUPS:
        rows = rows_at(g)
        a_east, b_east = face_weights(face_east(g), flow[0, rows, :], threshold)
        a_north, b_north = face_weights(face_north(g), flow[1, rows, :], threshold)
        coef[0, rows, :] = a_east
        coef[1, rows, :] = b_east
        coef[2, rows, :] = b_north
        a_south, b_south = south(g, a_north, b_north)
        coef[3, rows, :] = a_south
        leaving = a_east + a_north + coef[1, rows_at(g - 1), :] + b_south
        coef[4, rows, :] = jnp.where(depth_at(g) > threshold, 1.0 - leaving, 0.0)


def update(source, coef, g, south_value=None):
    rows = rows_at(g)
    value = source[rows, :]
    south = back_one(value) if south_value is None else south_value
    return (
        coef[4, rows, :] * value
        + coef[1, rows, :] * source[rows_at(g + 1), :]
        + coef[0, rows_at(g - 1), :] * source[rows_at(g - 1), :]
        + coef[2, rows, :] * ahead_one(value)
        + coef[3, rows, :] * south
    )


def halo_depth(levels, low, high, depth):
    for g in GROUPS:
        r = g - LOW
        if r < EDGE:
            value = low[4 * KL]
        elif r >= WIDE - EDGE:
            value = high[4 * KL]
        else:
            value = levels[rows_at(r - EDGE), :].astype(F32)
        depth[rows_at(g), :] = value
    for outside in OUTSIDE:
        depth[rows_at(outside), :] = jnp.zeros((8, 128), F32)


def levels_kernel(tracers, east, north, levels, low, high, new, total, depth, face, q0, q1, flow, coef):
    lane = lanes()
    halo_depth(levels, low, high, depth)
    for g in GROUPS:
        rows = rows_at(g)
        here = depth[rows, :]
        face[0, rows, :] = jnp.minimum(here, depth[rows_at(g + 1), :])
        face[1, rows, :] = jnp.where(lane == 127, 0.0, jnp.minimum(here, ahead_one(here)))
        total[rows, :] = jnp.zeros((8, 128), F32)

    def level(k, carry):
        threshold = k.astype(F32)
        for g in GROUPS:
            r = g - LOW
            rows = rows_at(g)
            if r < EDGE or r >= WIDE - EDGE:
                ref = low if r < EDGE else high
                q0[0, rows, :] = ref[k]
                q0[1, rows, :] = ref[KL + k]
                flow[0, rows, :] = ref[2 * KL + k]
                flow[1, rows, :] = ref[3 * KL + k]
            else:
                q0[0, rows, :] = tracers[0, k, rows_at(r - EDGE), :]
                q0[1, rows, :] = tracers[1, k, rows_at(r - EDGE), :]
        flow[0, PAD : PAD + SX, :] = east[k].astype(F32)
        flow[1, PAD : PAD + SX, :] = north[k].astype(F32)
        set_weights(
            lambda g: depth[rows_at(g), :],
            lambda g: face[0, rows_at(g), :],
            lambda g: face[1, rows_at(g), :],
            flow,
            coef,
            threshold,
            lambda g, a, b: (back_one(a), back_one(b)),
        )
        for tracer in range(2):
            for g in GROUPS:
                q1[tracer, rows_at(g), :] = update(q0.at[tracer], coef, g)
        for g in GROUPS:
            temperature = update(q1.at[0], coef, g)
            salinity = update(q1.at[1], coef, g)
            if PAD <= g < PAD + SX:
                new[0, k, rows_at(g - PAD), :] = temperature
                new[1, k, rows_at(g - PAD), :] = salinity
            total[rows_at(g), :] += temperature - 0.8 * salinity
        return carry

    lax.fori_loop(0, KL, level, 0)


def block_levels(tracers, east, north, levels, low, high):
    tall = (ROWS, 128)
    return pl.pallas_call(
        levels_kernel,
        out_shape=[jax.ShapeDtypeStruct(tracers.shape, F32), jax.ShapeDtypeStruct(tall, F32)],
        scratch_shapes=[pltpu.VMEM(s + tall, F32) for s in ((), (2,), (2,), (2,), (2,), (5,))],
        compiler_params=params(),
        cost_estimate=pl.CostEstimate(flops=20_000_000, bytes_accessed=6_000_000, transcendentals=0),
        name="block_levels",
    )(tracers, east, north, levels, low, high)


def operator_kernel(
    levels, low, high, own_rows, own_edges, one_in, two_in, blocked, wall_total,
    new, fields, sums,
    depth, strip_q, strip_depth, strip_flow, strip_total, first_q, coef, total, field, grid, staged, sems, *, count,
):
    lane = lanes()
    member = lane % 8
    blank = jnp.zeros((8, 128), F32)
    strip_level = (lane // 8).astype(F32)
    first = lax.axis_index("gy") == 0
    last = lax.axis_index("gy") == count - 1

    def own(which, a, g):
        r = g - LOW
        if r < EDGE:
            return own_edges[which, a, rows_at(0), :]
        if r >= WIDE - EDGE:
            return own_edges[which, a, rows_at(8), :]
        return own_rows[which, a, rows_at(r - EDGE), :]

    halo_depth(levels, low, high, depth)
    for g in GROUPS:
        rows = rows_at(g)
        sent = rows_at(g - LOW)
        from_low = list(split_one(*(one_in[a, sent, :] for a in range(SENT))))
        from_high = list(split_two(*(two_in[a, sent, :] for a in range(SENT))))
        from_low[4] = jnp.where(first, 0.0, from_low[4])
        from_high[4] = jnp.where(last, 0.0, from_high[4])
        for a in range(5):
            low_strip = jnp.where(member < 4, from_low[a], own(0, a, g))
            high_strip = jnp.where(member >= 3, from_high[a], own(1, a, g))
            for side, value in enumerate((low_strip, high_strip)):
                if a < 2:
                    strip_q[side, a, 0, rows, :] = value
                elif a < 4:
                    strip_flow[side, a - 2, rows, :] = value
                else:
                    strip_depth[side, rows, :] = value
    for outside in OUTSIDE:
        for side in range(2):
            strip_depth[side, rows_at(outside), :] = blank

    for side in range(2):
        at = strip_depth.at[side]

        def south(g, a_north, b_north, side=side):
            a_south, b_south = back_one(a_north), back_one(b_north)
            if side == 1:
                face = jnp.minimum(own(0, 4, g), own(1, 4, g))
                a_first, b_first = face_weights(face, own(0, 3, g), strip_level)
                a_south = jnp.where(member == 0, a_first, a_south)
                b_south = jnp.where(member == 0, b_first, b_south)
            return a_south, b_south

        set_weights(
            lambda g, at=at: at[rows_at(g), :],
            lambda g, at=at: jnp.minimum(at[rows_at(g), :], at[rows_at(g + 1), :]),
            lambda g, at=at: jnp.minimum(at[rows_at(g), :], ahead_one(at[rows_at(g), :])),
            strip_flow.at[side],
            coef,
            strip_level,
            south,
        )
        for tracer in range(2):
            source = strip_q.at[side, tracer, 0]
            for g in GROUPS:
                value = None
                if side == 1:
                    value = jnp.where(member == 0, own(0, tracer, g), back_one(source[rows_at(g), :]))
                strip_q[side, tracer, 1, rows_at(g), :] = update(source, coef, g, value)
        for g in GROUPS:
            rows = rows_at(g)
            temperature = update(strip_q.at[side, 0, 1], coef, g)
            salinity = update(strip_q.at[side, 1, 1], coef, g)
            strip_q[side, 0, 0, rows, :] = temperature
            strip_q[side, 1, 0, rows, :] = salinity
            value = temperature - 0.8 * salinity
            for shift in (8, 16, 32, 64):
                value = value + pltpu.roll(value, shift, 1)
            strip_total[side, rows, :] = value

    for tracer in range(2):
        for g in range(PAD, PAD + SX, 8):
            rows = rows_at(g)
            high_value = pltpu.roll(strip_q[1, tracer, 0, rows, :], 1, 1)
            first_q[tracer, rows, :] = jnp.where(member >= 4, strip_q[0, tracer, 0, rows, :], high_value)
    from_strip = (lane < 2) | (lane >= 126)

    def place(k, carry):
        turn = 124 - 8 * k
        for tracer in range(2):
            for g in range(0, SX, 8):
                rows = rows_at(g)
                value = pltpu.roll(first_q[tracer, rows_at(g + PAD), :], turn, 1)
                staged[tracer, k, rows, :] = jnp.where(from_strip, value, blocked[tracer, k, rows, :])
        for tracer in range(2):
            pltpu.make_async_copy(staged.at[tracer, k], new.at[tracer, k], sems.at[0]).start()
        return carry

    lax.fori_loop(0, KL, place, 0)

    def beside(low_value, high_value):
        return jnp.where(lane >= 64, pltpu.roll(low_value, 4, 1), pltpu.roll(high_value, 5, 1))

    def northward(main, side):
        a, b = ahead_one(main), ahead_one(side)
        return jnp.where(lane == 127, b, a), jnp.where(lane == 127, a, b)

    def southward(main, side):
        a, b = back_one(main), back_one(side)
        return jnp.where(lane == 0, b, a), jnp.where(lane == 0, a, b)

    for g in GROUPS + OUTSIDE:
        rows = rows_at(g)
        grid[0, 0, rows, :] = depth[rows, :]
        grid[0, 1, rows, :] = beside(strip_depth[0, rows, :], strip_depth[1, rows, :])
    for g in GROUPS:
        rows = rows_at(g)
        both = grid[0, 0, rows, :], grid[0, 1, rows, :]
        further = northward(*both)
        for part in range(2):
            grid[1, part, rows, :] = jnp.minimum(both[part], grid[0, part, rows_at(g + 1), :])
            grid[2, part, rows, :] = jnp.minimum(both[part], further[part])
        low_total = pltpu.roll(strip_total[0, rows, :], 4, 1)
        high_total = pltpu.roll(strip_total[1, rows, :], 5, 1)
        edge_total = jnp.where(lane < 64, low_total, high_total)
        total[0, rows, :] = jnp.where(from_strip, edge_total, wall_total[rows, :])
        total[1, rows, :] = jnp.where(lane >= 64, low_total, high_total)
    for part in range(2):
        grid[1, part, rows_at(LOW - 8), :] = blank
        for outside in OUTSIDE:
            for i in range(3):
                field[i, part, rows_at(outside), :] = blank
    scale = 1.0 / KL
    for g in GROUPS:
        rows = rows_at(g)
        souths = southward(grid[2, 0, rows, :], grid[2, 1, rows, :])
        for part in range(2):
            here = grid[0, part, rows, :]
            own_part = ALPHA * scale * here + jnp.where(here == 0.0, 1.0, 0.0)
            faces = grid[1, part, rows, :] + grid[1, part, rows_at(g - 1), :] + grid[2, part, rows, :] + souths[part]
            diagonal = own_part + scale * faces
            inverse = 1.0 / diagonal
            grid[3, part, rows, :] = inverse
            grid[4, part, rows, :] = own_part
            grid[5, part, rows, :] = diagonal
            field[0, part, rows, :] = 0.25 * total[part, rows, :] * inverse

    moments = [blank] * 6
    for i in range(3):
        for g in GROUPS:
            rows = rows_at(g)
            both = field[i, 0, rows, :], field[i, 1, rows, :]
            norths = northward(*both)
            souths = southward(*both)
            south_faces = southward(grid[2, 0, rows, :], grid[2, 1, rows, :])
            for part in range(2):
                if i == 2 and part == 1:
                    continue
                here = both[part]
                east_gap = here - field[i, part, rows_at(g + 1), :]
                north_gap = here - norths[part]
                east_face = scale * grid[1, part, rows, :]
                north_face = scale * grid[2, part, rows, :]
                own_part = grid[4, part, rows, :]
                if part == 0 and PAD <= g < PAD + SX:
                    moments[2 * i] += grid[5, 0, rows, :] * here * here
                    moments[2 * i + 1] += (
                        own_part * here * here + east_face * east_gap * east_gap + north_face * north_gap * north_gap
                    )
                if i < 2:
                    image = (
                        own_part * here
                        + east_face * east_gap
                        + scale * grid[1, part, rows_at(g - 1), :] * (here - field[i, part, rows_at(g - 1), :])
                        + north_face * north_gap
                        + scale * south_faces[part] * (here - souths[part])
                    )
                    field[i + 1, part, rows, :] = image * grid[3, part, rows, :]
        pltpu.make_async_copy(field.at[i, 0, PAD : PAD + SX, :], fields.at[i], sems.at[1]).start()
    row = jnp.zeros((8, 128), F32)
    for i in range(6):
        value = jnp.sum(jnp.sum(moments[i], axis=0, keepdims=True), axis=1, keepdims=True)
        row = jnp.where(lane == i, value, row)
    for g in range(0, 128, 8):
        sums[rows_at(g), :] = row
    pltpu.make_async_copy(field.at[:, 0, PAD : PAD + SX, :], fields, sems.at[1]).wait()
    pltpu.make_async_copy(staged, new, sems.at[0]).wait()


def operator(levels, low, high, own_rows, own_edges, one_in, two_in, blocked, wall_total, count):
    tall = (ROWS, 128)
    scratch = (
        (),
        (2, 2, 2),
        (2,),
        (2, 2),
        (2,),
        (2,),
        (5,),
        (2,),
        (3, 2),
        (6, 2),
    )
    return pl.pallas_call(
        functools.partial(operator_kernel, count=count),
        out_shape=[
            jax.ShapeDtypeStruct(blocked.shape, F32),
            jax.ShapeDtypeStruct((3, SX, SY), F32),
            jax.ShapeDtypeStruct((128, 128), F32),
        ],
        out_specs=[
            pl.BlockSpec(memory_space=pltpu.HBM),
            pl.BlockSpec(memory_space=pltpu.HBM),
            pl.BlockSpec(memory_space=pltpu.VMEM),
        ],
        scratch_shapes=[pltpu.VMEM(s + tall, F32) for s in scratch]
        + [pltpu.VMEM(blocked.shape, F32), pltpu.SemaphoreType.DMA((2,))],
        compiler_params=params(),
        name="operator",
    )(levels, low, high, own_rows, own_edges, one_in, two_in, blocked, wall_total)


def finish_kernel(sums, fields, out):
    value = sums[0:8, :]
    for g in range(8, 128, 8):
        value = value + sums[rows_at(g), :]
    value = jnp.sum(value, axis=0, keepdims=True)
    lane = lanes((1, 128))
    m0, m1, m2, m3, m4, m5 = (
        jnp.sum(jnp.where(lane == i, value, 0.0), axis=1, keepdims=True) for i in range(6)
    )
    floor = 4e-7
    l10 = m2 / m1
    l20 = m3 / m1
    d1 = m3 - l10 * m2
    t = m4 - l20 * m2
    has1 = d1 > floor * m3
    l21 = jnp.where(has1, t / d1, 0.0)
    d2 = m5 - l20 * m3 - l21 * t
    has2 = has1 & (d2 > floor * m5)
    y1 = m1 - l10 * m0
    y2 = m2 - l20 * m0 - l21 * y1
    c2 = jnp.where(has2, y2 / d2, 0.0)
    c1 = jnp.where(has1, y1 / d1, 0.0) - l21 * c2
    c0 = m0 / m1 - l10 * c1 - l20 * c2
    for g in range(0, SX, 8):
        rows = rows_at(g)
        out[rows, :] = c0 * fields[0, rows, :] + c1 * fields[1, rows, :] + c2 * fields[2, rows, :]


def finish(sums, fields):
    return pl.pallas_call(
        finish_kernel,
        out_shape=jax.ShapeDtypeStruct((SX, SY), F32),
        name="finish",
    )(sums, fields)


def shift(array, axis, step):
    count = lax.axis_size(axis)
    return lax.ppermute(array, axis, [(i, (i + step) % count) for i in range(count)])


def on_device(tracers, east, north, levels):
    first, final = edges(tracers, east, north, levels)
    high = shift(first, "gx", -1)
    low = shift(final, "gx", 1)
    own_rows, one, two = pack_rows(tracers, east, north, levels)
    own_edges, one, two = pack_edges(low, high, one, two)
    one_in = shift(one, "gy", 1)
    two_in = shift(two, "gy", -1)
    blocked, total = block_levels(tracers, east, north, levels, low, high)
    new, fields, sums = operator(
        levels, low, high, own_rows, own_edges, one_in, two_in, blocked, total, lax.axis_size("gy")
    )
    sums = lax.all_to_all(sums, ("gx", "gy"), split_axis=0, concat_axis=0, tiled=True)
    return new, finish(sums, fields)


def solution(mesh):
    placed = (P(None, None, "gx", "gy"), P(None, "gx", "gy"), P(None, "gx", "gy"), P("gx", "gy"))
    return jax.shard_map(
        on_device,
        mesh=mesh,
        in_specs=placed,
        out_specs=(P(None, None, "gx", "gy"), P("gx", "gy")),
        check_vma=False,
    )
```

```python
import functools

import jax
import jax.numpy as jnp
from jax import lax
from jax.experimental import pallas as pl
from jax.experimental.pallas import tpu as pltpu
from jax.sharding import PartitionSpec as P

KAPPA = 0.08
ALPHA = 0.05
F32 = jnp.float32

SX = 128
SY = 128
KL = 16
EDGE = 8
PAD = 16
ROWS = SX + 2 * PAD
WIDE = SX + 2 * EDGE
LOW = PAD - EDGE
ARRAYS = 2 * KL + 2 * KL + 1
VMEM = 40 * 1024 * 1024
GROUPS = tuple(range(LOW, LOW + WIDE, 8))
OUTSIDE = (LOW - 8, LOW + WIDE)
BATCHES = (GROUPS[:6], GROUPS[6:12], GROUPS[12:])
SENT = 3
FIELDS = 480


def params(limit=VMEM):
    return pltpu.CompilerParams(vmem_limit_bytes=limit)


def rows_at(row):
    return slice(row, row + 8)


def lanes(shape=(8, 128)):
    return lax.broadcasted_iota(jnp.int32, shape, len(shape) - 1)


def ahead_one(value):
    return pltpu.roll(value, 127, 1)


def back_one(value):
    return pltpu.roll(value, 1, 1)


def offsets(counts):
    starts, at = [], 8
    for a in range(4):
        starts.append(at)
        at += KL * counts[a]
    return starts, at


NEXT = (4, 4, 4, 4)
BEFORE = (5, 5, 4, 4)
NEXT_AT, NEXT_ROWS = offsets(NEXT)
BEFORE_AT, BEFORE_ROWS = offsets(BEFORE)
BEFORE_ROWS += 8


def edges_kernel(t, e, n, d, before, after, tiles, flows, depths, sems):
    copies = []
    for side, at in enumerate((0, SX - 8)):
        at16 = 0 if side == 0 else SX - 16
        copies += [
            (t.at[0, :, at : at + 8, :], tiles.at[side, 0]),
            (t.at[1, :, at : at + 8, :], tiles.at[side, 1]),
            (e.at[:, at16 : at16 + 16, :], flows.at[side, 0]),
            (n.at[:, at16 : at16 + 16, :], flows.at[side, 1]),
            (d.at[at : at + 8, :], depths.at[side]),
        ]
    copies = [pltpu.make_async_copy(src, dst, sems.at[i]) for i, (src, dst) in enumerate(copies)]
    for copy in copies:
        copy.start()
    for side, (out, starts, counts) in enumerate(((before, BEFORE_AT, BEFORE), (after, NEXT_AT, NEXT))):
        for i in range(5):
            copies[5 * side + i].wait()
        out[0:8, :] = depths[side].astype(F32)
        for a in range(4):
            for k in range(KL):
                value = tiles[side, a, k] if a < 2 else flows[side, a - 2, k].astype(F32)[8 * side : 8 * side + 8]
                from_row = 0 if side == 0 else 8 - counts[a]
                at = starts[a] + counts[a] * k
                out[at : at + counts[a], :] = value[from_row : from_row + counts[a]]
    before[BEFORE_ROWS - 8 : BEFORE_ROWS, :] = jnp.zeros((8, 128), F32)


def edges(tracers, east, north, levels):
    return pl.pallas_call(
        edges_kernel,
        in_specs=[pl.BlockSpec(memory_space=pltpu.HBM)] * 4,
        out_shape=[jax.ShapeDtypeStruct((rows, SY), F32) for rows in (BEFORE_ROWS, NEXT_ROWS)],
        scratch_shapes=[
            pltpu.VMEM((2, 2, KL, 8, SY), F32),
            pltpu.VMEM((2, 2, KL, 16, SY), jnp.bfloat16),
            pltpu.VMEM((2, 8, SY), jnp.int32),
            pltpu.SemaphoreType.DMA((10,)),
        ],
        compiler_params=params(62 * 1024 * 1024),
        name="edges",
    )(tracers, east, north, levels)


def low_tile(ref, a, k):
    if a == 4:
        return ref[0:8, :]
    at = NEXT_AT[a] + NEXT[a] * (k + 1) - 8
    return ref[at : at + 8, :]


def high_tile(ref, a, k):
    if a == 4:
        return ref[0:8, :]
    at = BEFORE_AT[a] + BEFORE[a] * k
    return ref[at : at + 8, :]


def pack(source, rows):
    group = lanes((rows, 128)) // 8
    one = jnp.zeros((rows, 128), F32)
    two = jnp.zeros((rows, 128), F32)
    for k in range(KL):
        value = source(k)
        here = group == k
        one = jnp.where(here, pltpu.roll(value, (8 * k - 124) % 128, 1), one)
        two = jnp.where(here, pltpu.roll(value, (8 * k - 125) % 128, 1), two)
    return one, two


def merge_one(t0, t1, e, n, d):
    member = lanes(t0.shape) % 8
    return (
        jnp.where(member < 4, t0, pltpu.roll(n, 4, 1)),
        jnp.where(member < 4, t1, pltpu.roll(e, 4, 1)),
        d,
    )


def split_one(a, b, c):
    return a, b, pltpu.roll(b, 124, 1), pltpu.roll(a, 124, 1), c


def merge_two(t0, t1, e, n, d):
    member = lanes(t0.shape) % 8
    return (
        jnp.where(member < 3, pltpu.roll(d, 125, 1), t0),
        jnp.where(member < 2, pltpu.roll(d, 122, 1), t1),
        jnp.where((member >= 3) & (member < 7), n, pltpu.roll(e, 4, 1)),
    )


def split_two(a, b, c):
    member = lanes(a.shape) % 8
    depth = jnp.where(member < 6, pltpu.roll(a, 3, 1), pltpu.roll(b, 6, 1))
    return a, b, pltpu.roll(c, 124, 1), c, depth


def pack_all(sources, rows, own, own_rows, sent_one, sent_two, sent_rows):
    packed = [pack(source, rows) for source in sources]
    for which in range(2):
        for a in range(5):
            own[which, a, own_rows, :] = packed[a][which]
    for sent, values in (
        (sent_one, merge_one(*(p[0] for p in packed))),
        (sent_two, merge_two(*(p[1] for p in packed))),
    ):
        for a in range(SENT):
            sent[a, sent_rows, :] = values[a]


def pack_rows_kernel(t, e, n, d, own, one, two):
    chunk = 16

    def body(i, carry):
        rows = pl.ds(pl.multiple_of(i * chunk, chunk), chunk)
        sources = (
            lambda k: t[0, k, rows, :],
            lambda k: t[1, k, rows, :],
            lambda k: e[k, rows, :].astype(F32),
            lambda k: n[k, rows, :].astype(F32),
            lambda k: d[rows, :].astype(F32),
        )
        pack_all(sources, chunk, own, rows, one, two, rows)
        return carry

    lax.fori_loop(0, SX // chunk, body, 0)


def pack_rows(tracers, east, north, levels):
    sent = jax.ShapeDtypeStruct((SENT, SX, 128), F32)
    return pl.pallas_call(
        pack_rows_kernel,
        out_shape=[jax.ShapeDtypeStruct((2, 5, SX, 128), F32), sent, sent],
        compiler_params=params(),
        name="pack_rows",
    )(tracers, east, north, levels)


def pack_edges_kernel(low_in, high_in, one_rows, two_rows, own, one, two, low, high):
    for a in range(5):
        for k in range(KL if a < 4 else 1):
            low[KL * a + k] = low_tile(low_in, a, k)
            high[KL * a + k] = high_tile(high_in, a, k)
    for g in range(0, SX, 8):
        for a in range(SENT):
            one[a, rows_at(g + EDGE), :] = one_rows[a, rows_at(g), :]
            two[a, rows_at(g + EDGE), :] = two_rows[a, rows_at(g), :]
    for ref, tile, own_at, at in ((low_in, low_tile, 0, 0), (high_in, high_tile, 8, WIDE - EDGE)):
        sources = [functools.partial(tile, ref, a) for a in range(5)]
        pack_all(sources, 8, own, rows_at(own_at), one, two, rows_at(at))


def pack_edges(low, high, one, two):
    sent = jax.ShapeDtypeStruct((SENT, WIDE, 128), F32)
    halo = jax.ShapeDtypeStruct((ARRAYS, EDGE, SY), F32)
    return pl.pallas_call(
        pack_edges_kernel,
        out_shape=[jax.ShapeDtypeStruct((2, 5, 2 * EDGE, 128), F32), sent, sent, halo, halo],
        compiler_params=params(),
        name="pack_edges",
    )(low, high, one, two)


def face_weights(face, flow_value, threshold):
    is_open = face > threshold
    ahead = jnp.where(is_open, KAPPA + jnp.maximum(flow_value, 0.0), 0.0)
    back = jnp.where(is_open, KAPPA - jnp.minimum(flow_value, 0.0), 0.0)
    return ahead, back


def set_weights(depth_at, face_east, face_north, flow, coef, threshold, south):
    coef[1, rows_at(LOW - 8), :] = jnp.zeros((8, 128), F32)
    for batch in BATCHES:
        a_north, b_north = {}, {}
        for g in batch:
            rows = rows_at(g)
            a_east, b_east = face_weights(face_east(g), flow[0, rows, :], threshold)
            a_north[g], b_north[g] = face_weights(face_north(g), flow[1, rows, :], threshold)
            coef[0, rows, :] = a_east
            coef[1, rows, :] = b_east
            coef[2, rows, :] = b_north[g]
        a_south = {g: back_one(a_north[g]) for g in batch}
        b_south = {g: back_one(b_north[g]) for g in batch}
        for g in batch:
            rows = rows_at(g)
            a_here, b_here = south(g, a_south[g], b_south[g])
            coef[3, rows, :] = a_here
            leaving = coef[0, rows, :] + a_north[g] + coef[1, rows_at(g - 1), :] + b_here
            coef[4, rows, :] = jnp.where(depth_at(g) > threshold, 1.0 - leaving, 0.0)


def update(source, coef, batch, south_value=None):
    ahead = {g: ahead_one(source[rows_at(g), :]) for g in batch}
    back = {g: back_one(source[rows_at(g), :]) for g in batch}
    result = {}
    for g in batch:
        rows = rows_at(g)
        south = back[g] if south_value is None else south_value(g, back[g])
        result[g] = (
            coef[4, rows, :] * source[rows, :]
            + coef[1, rows, :] * source[rows_at(g + 1), :]
            + coef[0, rows_at(g - 1), :] * source[rows_at(g - 1), :]
            + coef[2, rows, :] * ahead[g]
            + coef[3, rows, :] * south
        )
    return result


def halo_depth(levels, low, high, depth):
    for g in GROUPS:
        r = g - LOW
        if r < EDGE:
            value = low[4 * KL]
        elif r >= WIDE - EDGE:
            value = high[4 * KL]
        else:
            value = levels[rows_at(r - EDGE), :].astype(F32)
        depth[rows_at(g), :] = value
    for outside in OUTSIDE:
        depth[rows_at(outside), :] = jnp.zeros((8, 128), F32)


def levels_kernel(tracers, east, north, levels, low, high, new, total, depth, face, q0, q1, flow, coef):
    lane = lanes()
    halo_depth(levels, low, high, depth)
    for g in GROUPS:
        rows = rows_at(g)
        here = depth[rows, :]
        face[0, rows, :] = jnp.minimum(here, depth[rows_at(g + 1), :])
        face[1, rows, :] = jnp.where(lane == 127, 0.0, jnp.minimum(here, ahead_one(here)))
        total[rows, :] = jnp.zeros((8, 128), F32)

    def level(k, carry):
        threshold = k.astype(F32)
        for g in GROUPS:
            r = g - LOW
            rows = rows_at(g)
            if r < EDGE or r >= WIDE - EDGE:
                ref = low if r < EDGE else high
                q0[0, rows, :] = ref[k]
                q0[1, rows, :] = ref[KL + k]
                flow[0, rows, :] = ref[2 * KL + k]
                flow[1, rows, :] = ref[3 * KL + k]
            else:
                q0[0, rows, :] = tracers[0, k, rows_at(r - EDGE), :]
                q0[1, rows, :] = tracers[1, k, rows_at(r - EDGE), :]
        flow[0, PAD : PAD + SX, :] = east[k].astype(F32)
        flow[1, PAD : PAD + SX, :] = north[k].astype(F32)
        set_weights(
            lambda g: depth[rows_at(g), :],
            lambda g: face[0, rows_at(g), :],
            lambda g: face[1, rows_at(g), :],
            flow,
            coef,
            threshold,
            lambda g, a, b: (a, b),
        )
        for tracer in range(2):
            for batch in BATCHES:
                for g, value in update(q0.at[tracer], coef, batch).items():
                    q1[tracer, rows_at(g), :] = value
        for batch in BATCHES:
            temperature = update(q1.at[0], coef, batch)
            salinity = update(q1.at[1], coef, batch)
            for g in batch:
                if PAD <= g < PAD + SX:
                    new[0, k, rows_at(g - PAD), :] = temperature[g]
                    new[1, k, rows_at(g - PAD), :] = salinity[g]
                total[rows_at(g), :] += temperature[g] - 0.8 * salinity[g]
        return carry

    lax.fori_loop(0, KL, level, 0)


def block_levels(tracers, east, north, levels, low, high):
    tall = (ROWS, 128)
    return pl.pallas_call(
        levels_kernel,
        out_shape=[jax.ShapeDtypeStruct(tracers.shape, F32), jax.ShapeDtypeStruct(tall, F32)],
        scratch_shapes=[pltpu.VMEM(s + tall, F32) for s in ((), (2,), (2,), (2,), (2,), (5,))],
        compiler_params=params(),
        cost_estimate=pl.CostEstimate(flops=20_000_000, bytes_accessed=6_000_000, transcendentals=0),
        name="block_levels",
    )(tracers, east, north, levels, low, high)


def operator_kernel(
    levels, low, high, own_rows, own_edges, one_in, two_in, blocked, wall_total,
    new, fields, sums,
    depth, strip_q, strip_depth, strip_face, strip_flow, strip_total, first_q, coef, total, field, grid, staged, sems, *, count,
):
    lane = lanes()
    member = lane % 8
    blank = jnp.zeros((8, 128), F32)
    strip_level = (lane // 8).astype(F32)
    first = lax.axis_index("gy") == 0
    last = lax.axis_index("gy") == count - 1

    def own(which, a, g):
        r = g - LOW
        if r < EDGE:
            return own_edges[which, a, rows_at(0), :]
        if r >= WIDE - EDGE:
            return own_edges[which, a, rows_at(8), :]
        return own_rows[which, a, rows_at(r - EDGE), :]

    halo_depth(levels, low, high, depth)
    parts = {}
    for g in GROUPS:
        sent = rows_at(g - LOW)
        parts[g] = (
            list(split_one(*(one_in[a, sent, :] for a in range(SENT)))),
            list(split_two(*(two_in[a, sent, :] for a in range(SENT)))),
        )
    for g in GROUPS:
        rows = rows_at(g)
        from_low, from_high = parts[g]
        from_low[4] = jnp.where(first, 0.0, from_low[4])
        from_high[4] = jnp.where(last, 0.0, from_high[4])
        for a in range(5):
            low_strip = jnp.where(member < 4, from_low[a], own(0, a, g))
            high_strip = jnp.where(member >= 3, from_high[a], own(1, a, g))
            for side, value in enumerate((low_strip, high_strip)):
                if a < 2:
                    strip_q[side, a, 0, rows, :] = value
                elif a < 4:
                    strip_flow[side, a - 2, rows, :] = value
                else:
                    strip_depth[side, rows, :] = value
    for outside in OUTSIDE:
        for side in range(2):
            strip_depth[side, rows_at(outside), :] = blank

    ahead = {
        (side, g): ahead_one(strip_depth[side, rows_at(g), :]) for side in range(2) for g in GROUPS
    }
    for (side, g), value in ahead.items():
        strip_face[side, rows_at(g), :] = jnp.minimum(strip_depth[side, rows_at(g), :], value)

    for side in range(2):
        at = strip_depth.at[side]

        def south(g, a_south, b_south, side=side):
            if side == 1:
                face = jnp.minimum(own(0, 4, g), own(1, 4, g))
                a_first, b_first = face_weights(face, own(0, 3, g), strip_level)
                a_south = jnp.where(member == 0, a_first, a_south)
                b_south = jnp.where(member == 0, b_first, b_south)
            return a_south, b_south

        set_weights(
            lambda g, at=at: at[rows_at(g), :],
            lambda g, at=at: jnp.minimum(at[rows_at(g), :], at[rows_at(g + 1), :]),
            lambda g, side=side: strip_face[side, rows_at(g), :],
            strip_flow.at[side],
            coef,
            strip_level,
            south,
        )
        for tracer in range(2):
            source = strip_q.at[side, tracer, 0]
            from_own = None
            if side == 1:

                def from_own(g, value, tracer=tracer):
                    return jnp.where(member == 0, own(0, tracer, g), value)

            for batch in BATCHES:
                for g, value in update(source, coef, batch, from_own).items():
                    strip_q[side, tracer, 1, rows_at(g), :] = value
        for batch in BATCHES:
            temperature = update(strip_q.at[side, 0, 1], coef, batch)
            salinity = update(strip_q.at[side, 1, 1], coef, batch)
            for g in batch:
                rows = rows_at(g)
                strip_q[side, 0, 0, rows, :] = temperature[g]
                strip_q[side, 1, 0, rows, :] = salinity[g]
                strip_total[side, rows, :] = temperature[g] - 0.8 * salinity[g]
    for turn in (8, 16, 32, 64):
        values = {}
        for side in range(2):
            for g in GROUPS:
                value = strip_total[side, rows_at(g), :]
                values[side, g] = value + pltpu.roll(value, turn, 1)
        for (side, g), value in values.items():
            strip_total[side, rows_at(g), :] = value

    for tracer in range(2):
        for g in range(PAD, PAD + SX, 8):
            rows = rows_at(g)
            high_value = pltpu.roll(strip_q[1, tracer, 0, rows, :], 1, 1)
            first_q[tracer, rows, :] = jnp.where(member >= 4, strip_q[0, tracer, 0, rows, :], high_value)
    from_strip = (lane < 2) | (lane >= 126)

    def place(k, carry):
        turn = 124 - 8 * k
        for tracer in range(2):
            values = {g: pltpu.roll(first_q[tracer, rows_at(g + PAD), :], turn, 1) for g in range(0, SX, 8)}
            for g, value in values.items():
                rows = rows_at(g)
                staged[tracer, k, rows, :] = jnp.where(from_strip, value, blocked[tracer, k, rows, :])
        for tracer in range(2):
            pltpu.make_async_copy(staged.at[tracer, k], new.at[tracer, k], sems.at[0]).start()
        return carry

    lax.fori_loop(0, KL, place, 0)

    def beside(low_value, high_value):
        return jnp.where(lane >= 64, pltpu.roll(low_value, 4, 1), pltpu.roll(high_value, 5, 1))

    def northward(main, side):
        a, b = ahead_one(main), ahead_one(side)
        return jnp.where(lane == 127, b, a), jnp.where(lane == 127, a, b)

    def southward(main, side):
        a, b = back_one(main), back_one(side)
        return jnp.where(lane == 0, b, a), jnp.where(lane == 0, a, b)

    for g in GROUPS + OUTSIDE:
        rows = rows_at(g)
        grid[0, 0, rows, :] = depth[rows, :]
        grid[0, 1, rows, :] = beside(strip_depth[0, rows, :], strip_depth[1, rows, :])
    for g in GROUPS:
        rows = rows_at(g)
        both = grid[0, 0, rows, :], grid[0, 1, rows, :]
        further = northward(*both)
        for part in range(2):
            grid[1, part, rows, :] = jnp.minimum(both[part], grid[0, part, rows_at(g + 1), :])
            grid[2, part, rows, :] = jnp.minimum(both[part], further[part])
        low_total = pltpu.roll(strip_total[0, rows, :], 4, 1)
        high_total = pltpu.roll(strip_total[1, rows, :], 5, 1)
        edge_total = jnp.where(lane < 64, low_total, high_total)
        total[0, rows, :] = jnp.where(from_strip, edge_total, wall_total[rows, :])
        total[1, rows, :] = jnp.where(lane >= 64, low_total, high_total)
    for part in range(2):
        grid[1, part, rows_at(LOW - 8), :] = blank
        for outside in OUTSIDE:
            for i in range(3):
                field[i, part, rows_at(outside), :] = blank
    scale = 1.0 / KL
    for g in GROUPS:
        rows = rows_at(g)
        souths = southward(grid[2, 0, rows, :], grid[2, 1, rows, :])
        for part in range(2):
            here = grid[0, part, rows, :]
            own_part = ALPHA * scale * here + jnp.where(here == 0.0, 1.0, 0.0)
            faces = grid[1, part, rows, :] + grid[1, part, rows_at(g - 1), :] + grid[2, part, rows, :] + souths[part]
            diagonal = own_part + scale * faces
            inverse = 1.0 / diagonal
            grid[3, part, rows, :] = inverse
            grid[4, part, rows, :] = own_part
            grid[5, part, rows, :] = diagonal
            field[0, part, rows, :] = 0.25 * total[part, rows, :] * inverse

    moments = [blank] * 6
    for i in range(3):
        for g in GROUPS:
            rows = rows_at(g)
            both = field[i, 0, rows, :], field[i, 1, rows, :]
            norths = northward(*both)
            souths = southward(*both)
            south_faces = southward(grid[2, 0, rows, :], grid[2, 1, rows, :])
            for part in range(2):
                if i == 2 and part == 1:
                    continue
                here = both[part]
                east_gap = here - field[i, part, rows_at(g + 1), :]
                north_gap = here - norths[part]
                east_face = scale * grid[1, part, rows, :]
                north_face = scale * grid[2, part, rows, :]
                own_part = grid[4, part, rows, :]
                if part == 0 and PAD <= g < PAD + SX:
                    moments[2 * i] += grid[5, 0, rows, :] * here * here
                    moments[2 * i + 1] += (
                        own_part * here * here + east_face * east_gap * east_gap + north_face * north_gap * north_gap
                    )
                if i < 2:
                    image = (
                        own_part * here
                        + east_face * east_gap
                        + scale * grid[1, part, rows_at(g - 1), :] * (here - field[i, part, rows_at(g - 1), :])
                        + north_face * north_gap
                        + scale * south_faces[part] * (here - souths[part])
                    )
                    field[i + 1, part, rows, :] = image * grid[3, part, rows, :]
        pltpu.make_async_copy(field.at[i, 0, PAD : PAD + SX, :], fields.at[i], sems.at[1]).start()
    row = jnp.zeros((8, 128), F32)
    for i in range(6):
        value = jnp.sum(jnp.sum(moments[i], axis=0, keepdims=True), axis=1, keepdims=True)
        row = jnp.where(lane == i, value, row)
    for g in range(0, 128, 8):
        sums[rows_at(g), :] = row
    pltpu.make_async_copy(field.at[:, 0, PAD : PAD + SX, :], fields.at[0:3], sems.at[1]).wait()
    pltpu.make_async_copy(staged, new, sems.at[0]).wait()


def operator(levels, low, high, own_rows, own_edges, one_in, two_in, blocked, wall_total, count):
    tall = (ROWS, 128)
    scratch = (
        (),
        (2, 2, 2),
        (2,),
        (2,),
        (2, 2),
        (2,),
        (2,),
        (5,),
        (2,),
        (3, 2),
        (6, 2),
    )
    return pl.pallas_call(
        functools.partial(operator_kernel, count=count),
        out_shape=[
            jax.ShapeDtypeStruct(blocked.shape, F32),
            jax.ShapeDtypeStruct((FIELDS, SX, SY), F32),
            jax.ShapeDtypeStruct((128, 128), F32),
        ],
        out_specs=[
            pl.BlockSpec(memory_space=pltpu.HBM),
            pl.BlockSpec(memory_space=pltpu.HBM),
            pl.BlockSpec(memory_space=pltpu.VMEM),
        ],
        scratch_shapes=[pltpu.VMEM(s + tall, F32) for s in scratch]
        + [pltpu.VMEM(blocked.shape, F32), pltpu.SemaphoreType.DMA((2,))],
        compiler_params=params(),
        name="operator",
    )(levels, low, high, own_rows, own_edges, one_in, two_in, blocked, wall_total)


def finish_kernel(sums, fields_in, out, fields, sem):
    copy = pltpu.make_async_copy(fields_in.at[0:3], fields, sem)
    copy.start()
    value = sums[0:8, :]
    for g in range(8, 128, 8):
        value = value + sums[rows_at(g), :]
    value = jnp.sum(value, axis=0, keepdims=True)
    lane = lanes((1, 128))
    m0, m1, m2, m3, m4, m5 = (
        jnp.sum(jnp.where(lane == i, value, 0.0), axis=1, keepdims=True) for i in range(6)
    )
    floor = 4e-7
    l10 = m2 / m1
    l20 = m3 / m1
    d1 = m3 - l10 * m2
    t = m4 - l20 * m2
    has1 = d1 > floor * m3
    l21 = jnp.where(has1, t / d1, 0.0)
    d2 = m5 - l20 * m3 - l21 * t
    has2 = has1 & (d2 > floor * m5)
    y1 = m1 - l10 * m0
    y2 = m2 - l20 * m0 - l21 * y1
    c2 = jnp.where(has2, y2 / d2, 0.0)
    c1 = jnp.where(has1, y1 / d1, 0.0) - l21 * c2
    c0 = m0 / m1 - l10 * c1 - l20 * c2
    copy.wait()
    for g in range(0, SX, 8):
        rows = rows_at(g)
        out[rows, :] = c0 * fields[0, rows, :] + c1 * fields[1, rows, :] + c2 * fields[2, rows, :]


def finish(sums, fields):
    return pl.pallas_call(
        finish_kernel,
        in_specs=[pl.BlockSpec(memory_space=pltpu.VMEM), pl.BlockSpec(memory_space=pltpu.HBM)],
        out_shape=jax.ShapeDtypeStruct((SX, SY), F32),
        scratch_shapes=[pltpu.VMEM((3, SX, SY), F32), pltpu.SemaphoreType.DMA(())],
        name="finish",
    )(sums, fields)


def shift(array, axis, step):
    count = lax.axis_size(axis)
    return lax.ppermute(array, axis, [(i, (i + step) % count) for i in range(count)])


def on_device(tracers, east, north, levels):
    before, after = edges(tracers, east, north, levels)
    before = shift(before, "gx", -1)
    after = shift(after, "gx", 1)
    own_rows, one, two = pack_rows(tracers, east, north, levels)
    own_edges, one, two, low, high = pack_edges(after, before, one, two)
    one_in = shift(one, "gy", 1)
    two_in = shift(two, "gy", -1)
    blocked, total = block_levels(tracers, east, north, levels, low, high)
    new, fields, sums = operator(
        levels, low, high, own_rows, own_edges, one_in, two_in, blocked, total, lax.axis_size("gy")
    )
    sums = lax.all_to_all(sums, ("gx", "gy"), split_axis=0, concat_axis=0, tiled=True)
    return new, finish(sums, fields)


def solution(mesh):
    placed = (P(None, None, "gx", "gy"), P(None, "gx", "gy"), P(None, "gx", "gy"), P("gx", "gy"))
    return jax.shard_map(
        on_device,
        mesh=mesh,
        in_specs=placed,
        out_specs=(P(None, None, "gx", "gy"), P("gx", "gy")),
        check_vma=False,
    )
```

```python
import functools

import jax
import jax.numpy as jnp
from jax import lax
from jax.experimental import pallas as pl
from jax.experimental.pallas import tpu as pltpu
from jax.sharding import PartitionSpec as P

KAPPA = 0.08
ALPHA = 0.05
F32 = jnp.float32

SX = 128
SY = 128
KL = 16
EDGE = 8
PAD = 16
ROWS = SX + 2 * PAD
WIDE = SX + 2 * EDGE
LOW = PAD - EDGE
ARRAYS = 2 * KL + 2 * KL + 1
VMEM = 40 * 1024 * 1024
GROUPS = tuple(range(LOW, LOW + WIDE, 8))
OUTSIDE = (LOW - 8, LOW + WIDE)
BATCHES = (GROUPS[:6], GROUPS[6:12], GROUPS[12:])
SENT = 3


def params():
    return pltpu.CompilerParams(vmem_limit_bytes=VMEM)


def rows_at(row):
    return slice(row, row + 8)


def lanes(shape=(8, 128)):
    return lax.broadcasted_iota(jnp.int32, shape, len(shape) - 1)


def ahead_one(value):
    return pltpu.roll(value, 127, 1)


def back_one(value):
    return pltpu.roll(value, 1, 1)


def offsets(counts):
    starts, at = [], 8
    for a in range(4):
        starts.append(at)
        at += KL * counts[a]
    return starts, at


NEXT = (4, 4, 4, 4)
BEFORE = (5, 5, 4, 4)
NEXT_AT, NEXT_ROWS = offsets(NEXT)
BEFORE_AT, BEFORE_ROWS = offsets(BEFORE)
BEFORE_ROWS += 8


def edges_kernel(t, e, n, d, before, after, tiles, flows, depths, sems):
    copies = []
    for side, at in enumerate((0, SX - 8)):
        at16 = 0 if side == 0 else SX - 16
        copies += [
            (t.at[0, :, at : at + 8, :], tiles.at[side, 0]),
            (t.at[1, :, at : at + 8, :], tiles.at[side, 1]),
            (e.at[:, at16 : at16 + 16, :], flows.at[side, 0]),
            (n.at[:, at16 : at16 + 16, :], flows.at[side, 1]),
            (d.at[at : at + 8, :], depths.at[side]),
        ]
    copies = [pltpu.make_async_copy(src, dst, sems.at[i]) for i, (src, dst) in enumerate(copies)]
    for copy in copies:
        copy.start()
    for side, (out, starts, counts) in enumerate(((before, BEFORE_AT, BEFORE), (after, NEXT_AT, NEXT))):
        for i in range(5):
            copies[5 * side + i].wait()
        out[0:8, :] = depths[side].astype(F32)
        for a in range(4):
            for k in range(KL):
                value = tiles[side, a, k] if a < 2 else flows[side, a - 2, k].astype(F32)[8 * side : 8 * side + 8]
                from_row = 0 if side == 0 else 8 - counts[a]
                at = starts[a] + counts[a] * k
                out[at : at + counts[a], :] = value[from_row : from_row + counts[a]]
    before[BEFORE_ROWS - 8 : BEFORE_ROWS, :] = jnp.zeros((8, 128), F32)


def edges(tracers, east, north, levels):
    return pl.pallas_call(
        edges_kernel,
        in_specs=[pl.BlockSpec(memory_space=pltpu.HBM)] * 4,
        out_shape=[pltpu.VMEM((rows, SY), F32) for rows in (BEFORE_ROWS, NEXT_ROWS)],
        scratch_shapes=[
            pltpu.VMEM((2, 2, KL, 8, SY), F32),
            pltpu.VMEM((2, 2, KL, 16, SY), jnp.bfloat16),
            pltpu.VMEM((2, 8, SY), jnp.int32),
            pltpu.SemaphoreType.DMA((10,)),
        ],
        compiler_params=params(),
        name="edges",
    )(*(pltpu.with_memory_space_constraint(x, pltpu.HBM) for x in (tracers, east, north, levels)))


def low_tile(ref, a, k):
    if a == 4:
        return ref[0:8, :]
    at = NEXT_AT[a] + NEXT[a] * (k + 1) - 8
    return ref[at : at + 8, :]


def high_tile(ref, a, k):
    if a == 4:
        return ref[0:8, :]
    at = BEFORE_AT[a] + BEFORE[a] * k
    return ref[at : at + 8, :]


def pack(source, rows, last):
    group = lanes((rows, 128)) // 8
    one = jnp.zeros((rows, 128), F32)
    beyond = jnp.zeros((rows, 128), F32)
    for k in range(KL):
        value = source(k)
        one = jnp.where(group == k, pltpu.roll(value, (8 * k - 124) % 128, 1), one)
        if last:
            beyond = jnp.where(group == k, pltpu.roll(value, (8 * k + 3) % 128, 1), beyond)
    two = pltpu.roll(one, 127, 1)
    if last:
        two = jnp.where(lanes((rows, 128)) % 8 == 7, beyond, two)
    return one, two


def pack_depth(sources):
    lane = lanes(sources[0].shape)
    values = [pltpu.roll(x, turn, 1) for turn in (4, 3) for x in sources]
    values = [jnp.where(lane < 8, x, 0.0) for x in values]
    for turn in (8, 16, 32, 64):
        values = [x + pltpu.roll(x, turn, 1) for x in values]
    return list(zip(values[: len(sources)], values[len(sources) :], strict=True))


def merge_one(t0, t1, e, n, d):
    member = lanes(t0.shape) % 8
    return (
        jnp.where(member < 4, t0, pltpu.roll(n, 4, 1)),
        jnp.where(member < 4, t1, pltpu.roll(e, 4, 1)),
        d,
    )


def split_one(a, b, c):
    return a, b, pltpu.roll(b, 124, 1), pltpu.roll(a, 124, 1), c


def merge_two(t0, t1, e, n, d):
    member = lanes(t0.shape) % 8
    return (
        jnp.where(member < 3, pltpu.roll(d, 125, 1), t0),
        jnp.where(member < 2, pltpu.roll(d, 122, 1), t1),
        jnp.where((member >= 3) & (member < 7), n, pltpu.roll(e, 4, 1)),
    )


def split_two(a, b, c):
    member = lanes(a.shape) % 8
    depth = jnp.where(member < 6, pltpu.roll(a, 3, 1), pltpu.roll(b, 6, 1))
    return a, b, pltpu.roll(c, 124, 1), c, depth


def pack_all(sources, depths, rows, own, own_rows, sent_one, sent_two, sent_rows):
    packed = [pack(source, rows, a < 2) for a, source in enumerate(sources)] + [depths]
    for which in range(2):
        for a in range(5):
            own[which, a, own_rows, :] = packed[a][which]
    for sent, values in (
        (sent_one, merge_one(*(p[0] for p in packed))),
        (sent_two, merge_two(*(p[1] for p in packed))),
    ):
        for a in range(SENT):
            sent[a, sent_rows, :] = values[a]


def pack_rows_kernel(t, e, n, d, own, one, two):
    chunk = 16
    groups = range(0, SX, 8)
    for g, pair in zip(groups, pack_depth([d[rows_at(g), :].astype(F32) for g in groups]), strict=True):
        for which in range(2):
            own[which, 4, rows_at(g), :] = pair[which]

    def body(i, carry):
        rows = pl.ds(pl.multiple_of(i * chunk, chunk), chunk)
        sources = (
            lambda k: t[0, k, rows, :],
            lambda k: t[1, k, rows, :],
            lambda k: e[k, rows, :].astype(F32),
            lambda k: n[k, rows, :].astype(F32),
        )
        depths = own[0, 4, rows, :], own[1, 4, rows, :]
        pack_all(sources, depths, chunk, own, rows, one, two, rows)
        return carry

    lax.fori_loop(0, SX // chunk, body, 0)


def pack_rows(tracers, east, north, levels):
    sent = jax.ShapeDtypeStruct((SENT, SX, 128), F32)
    return pl.pallas_call(
        pack_rows_kernel,
        out_shape=[jax.ShapeDtypeStruct((2, 5, SX, 128), F32), sent, sent],
        compiler_params=params(),
        name="pack_rows",
    )(tracers, east, north, levels)


def pack_edges_kernel(low_in, high_in, one_rows, two_rows, own, one, two, low, high):
    for a in range(5):
        for k in range(KL if a < 4 else 1):
            low[KL * a + k] = low_tile(low_in, a, k)
            high[KL * a + k] = high_tile(high_in, a, k)
    for g in range(0, SX, 8):
        for a in range(SENT):
            one[a, rows_at(g + EDGE), :] = one_rows[a, rows_at(g), :]
            two[a, rows_at(g + EDGE), :] = two_rows[a, rows_at(g), :]
    depths = pack_depth([low_tile(low_in, 4, 0), high_tile(high_in, 4, 0)])
    for side, (ref, tile, at) in enumerate(((low_in, low_tile, 0), (high_in, high_tile, WIDE - EDGE))):
        sources = [functools.partial(tile, ref, a) for a in range(4)]
        pack_all(sources, depths[side], 8, own, rows_at(8 * side), one, two, rows_at(at))


def pack_edges(low, high, one, two):
    sent = jax.ShapeDtypeStruct((SENT, WIDE, 128), F32)
    halo = jax.ShapeDtypeStruct((ARRAYS, EDGE, SY), F32)
    return pl.pallas_call(
        pack_edges_kernel,
        out_shape=[jax.ShapeDtypeStruct((2, 5, 2 * EDGE, 128), F32), sent, sent, halo, halo],
        compiler_params=params(),
        name="pack_edges",
    )(low, high, one, two)


def face_weights(face, flow_value, threshold):
    is_open = face > threshold
    ahead = jnp.where(is_open, KAPPA + jnp.maximum(flow_value, 0.0), 0.0)
    back = jnp.where(is_open, KAPPA - jnp.minimum(flow_value, 0.0), 0.0)
    return ahead, back


def set_weights(depth_at, face_east, face_north, flow, coef, threshold, south):
    coef[1, rows_at(LOW - 8), :] = jnp.zeros((8, 128), F32)
    for batch in BATCHES:
        a_north, b_north = {}, {}
        for g in batch:
            rows = rows_at(g)
            a_east, b_east = face_weights(face_east(g), flow[0, rows, :], threshold)
            a_north[g], b_north[g] = face_weights(face_north(g), flow[1, rows, :], threshold)
            coef[0, rows, :] = a_east
            coef[1, rows, :] = b_east
            coef[2, rows, :] = b_north[g]
        a_south = {g: back_one(a_north[g]) for g in batch}
        b_south = {g: back_one(b_north[g]) for g in batch}
        for g in batch:
            rows = rows_at(g)
            a_here, b_here = south(g, a_south[g], b_south[g])
            coef[3, rows, :] = a_here
            leaving = coef[0, rows, :] + a_north[g] + coef[1, rows_at(g - 1), :] + b_here
            coef[4, rows, :] = jnp.where(depth_at(g) > threshold, 1.0 - leaving, 0.0)


def update(source, coef, batch, south_value=None):
    ahead = {g: ahead_one(source[rows_at(g), :]) for g in batch}
    back = {g: back_one(source[rows_at(g), :]) for g in batch}
    result = {}
    for g in batch:
        rows = rows_at(g)
        south = back[g] if south_value is None else south_value(g, back[g])
        result[g] = (
            coef[4, rows, :] * source[rows, :]
            + coef[1, rows, :] * source[rows_at(g + 1), :]
            + coef[0, rows_at(g - 1), :] * source[rows_at(g - 1), :]
            + coef[2, rows, :] * ahead[g]
            + coef[3, rows, :] * south
        )
    return result


def halo_depth(levels, low, high, depth):
    for g in GROUPS:
        r = g - LOW
        if r < EDGE:
            value = low[4 * KL]
        elif r >= WIDE - EDGE:
            value = high[4 * KL]
        else:
            value = levels[rows_at(r - EDGE), :].astype(F32)
        depth[rows_at(g), :] = value
    for outside in OUTSIDE:
        depth[rows_at(outside), :] = jnp.zeros((8, 128), F32)


def levels_kernel(tracers, east, north, levels, low, high, new, total, depth, face, q0, q1, flow, coef):
    lane = lanes()
    halo_depth(levels, low, high, depth)
    for g in GROUPS:
        rows = rows_at(g)
        here = depth[rows, :]
        face[0, rows, :] = jnp.minimum(here, depth[rows_at(g + 1), :])
        face[1, rows, :] = jnp.where(lane == 127, 0.0, jnp.minimum(here, ahead_one(here)))
        total[rows, :] = jnp.zeros((8, 128), F32)

    def level(k, carry):
        threshold = k.astype(F32)
        for g in GROUPS:
            r = g - LOW
            rows = rows_at(g)
            if r < EDGE or r >= WIDE - EDGE:
                ref = low if r < EDGE else high
                q0[0, rows, :] = ref[k]
                q0[1, rows, :] = ref[KL + k]
                flow[0, rows, :] = ref[2 * KL + k]
                flow[1, rows, :] = ref[3 * KL + k]
            else:
                q0[0, rows, :] = tracers[0, k, rows_at(r - EDGE), :]
                q0[1, rows, :] = tracers[1, k, rows_at(r - EDGE), :]
        flow[0, PAD : PAD + SX, :] = east[k].astype(F32)
        flow[1, PAD : PAD + SX, :] = north[k].astype(F32)
        set_weights(
            lambda g: depth[rows_at(g), :],
            lambda g: face[0, rows_at(g), :],
            lambda g: face[1, rows_at(g), :],
            flow,
            coef,
            threshold,
            lambda g, a, b: (a, b),
        )
        for tracer in range(2):
            for batch in BATCHES:
                for g, value in update(q0.at[tracer], coef, batch).items():
                    q1[tracer, rows_at(g), :] = value
        for batch in BATCHES:
            temperature = update(q1.at[0], coef, batch)
            salinity = update(q1.at[1], coef, batch)
            for g in batch:
                if PAD <= g < PAD + SX:
                    new[0, k, rows_at(g - PAD), :] = temperature[g]
                    new[1, k, rows_at(g - PAD), :] = salinity[g]
                total[rows_at(g), :] += temperature[g] - 0.8 * salinity[g]
        return carry

    lax.fori_loop(0, KL, level, 0)


def block_levels(tracers, east, north, levels, low, high):
    tall = (ROWS, 128)
    return pl.pallas_call(
        levels_kernel,
        out_shape=[jax.ShapeDtypeStruct(tracers.shape, F32), jax.ShapeDtypeStruct(tall, F32)],
        scratch_shapes=[pltpu.VMEM(s + tall, F32) for s in ((), (2,), (2,), (2,), (2,), (5,))],
        compiler_params=params(),
        cost_estimate=pl.CostEstimate(flops=20_000_000, bytes_accessed=6_000_000, transcendentals=0),
        name="block_levels",
    )(tracers, east, north, levels, low, high)


def operator_kernel(
    levels, low, high, own_rows, own_edges, one_in, two_in, blocked, wall_total,
    new, fields, sums,
    depth, strip_q, strip_depth, strip_face, strip_flow, strip_total, first_q, coef, total, field, grid, staged, sems, *, count,
):
    lane = lanes()
    member = lane % 8
    blank = jnp.zeros((8, 128), F32)
    strip_level = (lane // 8).astype(F32)
    first = lax.axis_index("gy") == 0
    last = lax.axis_index("gy") == count - 1

    def own(which, a, g):
        r = g - LOW
        if r < EDGE:
            return own_edges[which, a, rows_at(0), :]
        if r >= WIDE - EDGE:
            return own_edges[which, a, rows_at(8), :]
        return own_rows[which, a, rows_at(r - EDGE), :]

    halo_depth(levels, low, high, depth)
    parts = {}
    for g in GROUPS:
        sent = rows_at(g - LOW)
        parts[g] = (
            list(split_one(*(one_in[a, sent, :] for a in range(SENT)))),
            list(split_two(*(two_in[a, sent, :] for a in range(SENT)))),
        )
    for g in GROUPS:
        rows = rows_at(g)
        from_low, from_high = parts[g]
        from_low[4] = jnp.where(first, 0.0, from_low[4])
        from_high[4] = jnp.where(last, 0.0, from_high[4])
        for a in range(5):
            low_strip = jnp.where(member < 4, from_low[a], own(0, a, g))
            high_strip = jnp.where(member >= 3, from_high[a], own(1, a, g))
            for side, value in enumerate((low_strip, high_strip)):
                if a < 2:
                    strip_q[side, a, 0, rows, :] = value
                elif a < 4:
                    strip_flow[side, a - 2, rows, :] = value
                else:
                    strip_depth[side, rows, :] = value
    for outside in OUTSIDE:
        for side in range(2):
            strip_depth[side, rows_at(outside), :] = blank

    ahead = {
        (side, g): ahead_one(strip_depth[side, rows_at(g), :]) for side in range(2) for g in GROUPS
    }
    for (side, g), value in ahead.items():
        strip_face[side, rows_at(g), :] = jnp.minimum(strip_depth[side, rows_at(g), :], value)

    for side in range(2):
        at = strip_depth.at[side]

        def south(g, a_south, b_south, side=side):
            if side == 1:
                face = jnp.minimum(own(0, 4, g), own(1, 4, g))
                a_first, b_first = face_weights(face, own(0, 3, g), strip_level)
                a_south = jnp.where(member == 0, a_first, a_south)
                b_south = jnp.where(member == 0, b_first, b_south)
            return a_south, b_south

        set_weights(
            lambda g, at=at: at[rows_at(g), :],
            lambda g, at=at: jnp.minimum(at[rows_at(g), :], at[rows_at(g + 1), :]),
            lambda g, side=side: strip_face[side, rows_at(g), :],
            strip_flow.at[side],
            coef,
            strip_level,
            south,
        )
        for tracer in range(2):
            source = strip_q.at[side, tracer, 0]
            from_own = None
            if side == 1:

                def from_own(g, value, tracer=tracer):
                    return jnp.where(member == 0, own(0, tracer, g), value)

            for batch in BATCHES:
                for g, value in update(source, coef, batch, from_own).items():
                    strip_q[side, tracer, 1, rows_at(g), :] = value
        for batch in BATCHES:
            temperature = update(strip_q.at[side, 0, 1], coef, batch)
            salinity = update(strip_q.at[side, 1, 1], coef, batch)
            for g in batch:
                rows = rows_at(g)
                strip_q[side, 0, 0, rows, :] = temperature[g]
                strip_q[side, 1, 0, rows, :] = salinity[g]
                strip_total[side, rows, :] = temperature[g] - 0.8 * salinity[g]
    for turn in (8, 16, 32, 64):
        values = {}
        for side in range(2):
            for g in GROUPS:
                value = strip_total[side, rows_at(g), :]
                values[side, g] = value + pltpu.roll(value, turn, 1)
        for (side, g), value in values.items():
            strip_total[side, rows_at(g), :] = value

    for tracer in range(2):
        for g in range(PAD, PAD + SX, 8):
            rows = rows_at(g)
            high_value = pltpu.roll(strip_q[1, tracer, 0, rows, :], 1, 1)
            first_q[tracer, rows, :] = jnp.where(member >= 4, strip_q[0, tracer, 0, rows, :], high_value)
    from_strip = (lane < 2) | (lane >= 126)

    def place(k, carry):
        turn = 124 - 8 * k
        for tracer in range(2):
            values = {g: pltpu.roll(first_q[tracer, rows_at(g + PAD), :], turn, 1) for g in range(0, SX, 8)}
            for g, value in values.items():
                rows = rows_at(g)
                staged[tracer, k, rows, :] = jnp.where(from_strip, value, blocked[tracer, k, rows, :])
        for tracer in range(2):
            pltpu.make_async_copy(staged.at[tracer, k], new.at[tracer, k], sems.at[0]).start()
        return carry

    lax.fori_loop(0, KL, place, 0)

    def beside(low_value, high_value):
        return jnp.where(lane >= 64, pltpu.roll(low_value, 4, 1), pltpu.roll(high_value, 5, 1))

    def northward(main, side):
        a, b = ahead_one(main), ahead_one(side)
        return jnp.where(lane == 127, b, a), jnp.where(lane == 127, a, b)

    def southward(main, side):
        a, b = back_one(main), back_one(side)
        return jnp.where(lane == 0, b, a), jnp.where(lane == 0, a, b)

    for g in GROUPS + OUTSIDE:
        rows = rows_at(g)
        grid[0, 0, rows, :] = depth[rows, :]
        grid[0, 1, rows, :] = beside(strip_depth[0, rows, :], strip_depth[1, rows, :])
    for g in GROUPS:
        rows = rows_at(g)
        both = grid[0, 0, rows, :], grid[0, 1, rows, :]
        further = northward(*both)
        for part in range(2):
            grid[1, part, rows, :] = jnp.minimum(both[part], grid[0, part, rows_at(g + 1), :])
            grid[2, part, rows, :] = jnp.minimum(both[part], further[part])
        low_total = pltpu.roll(strip_total[0, rows, :], 4, 1)
        high_total = pltpu.roll(strip_total[1, rows, :], 5, 1)
        edge_total = jnp.where(lane < 64, low_total, high_total)
        total[0, rows, :] = jnp.where(from_strip, edge_total, wall_total[rows, :])
        total[1, rows, :] = jnp.where(lane >= 64, low_total, high_total)
    for part in range(2):
        grid[1, part, rows_at(LOW - 8), :] = blank
        for outside in OUTSIDE:
            for i in range(3):
                field[i, part, rows_at(outside), :] = blank
    scale = 1.0 / KL
    for g in GROUPS:
        rows = rows_at(g)
        souths = southward(grid[2, 0, rows, :], grid[2, 1, rows, :])
        for part in range(2):
            here = grid[0, part, rows, :]
            own_part = ALPHA * scale * here + jnp.where(here == 0.0, 1.0, 0.0)
            faces = grid[1, part, rows, :] + grid[1, part, rows_at(g - 1), :] + grid[2, part, rows, :] + souths[part]
            diagonal = own_part + scale * faces
            inverse = 1.0 / diagonal
            grid[3, part, rows, :] = inverse
            grid[4, part, rows, :] = own_part
            grid[5, part, rows, :] = diagonal
            field[0, part, rows, :] = 0.25 * total[part, rows, :] * inverse

    moments = [blank] * 6
    for i in range(3):
        for g in GROUPS:
            rows = rows_at(g)
            both = field[i, 0, rows, :], field[i, 1, rows, :]
            norths = northward(*both)
            souths = southward(*both)
            south_faces = southward(grid[2, 0, rows, :], grid[2, 1, rows, :])
            for part in range(2):
                if i == 2 and part == 1:
                    continue
                here = both[part]
                east_gap = here - field[i, part, rows_at(g + 1), :]
                north_gap = here - norths[part]
                east_face = scale * grid[1, part, rows, :]
                north_face = scale * grid[2, part, rows, :]
                own_part = grid[4, part, rows, :]
                if part == 0 and PAD <= g < PAD + SX:
                    moments[2 * i] += grid[5, 0, rows, :] * here * here
                    moments[2 * i + 1] += (
                        own_part * here * here + east_face * east_gap * east_gap + north_face * north_gap * north_gap
                    )
                if i < 2:
                    image = (
                        own_part * here
                        + east_face * east_gap
                        + scale * grid[1, part, rows_at(g - 1), :] * (here - field[i, part, rows_at(g - 1), :])
                        + north_face * north_gap
                        + scale * south_faces[part] * (here - souths[part])
                    )
                    field[i + 1, part, rows, :] = image * grid[3, part, rows, :]
        pltpu.make_async_copy(field.at[i, 0, PAD : PAD + SX, :], fields.at[i], sems.at[1]).start()
    row = jnp.zeros((8, 128), F32)
    for i in range(6):
        value = jnp.sum(jnp.sum(moments[i], axis=0, keepdims=True), axis=1, keepdims=True)
        row = jnp.where(lane == i, value, row)
    for g in range(0, 128, 8):
        sums[rows_at(g), :] = row
    pltpu.make_async_copy(field.at[:, 0, PAD : PAD + SX, :], fields, sems.at[1]).wait()
    pltpu.make_async_copy(staged, new, sems.at[0]).wait()


def operator(levels, low, high, own_rows, own_edges, one_in, two_in, blocked, wall_total, count):
    tall = (ROWS, 128)
    scratch = (
        (),
        (2, 2, 2),
        (2,),
        (2,),
        (2, 2),
        (2,),
        (2,),
        (5,),
        (2,),
        (3, 2),
        (6, 2),
    )
    return pl.pallas_call(
        functools.partial(operator_kernel, count=count),
        out_shape=[
            jax.ShapeDtypeStruct(blocked.shape, F32),
            pltpu.HBM((3, SX, SY), F32),
            jax.ShapeDtypeStruct((128, 128), F32),
        ],
        out_specs=[
            pl.BlockSpec(memory_space=pltpu.HBM),
            pl.BlockSpec(memory_space=pltpu.HBM),
            pl.BlockSpec(memory_space=pltpu.VMEM),
        ],
        scratch_shapes=[pltpu.VMEM(s + tall, F32) for s in scratch]
        + [pltpu.VMEM(blocked.shape, F32), pltpu.SemaphoreType.DMA((2,))],
        compiler_params=params(),
        name="operator",
    )(levels, low, high, own_rows, own_edges, one_in, two_in, blocked, wall_total)


def finish_kernel(sums_in, fields_in, out, sums, fields, sems):
    first_copy = pltpu.make_async_copy(sums_in, sums, sems.at[0])
    copy = pltpu.make_async_copy(fields_in, fields, sems.at[1])
    first_copy.start()
    copy.start()
    first_copy.wait()
    value = sums[0:8, :]
    for g in range(8, 128, 8):
        value = value + sums[rows_at(g), :]
    value = jnp.sum(value, axis=0, keepdims=True)
    lane = lanes((1, 128))
    m0, m1, m2, m3, m4, m5 = (
        jnp.sum(jnp.where(lane == i, value, 0.0), axis=1, keepdims=True) for i in range(6)
    )
    floor = 4e-7
    l10 = m2 / m1
    l20 = m3 / m1
    d1 = m3 - l10 * m2
    t = m4 - l20 * m2
    has1 = d1 > floor * m3
    l21 = jnp.where(has1, t / d1, 0.0)
    d2 = m5 - l20 * m3 - l21 * t
    has2 = has1 & (d2 > floor * m5)
    y1 = m1 - l10 * m0
    y2 = m2 - l20 * m0 - l21 * y1
    c2 = jnp.where(has2, y2 / d2, 0.0)
    c1 = jnp.where(has1, y1 / d1, 0.0) - l21 * c2
    c0 = m0 / m1 - l10 * c1 - l20 * c2
    copy.wait()
    for g in range(0, SX, 8):
        rows = rows_at(g)
        out[rows, :] = c0 * fields[0, rows, :] + c1 * fields[1, rows, :] + c2 * fields[2, rows, :]


def finish(sums, fields):
    return pl.pallas_call(
        finish_kernel,
        in_specs=[pl.BlockSpec(memory_space=pl.ANY)] * 2,
        out_shape=jax.ShapeDtypeStruct((SX, SY), F32),
        scratch_shapes=[
            pltpu.VMEM((128, 128), F32),
            pltpu.VMEM((3, SX, SY), F32),
            pltpu.SemaphoreType.DMA((2,)),
        ],
        name="finish",
    )(sums, pltpu.with_memory_space_constraint(fields, pltpu.HBM))


def shift(array, axis, step):
    count = lax.axis_size(axis)
    return lax.ppermute(array, axis, [(i, (i + step) % count) for i in range(count)])


def on_device(tracers, east, north, levels):
    before, after = edges(tracers, east, north, levels)
    before = shift(before, "gx", -1)
    after = shift(after, "gx", 1)
    own_rows, one, two = pack_rows(tracers, east, north, levels)
    own_edges, one, two, low, high = pack_edges(after, before, one, two)
    one_in = shift(one, "gy", 1)
    two_in = shift(two, "gy", -1)
    blocked, total = block_levels(tracers, east, north, levels, low, high)
    new, fields, sums = operator(
        levels, low, high, own_rows, own_edges, one_in, two_in, blocked, total, lax.axis_size("gy")
    )
    sums = lax.all_to_all(sums, ("gx", "gy"), split_axis=0, concat_axis=0, tiled=True)
    return new, finish(sums, fields)


def solution(mesh):
    placed = (P(None, None, "gx", "gy"), P(None, "gx", "gy"), P(None, "gx", "gy"), P("gx", "gy"))
    return jax.shard_map(
        on_device,
        mesh=mesh,
        in_specs=placed,
        out_specs=(P(None, None, "gx", "gy"), P("gx", "gy")),
        check_vma=False,
    )
```

```python
import functools

import jax
import jax.numpy as jnp
from jax import lax
from jax.experimental import pallas as pl
from jax.experimental.pallas import tpu as pltpu
from jax.sharding import PartitionSpec as P

KAPPA = 0.08
ALPHA = 0.05
F32 = jnp.float32

SX = 128
SY = 128
KL = 16
EDGE = 8
PAD = 16
ROWS = SX + 2 * PAD
WIDE = SX + 2 * EDGE
LOW = PAD - EDGE
ARRAYS = 2 * KL + 2 * KL + 1
VMEM = 40 * 1024 * 1024
GROUPS = tuple(range(LOW, LOW + WIDE, 8))
OUTSIDE = (LOW - 8, LOW + WIDE)
BATCHES = (GROUPS[:6], GROUPS[6:12], GROUPS[12:])
INNER = GROUPS[1:-1]
INNER_BATCHES = (INNER[:6], INNER[6:11], INNER[11:])
ENDS = (GROUPS[0], GROUPS[1], GROUPS[-2], GROUPS[-1])
END_BATCHES = (GROUPS[:3] + GROUPS[-3:],)
END_OUTSIDE = (GROUPS[0] - 8, GROUPS[3], GROUPS[-4], GROUPS[-1] + 8)
SENT = 3


def params():
    return pltpu.CompilerParams(vmem_limit_bytes=VMEM)


def rows_at(row):
    return slice(row, row + 8)


def lanes(shape=(8, 128)):
    return lax.broadcasted_iota(jnp.int32, shape, len(shape) - 1)


def ahead_one(value):
    return pltpu.roll(value, 127, 1)


def back_one(value):
    return pltpu.roll(value, 1, 1)


def offsets(counts):
    starts, at = [], 8
    for a in range(4):
        starts.append(at)
        at += KL * counts[a]
    return starts, at


NEXT = (4, 4, 4, 4)
BEFORE = (5, 5, 4, 4)
NEXT_AT, NEXT_ROWS = offsets(NEXT)
BEFORE_AT, BEFORE_ROWS = offsets(BEFORE)
BEFORE_ROWS += 8


def edges_kernel(t, e, n, d, before, after, tiles, flows, depths, sems):
    copies = []
    for side, at in enumerate((0, SX - 8)):
        at16 = 0 if side == 0 else SX - 16
        copies += [
            (t.at[0, :, at : at + 8, :], tiles.at[side, 0]),
            (t.at[1, :, at : at + 8, :], tiles.at[side, 1]),
            (e.at[:, at16 : at16 + 16, :], flows.at[side, 0]),
            (n.at[:, at16 : at16 + 16, :], flows.at[side, 1]),
            (d.at[at : at + 8, :], depths.at[side]),
        ]
    copies = [pltpu.make_async_copy(src, dst, sems.at[i]) for i, (src, dst) in enumerate(copies)]
    for copy in copies:
        copy.start()
    for side, (out, starts, counts) in enumerate(((before, BEFORE_AT, BEFORE), (after, NEXT_AT, NEXT))):
        for i in range(5):
            copies[5 * side + i].wait()
        out[0:8, :] = depths[side].astype(F32)
        for a in range(4):
            for k in range(KL):
                value = tiles[side, a, k] if a < 2 else flows[side, a - 2, k].astype(F32)[8 * side : 8 * side + 8]
                from_row = 0 if side == 0 else 8 - counts[a]
                at = starts[a] + counts[a] * k
                out[at : at + counts[a], :] = value[from_row : from_row + counts[a]]
    before[BEFORE_ROWS - 8 : BEFORE_ROWS, :] = jnp.zeros((8, 128), F32)


def edges(tracers, east, north, levels):
    return pl.pallas_call(
        edges_kernel,
        in_specs=[pl.BlockSpec(memory_space=pltpu.HBM)] * 4,
        out_shape=[pltpu.VMEM((rows, SY), F32) for rows in (BEFORE_ROWS, NEXT_ROWS)],
        scratch_shapes=[
            pltpu.VMEM((2, 2, KL, 8, SY), F32),
            pltpu.VMEM((2, 2, KL, 16, SY), jnp.bfloat16),
            pltpu.VMEM((2, 8, SY), jnp.int32),
            pltpu.SemaphoreType.DMA((10,)),
        ],
        compiler_params=params(),
        name="edges",
    )(*(pltpu.with_memory_space_constraint(x, pltpu.HBM) for x in (tracers, east, north, levels)))


def low_tile(ref, a, k):
    if a == 4:
        return ref[0:8, :]
    at = NEXT_AT[a] + NEXT[a] * (k + 1) - 8
    return ref[at : at + 8, :]


def high_tile(ref, a, k):
    if a == 4:
        return ref[0:8, :]
    at = BEFORE_AT[a] + BEFORE[a] * k
    return ref[at : at + 8, :]


def pack(source, rows, last):
    group = lanes((rows, 128)) // 8
    one = jnp.zeros((rows, 128), F32)
    beyond = jnp.zeros((rows, 128), F32)
    for k in range(KL):
        value = source(k)
        one = jnp.where(group == k, pltpu.roll(value, (8 * k - 124) % 128, 1), one)
        if last:
            beyond = jnp.where(group == k, pltpu.roll(value, (8 * k + 3) % 128, 1), beyond)
    two = pltpu.roll(one, 127, 1)
    if last:
        two = jnp.where(lanes((rows, 128)) % 8 == 7, beyond, two)
    return one, two


def pack_depth(sources):
    lane = lanes(sources[0].shape)
    values = [pltpu.roll(x, turn, 1) for turn in (4, 3) for x in sources]
    values = [jnp.where(lane < 8, x, 0.0) for x in values]
    for turn in (8, 16, 32, 64):
        values = [x + pltpu.roll(x, turn, 1) for x in values]
    return list(zip(values[: len(sources)], values[len(sources) :], strict=True))


def merge_one(t0, t1, e, n, d):
    member = lanes(t0.shape) % 8
    return (
        jnp.where(member < 4, t0, pltpu.roll(n, 4, 1)),
        jnp.where(member < 4, t1, pltpu.roll(e, 4, 1)),
        d,
    )


def split_one(a, b, c):
    return a, b, pltpu.roll(b, 124, 1), pltpu.roll(a, 124, 1), c


def merge_two(t0, t1, e, n, d):
    member = lanes(t0.shape) % 8
    return (
        jnp.where(member < 3, pltpu.roll(d, 125, 1), t0),
        jnp.where(member < 2, pltpu.roll(d, 122, 1), t1),
        jnp.where((member >= 3) & (member < 7), n, pltpu.roll(e, 4, 1)),
    )


def split_two(a, b, c):
    member = lanes(a.shape) % 8
    depth = jnp.where(member < 6, pltpu.roll(a, 3, 1), pltpu.roll(b, 6, 1))
    return a, b, pltpu.roll(c, 124, 1), c, depth


def pack_all(sources, depths, rows, own, own_rows, sent_one, sent_two, sent_rows):
    packed = [pack(source, rows, a < 2) for a, source in enumerate(sources)] + [depths]
    for which in range(2):
        for a in range(5):
            own[which, a, own_rows, :] = packed[a][which]
    for sent, values in (
        (sent_one, merge_one(*(p[0] for p in packed))),
        (sent_two, merge_two(*(p[1] for p in packed))),
    ):
        for a in range(SENT):
            sent[a, sent_rows, :] = values[a]


def pack_block(t, e, n, d, own, one, two):
    chunk = 16
    groups = range(0, SX, 8)
    for g, pair in zip(groups, pack_depth([d[rows_at(g), :].astype(F32) for g in groups]), strict=True):
        for which in range(2):
            own[which, 4, rows_at(g), :] = pair[which]

    def body(i, carry):
        rows = pl.ds(pl.multiple_of(i * chunk, chunk), chunk)
        sources = (
            lambda k: t[0, k, rows, :],
            lambda k: t[1, k, rows, :],
            lambda k: e[k, rows, :].astype(F32),
            lambda k: n[k, rows, :].astype(F32),
        )
        depths = own[0, 4, rows, :], own[1, 4, rows, :]
        pack_all(sources, depths, chunk, own, rows, one, two, rows)
        return carry

    lax.fori_loop(0, SX // chunk, body, 0)


def pack_edges_kernel(low_in, high_in, after, own, one, two, low, high):
    del after
    for a in range(5):
        for k in range(KL if a < 4 else 1):
            low[KL * a + k] = low_tile(low_in, a, k)
            high[KL * a + k] = high_tile(high_in, a, k)
    depths = pack_depth([low_tile(low_in, 4, 0), high_tile(high_in, 4, 0)])
    for side, (ref, tile) in enumerate(((low_in, low_tile), (high_in, high_tile))):
        sources = [functools.partial(tile, ref, a) for a in range(4)]
        pack_all(sources, depths[side], 8, own, rows_at(8 * side), one, two, rows_at(8 * side))


def pack_edges(low, high, after):
    sent = jax.ShapeDtypeStruct((SENT, 2 * EDGE, 128), F32)
    halo = jax.ShapeDtypeStruct((ARRAYS, EDGE, SY), F32)
    return pl.pallas_call(
        pack_edges_kernel,
        in_specs=[pl.BlockSpec(memory_space=pltpu.VMEM)] * 2 + [pl.BlockSpec(memory_space=pl.ANY)],
        out_shape=[jax.ShapeDtypeStruct((2, 5, 2 * EDGE, 128), F32), sent, sent, halo, halo],
        compiler_params=params(),
        name="pack_edges",
    )(low, high, after)


def face_weights(face, flow_value, threshold):
    is_open = face > threshold
    ahead = jnp.where(is_open, KAPPA + jnp.maximum(flow_value, 0.0), 0.0)
    back = jnp.where(is_open, KAPPA - jnp.minimum(flow_value, 0.0), 0.0)
    return ahead, back


def set_weights(batches, depth_at, face_east, face_north, flow, coef, threshold, south):
    for batch in batches:
        a_north, b_north = {}, {}
        for g in batch:
            rows = rows_at(g)
            a_east, b_east = face_weights(face_east(g), flow[0, rows, :], threshold)
            a_north[g], b_north[g] = face_weights(face_north(g), flow[1, rows, :], threshold)
            coef[0, rows, :] = a_east
            coef[1, rows, :] = b_east
            coef[2, rows, :] = b_north[g]
        a_south = {g: back_one(a_north[g]) for g in batch}
        b_south = {g: back_one(b_north[g]) for g in batch}
        for g in batch:
            rows = rows_at(g)
            a_here, b_here = south(g, a_south[g], b_south[g])
            coef[3, rows, :] = a_here
            leaving = coef[0, rows, :] + a_north[g] + coef[1, rows_at(g - 1), :] + b_here
            coef[4, rows, :] = jnp.where(depth_at(g) > threshold, 1.0 - leaving, 0.0)


def update(source, coef, batch, south_value=None):
    ahead = {g: ahead_one(source[rows_at(g), :]) for g in batch}
    back = {g: back_one(source[rows_at(g), :]) for g in batch}
    result = {}
    for g in batch:
        rows = rows_at(g)
        south = back[g] if south_value is None else south_value(g, back[g])
        result[g] = (
            coef[4, rows, :] * source[rows, :]
            + coef[1, rows, :] * source[rows_at(g + 1), :]
            + coef[0, rows_at(g - 1), :] * source[rows_at(g - 1), :]
            + coef[2, rows, :] * ahead[g]
            + coef[3, rows, :] * south
        )
    return result


def halo_depth(levels, low, high, depth):
    for g in GROUPS:
        r = g - LOW
        if r < EDGE:
            value = low[4 * KL]
        elif r >= WIDE - EDGE:
            value = high[4 * KL]
        else:
            value = levels[rows_at(r - EDGE), :].astype(F32)
        depth[rows_at(g), :] = value
    for outside in OUTSIDE:
        depth[rows_at(outside), :] = jnp.zeros((8, 128), F32)


def every_level(batches, results, load, store, depth, face, q0, q1, flow, coef):
    def level(k, carry):
        load(k)
        set_weights(
            batches,
            lambda g: depth[rows_at(g), :],
            lambda g: face[0, rows_at(g), :],
            lambda g: face[1, rows_at(g), :],
            flow,
            coef,
            k.astype(F32),
            lambda g, a, b: (a, b),
        )
        for tracer in range(2):
            for batch in batches:
                for g, value in update(q0.at[tracer], coef, batch).items():
                    q1[tracer, rows_at(g), :] = value
        for batch in results:
            temperature = update(q1.at[0], coef, batch)
            salinity = update(q1.at[1], coef, batch)
            for g in batch:
                store(k, g, temperature[g], salinity[g])
        return carry

    lax.fori_loop(0, KL, level, 0)


def set_faces(groups, depth, face):
    lane = lanes()
    ahead = {g: ahead_one(depth[rows_at(g), :]) for g in groups}
    for g in groups:
        rows = rows_at(g)
        here = depth[rows, :]
        face[0, rows, :] = jnp.minimum(here, depth[rows_at(g + 1), :])
        face[1, rows, :] = jnp.where(lane == 127, 0.0, jnp.minimum(here, ahead[g]))


def block_kernel(tracers, east, north, levels, after, own, one, two, new, total, depth, face, q0, q1, flow, coef):
    del after
    pack_block(tracers, east, north, levels, own, one, two)
    blank = jnp.zeros((8, 128), F32)
    for g in INNER:
        depth[rows_at(g), :] = levels[rows_at(g - PAD), :].astype(F32)
        total[rows_at(g), :] = blank
    for g in (GROUPS[0], GROUPS[-1]):
        depth[rows_at(g), :] = blank
        total[rows_at(g), :] = blank
        for i in range(2):
            coef[i, rows_at(g), :] = blank
            q0[i, rows_at(g), :] = blank
            q1[i, rows_at(g), :] = blank
    set_faces(INNER, depth, face)

    def load(k):
        for tracer in range(2):
            q0[tracer, PAD : PAD + SX, :] = tracers[tracer, k]
        flow[0, PAD : PAD + SX, :] = east[k].astype(F32)
        flow[1, PAD : PAD + SX, :] = north[k].astype(F32)

    def store(k, g, temperature, salinity):
        new[0, k, rows_at(g - PAD), :] = temperature
        new[1, k, rows_at(g - PAD), :] = salinity
        total[rows_at(g), :] += temperature - 0.8 * salinity

    every_level(INNER_BATCHES, INNER_BATCHES, load, store, depth, face, q0, q1, flow, coef)


LEVEL_SCRATCH = [pltpu.VMEM(shape + (ROWS, 128), F32) for shape in ((), (2,), (2,), (2,), (2,), (5,))]


def block(tracers, east, north, levels, after):
    sent = pltpu.VMEM((SENT, SX, 128), F32)
    return pl.pallas_call(
        block_kernel,
        in_specs=[pl.BlockSpec(memory_space=pltpu.VMEM)] * 4 + [pl.BlockSpec(memory_space=pl.ANY)],
        out_shape=[
            pltpu.VMEM((2, 5, SX, 128), F32),
            sent,
            sent,
            pltpu.VMEM(tracers.shape, F32),
            pltpu.VMEM((ROWS, 128), F32),
        ],
        scratch_shapes=LEVEL_SCRATCH,
        compiler_params=params(),
        cost_estimate=pl.CostEstimate(flops=20_000_000, bytes_accessed=24_000_000, transcendentals=0),
        name="block",
    )(tracers, east, north, levels, after)


def ends_kernel(tracers, east, north, levels, low, high, new, total, depth, face, q0, q1, flow, coef):
    blank = jnp.zeros((8, 128), F32)
    halo_depth(levels, low, high, depth)
    set_faces(END_BATCHES[0], depth, face)
    for g in ENDS:
        total[rows_at(g), :] = blank
    for at in END_OUTSIDE:
        for i in range(2):
            coef[i, rows_at(at), :] = blank
            q0[i, rows_at(at), :] = blank
            q1[i, rows_at(at), :] = blank

    def load(k):
        for g, ref in ((GROUPS[0], low), (GROUPS[-1], high)):
            for i in range(2):
                q0[i, rows_at(g), :] = ref[KL * i + k]
                flow[i, rows_at(g), :] = ref[KL * (2 + i) + k]
        for at in (0, SX - 16):
            rows = slice(at, at + 16)
            out = slice(PAD + at, PAD + at + 16)
            for tracer in range(2):
                q0[tracer, out, :] = tracers[tracer, k, rows, :]
            flow[0, out, :] = east[k, rows, :].astype(F32)
            flow[1, out, :] = north[k, rows, :].astype(F32)

    def store(k, g, temperature, salinity):
        if g == ENDS[1] or g == ENDS[2]:
            rows = rows_at(0 if g == ENDS[1] else 8)
            new[0, k, rows, :] = temperature
            new[1, k, rows, :] = salinity
        total[rows_at(g), :] += temperature - 0.8 * salinity

    every_level(END_BATCHES, (ENDS,), load, store, depth, face, q0, q1, flow, coef)


def end_levels(tracers, east, north, levels, low, high):
    return pl.pallas_call(
        ends_kernel,
        out_shape=[pltpu.VMEM((2, KL, 16, SY), F32), pltpu.VMEM((ROWS, 128), F32)],
        scratch_shapes=LEVEL_SCRATCH,
        compiler_params=params(),
        cost_estimate=pl.CostEstimate(flops=5_000_000, bytes_accessed=6_000_000, transcendentals=0),
        name="end_levels",
    )(tracers, east, north, levels, low, high)


def operator_kernel(
    levels, low, high, own_rows, own_edges, one_rows, two_rows, one_edges, two_edges,
    blocked, ends, wall_total, ends_total,
    new, fields, sums,
    depth, strip_q, strip_depth, strip_face, strip_flow, strip_total, first_q, coef, total, field, grid, staged, sems, *, count,
):
    lane = lanes()
    member = lane % 8
    blank = jnp.zeros((8, 128), F32)
    strip_level = (lane // 8).astype(F32)
    first = lax.axis_index("gy") == 0
    last = lax.axis_index("gy") == count - 1

    def own(which, a, g):
        r = g - LOW
        if r < EDGE:
            return own_edges[which, a, rows_at(0), :]
        if r >= WIDE - EDGE:
            return own_edges[which, a, rows_at(8), :]
        return own_rows[which, a, rows_at(r - EDGE), :]

    def sent(of_rows, of_edges, g):
        r = g - LOW
        if r < EDGE:
            ref, rows = of_edges, rows_at(0)
        elif r >= WIDE - EDGE:
            ref, rows = of_edges, rows_at(8)
        else:
            ref, rows = of_rows, rows_at(r - EDGE)
        return [ref[a, rows, :] for a in range(SENT)]

    halo_depth(levels, low, high, depth)
    parts = {}
    for g in GROUPS:
        parts[g] = (
            list(split_one(*sent(one_rows, one_edges, g))),
            list(split_two(*sent(two_rows, two_edges, g))),
        )
    for g in GROUPS:
        rows = rows_at(g)
        from_low, from_high = parts[g]
        from_low[4] = jnp.where(first, 0.0, from_low[4])
        from_high[4] = jnp.where(last, 0.0, from_high[4])
        for a in range(5):
            low_strip = jnp.where(member < 4, from_low[a], own(0, a, g))
            high_strip = jnp.where(member >= 3, from_high[a], own(1, a, g))
            for side, value in enumerate((low_strip, high_strip)):
                if a < 2:
                    strip_q[side, a, 0, rows, :] = value
                elif a < 4:
                    strip_flow[side, a - 2, rows, :] = value
                else:
                    strip_depth[side, rows, :] = value
    for outside in OUTSIDE:
        for side in range(2):
            strip_depth[side, rows_at(outside), :] = blank

    ahead = {
        (side, g): ahead_one(strip_depth[side, rows_at(g), :]) for side in range(2) for g in GROUPS
    }
    for (side, g), value in ahead.items():
        strip_face[side, rows_at(g), :] = jnp.minimum(strip_depth[side, rows_at(g), :], value)

    for side in range(2):
        at = strip_depth.at[side]

        def south(g, a_south, b_south, side=side):
            if side == 1:
                face = jnp.minimum(own(0, 4, g), own(1, 4, g))
                a_first, b_first = face_weights(face, own(0, 3, g), strip_level)
                a_south = jnp.where(member == 0, a_first, a_south)
                b_south = jnp.where(member == 0, b_first, b_south)
            return a_south, b_south

        coef[1, rows_at(LOW - 8), :] = blank
        set_weights(
            BATCHES,
            lambda g, at=at: at[rows_at(g), :],
            lambda g, at=at: jnp.minimum(at[rows_at(g), :], at[rows_at(g + 1), :]),
            lambda g, side=side: strip_face[side, rows_at(g), :],
            strip_flow.at[side],
            coef,
            strip_level,
            south,
        )
        for tracer in range(2):
            source = strip_q.at[side, tracer, 0]
            from_own = None
            if side == 1:

                def from_own(g, value, tracer=tracer):
                    return jnp.where(member == 0, own(0, tracer, g), value)

            for batch in BATCHES:
                for g, value in update(source, coef, batch, from_own).items():
                    strip_q[side, tracer, 1, rows_at(g), :] = value
        for batch in BATCHES:
            temperature = update(strip_q.at[side, 0, 1], coef, batch)
            salinity = update(strip_q.at[side, 1, 1], coef, batch)
            for g in batch:
                rows = rows_at(g)
                strip_q[side, 0, 0, rows, :] = temperature[g]
                strip_q[side, 1, 0, rows, :] = salinity[g]
                strip_total[side, rows, :] = temperature[g] - 0.8 * salinity[g]
    for turn in (8, 16, 32, 64):
        values = {}
        for side in range(2):
            for g in GROUPS:
                value = strip_total[side, rows_at(g), :]
                values[side, g] = value + pltpu.roll(value, turn, 1)
        for (side, g), value in values.items():
            strip_total[side, rows_at(g), :] = value

    for tracer in range(2):
        for g in range(PAD, PAD + SX, 8):
            rows = rows_at(g)
            high_value = pltpu.roll(strip_q[1, tracer, 0, rows, :], 1, 1)
            first_q[tracer, rows, :] = jnp.where(member >= 4, strip_q[0, tracer, 0, rows, :], high_value)
    from_strip = (lane < 2) | (lane >= 126)

    def place(k, carry):
        turn = 124 - 8 * k
        for tracer in range(2):
            values = {g: pltpu.roll(first_q[tracer, rows_at(g + PAD), :], turn, 1) for g in range(0, SX, 8)}
            for g, value in values.items():
                rows = rows_at(g)
                if g == 0 or g == SX - 8:
                    here = ends[tracer, k, rows_at(0 if g == 0 else 8), :]
                else:
                    here = blocked[tracer, k, rows, :]
                staged[tracer, k, rows, :] = jnp.where(from_strip, value, here)
        for tracer in range(2):
            pltpu.make_async_copy(staged.at[tracer, k], new.at[tracer, k], sems.at[0]).start()
        return carry

    lax.fori_loop(0, KL, place, 0)

    def beside(low_value, high_value):
        return jnp.where(lane >= 64, pltpu.roll(low_value, 4, 1), pltpu.roll(high_value, 5, 1))

    def northward(main, side):
        a, b = ahead_one(main), ahead_one(side)
        return jnp.where(lane == 127, b, a), jnp.where(lane == 127, a, b)

    def southward(main, side):
        a, b = back_one(main), back_one(side)
        return jnp.where(lane == 0, b, a), jnp.where(lane == 0, a, b)

    for g in GROUPS + OUTSIDE:
        rows = rows_at(g)
        grid[0, 0, rows, :] = depth[rows, :]
        grid[0, 1, rows, :] = beside(strip_depth[0, rows, :], strip_depth[1, rows, :])
    for g in GROUPS:
        rows = rows_at(g)
        both = grid[0, 0, rows, :], grid[0, 1, rows, :]
        further = northward(*both)
        for part in range(2):
            grid[1, part, rows, :] = jnp.minimum(both[part], grid[0, part, rows_at(g + 1), :])
            grid[2, part, rows, :] = jnp.minimum(both[part], further[part])
        low_total = pltpu.roll(strip_total[0, rows, :], 4, 1)
        high_total = pltpu.roll(strip_total[1, rows, :], 5, 1)
        edge_total = jnp.where(lane < 64, low_total, high_total)
        here = (ends_total if g in ENDS else wall_total)[rows, :]
        total[0, rows, :] = jnp.where(from_strip, edge_total, here)
        total[1, rows, :] = jnp.where(lane >= 64, low_total, high_total)
    for part in range(2):
        grid[1, part, rows_at(LOW - 8), :] = blank
        for outside in OUTSIDE:
            for i in range(3):
                field[i, part, rows_at(outside), :] = blank
    scale = 1.0 / KL
    for g in GROUPS:
        rows = rows_at(g)
        souths = southward(grid[2, 0, rows, :], grid[2, 1, rows, :])
        for part in range(2):
            here = grid[0, part, rows, :]
            own_part = ALPHA * scale * here + jnp.where(here == 0.0, 1.0, 0.0)
            faces = grid[1, part, rows, :] + grid[1, part, rows_at(g - 1), :] + grid[2, part, rows, :] + souths[part]
            diagonal = own_part + scale * faces
            inverse = 1.0 / diagonal
            grid[3, part, rows, :] = inverse
            grid[4, part, rows, :] = own_part
            grid[5, part, rows, :] = diagonal
            field[0, part, rows, :] = 0.25 * total[part, rows, :] * inverse

    moments = [blank] * 6
    for i in range(3):
        for g in GROUPS:
            rows = rows_at(g)
            both = field[i, 0, rows, :], field[i, 1, rows, :]
            norths = northward(*both)
            souths = southward(*both)
            south_faces = southward(grid[2, 0, rows, :], grid[2, 1, rows, :])
            for part in range(2):
                if i == 2 and part == 1:
                    continue
                here = both[part]
                east_gap = here - field[i, part, rows_at(g + 1), :]
                north_gap = here - norths[part]
                east_face = scale * grid[1, part, rows, :]
                north_face = scale * grid[2, part, rows, :]
                own_part = grid[4, part, rows, :]
                if part == 0 and PAD <= g < PAD + SX:
                    moments[2 * i] += grid[5, 0, rows, :] * here * here
                    moments[2 * i + 1] += (
                        own_part * here * here + east_face * east_gap * east_gap + north_face * north_gap * north_gap
                    )
                if i < 2:
                    image = (
                        own_part * here
                        + east_face * east_gap
                        + scale * grid[1, part, rows_at(g - 1), :] * (here - field[i, part, rows_at(g - 1), :])
                        + north_face * north_gap
                        + scale * south_faces[part] * (here - souths[part])
                    )
                    field[i + 1, part, rows, :] = image * grid[3, part, rows, :]
        pltpu.make_async_copy(field.at[i, 0, PAD : PAD + SX, :], fields.at[i], sems.at[1]).start()
    row = jnp.zeros((8, 128), F32)
    for i in range(6):
        value = jnp.sum(jnp.sum(moments[i], axis=0, keepdims=True), axis=1, keepdims=True)
        row = jnp.where(lane == i, value, row)
    for g in range(0, 128, 8):
        sums[rows_at(g), :] = row
    pltpu.make_async_copy(field.at[:, 0, PAD : PAD + SX, :], fields, sems.at[1]).wait()
    pltpu.make_async_copy(staged, new, sems.at[0]).wait()


def operator(*arrays, count):
    tall = (ROWS, 128)
    scratch = (
        (),
        (2, 2, 2),
        (2,),
        (2,),
        (2, 2),
        (2,),
        (2,),
        (5,),
        (2,),
        (3, 2),
        (6, 2),
    )
    return pl.pallas_call(
        functools.partial(operator_kernel, count=count),
        out_shape=[
            jax.ShapeDtypeStruct((2, KL, SX, SY), F32),
            pltpu.HBM((3, SX, SY), F32),
            jax.ShapeDtypeStruct((128, 128), F32),
        ],
        out_specs=[
            pl.BlockSpec(memory_space=pltpu.HBM),
            pl.BlockSpec(memory_space=pltpu.HBM),
            pl.BlockSpec(memory_space=pltpu.VMEM),
        ],
        scratch_shapes=[pltpu.VMEM(s + tall, F32) for s in scratch]
        + [pltpu.VMEM((2, KL, SX, SY), F32), pltpu.SemaphoreType.DMA((2,))],
        compiler_params=params(),
        name="operator",
    )(*arrays)


def finish_kernel(sums_in, fields_in, out, sums, fields, sems):
    first_copy = pltpu.make_async_copy(sums_in, sums, sems.at[0])
    copy = pltpu.make_async_copy(fields_in, fields, sems.at[1])
    first_copy.start()
    copy.start()
    first_copy.wait()
    value = sums[0:8, :]
    for g in range(8, 128, 8):
        value = value + sums[rows_at(g), :]
    value = jnp.sum(value, axis=0, keepdims=True)
    lane = lanes((1, 128))
    m0, m1, m2, m3, m4, m5 = (
        jnp.sum(jnp.where(lane == i, value, 0.0), axis=1, keepdims=True) for i in range(6)
    )
    floor = 4e-7
    l10 = m2 / m1
    l20 = m3 / m1
    d1 = m3 - l10 * m2
    t = m4 - l20 * m2
    has1 = d1 > floor * m3
    l21 = jnp.where(has1, t / d1, 0.0)
    d2 = m5 - l20 * m3 - l21 * t
    has2 = has1 & (d2 > floor * m5)
    y1 = m1 - l10 * m0
    y2 = m2 - l20 * m0 - l21 * y1
    c2 = jnp.where(has2, y2 / d2, 0.0)
    c1 = jnp.where(has1, y1 / d1, 0.0) - l21 * c2
    c0 = m0 / m1 - l10 * c1 - l20 * c2
    copy.wait()
    for g in range(0, SX, 8):
        rows = rows_at(g)
        out[rows, :] = c0 * fields[0, rows, :] + c1 * fields[1, rows, :] + c2 * fields[2, rows, :]


def finish(sums, fields):
    return pl.pallas_call(
        finish_kernel,
        in_specs=[pl.BlockSpec(memory_space=pl.ANY)] * 2,
        out_shape=jax.ShapeDtypeStruct((SX, SY), F32),
        scratch_shapes=[
            pltpu.VMEM((128, 128), F32),
            pltpu.VMEM((3, SX, SY), F32),
            pltpu.SemaphoreType.DMA((2,)),
        ],
        name="finish",
    )(sums, pltpu.with_memory_space_constraint(fields, pltpu.HBM))


def shift(array, axis, step, around):
    count = lax.axis_size(axis)
    pairs = [(i, (i + step) % count) for i in range(count) if around or 0 <= i + step < count]
    return lax.ppermute(array, axis, pairs)


def on_device(tracers, east, north, levels):
    to_before, to_after = edges(tracers, east, north, levels)
    before = shift(to_before, "gx", -1, True)
    after = shift(to_after, "gx", 1, True)
    own_rows, one, two, blocked, total = block(tracers, east, north, levels, to_before)
    one, two, after, before = lax.optimization_barrier((one, two, after, before))
    one_rows = shift(one, "gy", 1, False)
    two_rows = shift(two, "gy", -1, False)
    own_edges, one, two, low, high = pack_edges(after, before, total)
    one_edges = shift(one, "gy", 1, False)
    two_edges = shift(two, "gy", -1, False)
    ends, ends_total = end_levels(tracers, east, north, levels, low, high)
    new, fields, sums = operator(
        levels, low, high, own_rows, own_edges, one_rows, two_rows, one_edges, two_edges,
        blocked, ends, total, ends_total, count=lax.axis_size("gy"),
    )
    sums = lax.all_to_all(sums, ("gx", "gy"), split_axis=0, concat_axis=0, tiled=True)
    return new, finish(sums, fields)


def solution(mesh):
    placed = (P(None, None, "gx", "gy"), P(None, "gx", "gy"), P(None, "gx", "gy"), P("gx", "gy"))
    return jax.shard_map(
        on_device,
        mesh=mesh,
        in_specs=placed,
        out_specs=(P(None, None, "gx", "gy"), P("gx", "gy")),
        check_vma=False,
    )
```

```python
import functools

import jax
import jax.numpy as jnp
from jax import lax
from jax.experimental import pallas as pl
from jax.experimental.pallas import tpu as pltpu
from jax.sharding import PartitionSpec as P

KAPPA = 0.08
ALPHA = 0.05
F32 = jnp.float32

SX = 128
SY = 128
KL = 16
EDGE = 8
PAD = 16
ROWS = SX + 2 * PAD
WIDE = SX + 2 * EDGE
LOW = PAD - EDGE
ARRAYS = 2 * KL + 2 * KL + 1
VMEM = 40 * 1024 * 1024
GROUPS = tuple(range(LOW, LOW + WIDE, 8))
OUTSIDE = (LOW - 8, LOW + WIDE)
INNER = GROUPS[1:-1]
END_GROUPS = (8, 24, 32)
END_ROWS = 48
SENT = 3


def params():
    return pltpu.CompilerParams(vmem_limit_bytes=VMEM)


def is_even(axis):
    return lax.rem(lax.axis_index(axis), 2) == 0


def rows_at(row):
    return slice(row, row + 8)


def lanes(shape=(8, 128)):
    return lax.broadcasted_iota(jnp.int32, shape, len(shape) - 1)


def ahead_one(value):
    return pltpu.roll(value, 127, 1)


def back_one(value):
    return pltpu.roll(value, 1, 1)


def offsets(counts):
    starts, at = [], 8
    for a in range(4):
        starts.append(at)
        at += KL * counts[a]
    return starts, at


NEXT = (4, 4, 4, 4)
BEFORE = (5, 5, 4, 4)
NEXT_AT, NEXT_ROWS = offsets(NEXT)
BEFORE_AT, BEFORE_ROWS = offsets(BEFORE)
BEFORE_ROWS += 8
assert NEXT_ROWS <= BEFORE_ROWS


def edges_kernel(t, e, n, d, first_pair, second_pair, tiles, flows, depths, sems):
    copies = []
    for side, at in enumerate((0, SX - 8)):
        at16 = 0 if side == 0 else SX - 16
        copies += [
            (t.at[0, :, at : at + 8, :], tiles.at[side, 0]),
            (t.at[1, :, at : at + 8, :], tiles.at[side, 1]),
            (e.at[:, at16 : at16 + 16, :], flows.at[side, 0]),
            (n.at[:, at16 : at16 + 16, :], flows.at[side, 1]),
            (d.at[at : at + 8, :], depths.at[side]),
        ]
    copies = [pltpu.make_async_copy(src, dst, sems.at[i]) for i, (src, dst) in enumerate(copies)]
    for copy in copies:
        copy.start()
    for copy in copies:
        copy.wait()

    def write(before, after):
        for side, (out, starts, counts) in enumerate(((before, BEFORE_AT, BEFORE), (after, NEXT_AT, NEXT))):
            out[0:8, :] = depths[side].astype(F32)
            for a in range(4):
                for k in range(KL):
                    value = tiles[side, a, k] if a < 2 else flows[side, a - 2, k].astype(F32)[8 * side : 8 * side + 8]
                    from_row = 0 if side == 0 else 8 - counts[a]
                    at = starts[a] + counts[a] * k
                    out[at : at + counts[a], :] = value[from_row : from_row + counts[a]]
        before[BEFORE_ROWS - 8 : BEFORE_ROWS, :] = jnp.zeros((8, 128), F32)
        after[NEXT_ROWS:BEFORE_ROWS, :] = jnp.zeros((BEFORE_ROWS - NEXT_ROWS, 128), F32)

    @pl.when(is_even("gx"))
    def _():
        write(second_pair, first_pair)

    @pl.when(~is_even("gx"))
    def _():
        write(first_pair, second_pair)


def edges(tracers, east, north, levels):
    return pl.pallas_call(
        edges_kernel,
        in_specs=[pl.BlockSpec(memory_space=pltpu.HBM)] * 4,
        out_shape=[pltpu.VMEM((BEFORE_ROWS, SY), F32)] * 2,
        scratch_shapes=[
            pltpu.VMEM((2, 2, KL, 8, SY), F32),
            pltpu.VMEM((2, 2, KL, 16, SY), jnp.bfloat16),
            pltpu.VMEM((2, 8, SY), jnp.int32),
            pltpu.SemaphoreType.DMA((10,)),
        ],
        compiler_params=params(),
        name="edges",
    )(*(pltpu.with_memory_space_constraint(x, pltpu.HBM) for x in (tracers, east, north, levels)))


def low_tile(ref, a, k):
    if a == 4:
        return ref[0:8, :]
    at = NEXT_AT[a] + NEXT[a] * (k + 1) - 8
    return ref[at : at + 8, :]


def high_tile(ref, a, k):
    if a == 4:
        return ref[0:8, :]
    at = BEFORE_AT[a] + BEFORE[a] * k
    return ref[at : at + 8, :]


def pack(source, rows, last):
    group = lanes((rows, 128)) // 8
    one = jnp.zeros((rows, 128), F32)
    beyond = jnp.zeros((rows, 128), F32)
    for k in range(KL):
        value = source(k)
        one = jnp.where(group == k, pltpu.roll(value, (8 * k - 124) % 128, 1), one)
        if last:
            beyond = jnp.where(group == k, pltpu.roll(value, (8 * k + 3) % 128, 1), beyond)
    two = pltpu.roll(one, 127, 1)
    if last:
        two = jnp.where(lanes((rows, 128)) % 8 == 7, beyond, two)
    return one, two


def pack_depth(sources):
    lane = lanes(sources[0].shape)
    values = [pltpu.roll(x, turn, 1) for turn in (4, 3) for x in sources]
    values = [jnp.where(lane < 8, x, 0.0) for x in values]
    for turn in (8, 16, 32, 64):
        values = [x + pltpu.roll(x, turn, 1) for x in values]
    return list(zip(values[: len(sources)], values[len(sources) :], strict=True))


def merge_one(t0, t1, e, n, d):
    member = lanes(t0.shape) % 8
    return (
        jnp.where(member < 4, t0, pltpu.roll(n, 4, 1)),
        jnp.where(member < 4, t1, pltpu.roll(e, 4, 1)),
        d,
    )


def split_one(a, b, c):
    return a, b, pltpu.roll(b, 124, 1), pltpu.roll(a, 124, 1), c


def merge_two(t0, t1, e, n, d):
    member = lanes(t0.shape) % 8
    return (
        jnp.where(member < 3, pltpu.roll(d, 125, 1), t0),
        jnp.where(member < 2, pltpu.roll(d, 122, 1), t1),
        jnp.where((member >= 3) & (member < 7), n, pltpu.roll(e, 4, 1)),
    )


def split_two(a, b, c):
    member = lanes(a.shape) % 8
    depth = jnp.where(member < 6, pltpu.roll(a, 3, 1), pltpu.roll(b, 6, 1))
    return a, b, pltpu.roll(c, 124, 1), c, depth


def pack_all(sources, depths, rows, own, own_rows, first_pair, second_pair, sent_rows):
    packed = [pack(source, rows, a < 2) for a, source in enumerate(sources)] + [depths]
    for which in range(2):
        for a in range(5):
            own[which, a, own_rows, :] = packed[a][which]
    even = is_even("gy")
    ones = merge_one(*(p[0] for p in packed))
    twos = merge_two(*(p[1] for p in packed))
    for a in range(SENT):
        first_pair[a, sent_rows, :] = jnp.where(even, ones[a], twos[a])
        second_pair[a, sent_rows, :] = jnp.where(even, twos[a], ones[a])


def pack_block(t, e, n, d, own, one, two):
    chunk = 32
    groups = range(0, SX, 8)
    for g, pair in zip(groups, pack_depth([d[rows_at(g), :].astype(F32) for g in groups]), strict=True):
        for which in range(2):
            own[which, 4, rows_at(g), :] = pair[which]

    def body(i, carry):
        rows = pl.ds(pl.multiple_of(i * chunk, chunk), chunk)
        sources = (
            lambda k: t[0, k, rows, :],
            lambda k: t[1, k, rows, :],
            lambda k: e[k, rows, :].astype(F32),
            lambda k: n[k, rows, :].astype(F32),
        )
        depths = own[0, 4, rows, :], own[1, 4, rows, :]
        pack_all(sources, depths, chunk, own, rows, one, two, rows)
        return carry

    lax.fori_loop(0, SX // chunk, body, 0)


def pack_edges_kernel(first_pair, second_pair, after, own, one, two, low, high, low_in, high_in):
    del after
    even = is_even("gx")
    for at in range(0, BEFORE_ROWS, 8):
        rows = rows_at(at)
        value, other = first_pair[rows, :], second_pair[rows, :]
        low_in[rows, :] = jnp.where(even, other, value)
        high_in[rows, :] = jnp.where(even, value, other)
    for a in range(5):
        for k in range(KL if a < 4 else 1):
            low[KL * a + k] = low_tile(low_in, a, k)
            high[KL * a + k] = high_tile(high_in, a, k)
    depths = pack_depth([low_tile(low_in, 4, 0), high_tile(high_in, 4, 0)])
    for side, (ref, tile) in enumerate(((low_in, low_tile), (high_in, high_tile))):
        sources = [functools.partial(tile, ref, a) for a in range(4)]
        pack_all(sources, depths[side], 8, own, rows_at(8 * side), one, two, rows_at(8 * side))


def pack_edges(low, high, after):
    sent = jax.ShapeDtypeStruct((SENT, 2 * EDGE, 128), F32)
    halo = jax.ShapeDtypeStruct((ARRAYS, EDGE, SY), F32)
    return pl.pallas_call(
        pack_edges_kernel,
        in_specs=[pl.BlockSpec(memory_space=pltpu.VMEM)] * 2 + [pl.BlockSpec(memory_space=pl.ANY)],
        out_shape=[jax.ShapeDtypeStruct((2, 5, 2 * EDGE, 128), F32), sent, sent, halo, halo],
        scratch_shapes=[pltpu.VMEM((BEFORE_ROWS, SY), F32)] * 2,
        compiler_params=params(),
        name="pack_edges",
    )(low, high, after)


def face_weights(face, flow_value, threshold):
    is_open = face > threshold
    ahead = jnp.where(is_open, KAPPA + jnp.maximum(flow_value, 0.0), 0.0)
    back = jnp.where(is_open, KAPPA - jnp.minimum(flow_value, 0.0), 0.0)
    return ahead, back


def two_steps(copies, groups, threshold, depth_at, faces, flow, coef, q0, q1, first_row=None):
    parts = [(c, g) for c in range(copies) for g in groups]
    every = [(c, t, g) for c, g in parts for t in range(2)]
    for c, g in parts:
        rows = rows_at(g)
        east, north = faces(c, g)
        coef[c, 0, rows, :], coef[c, 1, rows, :] = face_weights(east, flow[c, 0, rows, :], threshold(c))
        coef[c, 3, rows, :], coef[c, 2, rows, :] = face_weights(north, flow[c, 1, rows, :], threshold(c))
    b_south = {(c, g): back_one(coef[c, 2, rows_at(g), :]) for c, g in parts}

    def shifted(source):
        ahead = {(c, t, g): ahead_one(source[c, t, rows_at(g), :]) for c, t, g in every}
        behind = {
            (c, t, g): back_one(coef[c, 3, rows_at(g), :] * source[c, t, rows_at(g), :]) for c, t, g in every
        }
        return ahead, behind

    def combine(source, c, t, g, ahead, behind):
        rows = rows_at(g)
        return (
            coef[c, 4, rows, :] * source[c, t, rows, :]
            + coef[c, 1, rows, :] * source[c, t, rows_at(g + 1), :]
            + coef[c, 0, rows_at(g - 1), :] * source[c, t, rows_at(g - 1), :]
            + coef[c, 2, rows, :] * ahead
            + behind
        )

    ahead, behind = shifted(q0)
    for c, g in parts:
        rows = rows_at(g)
        b_here = b_south[c, g]
        if first_row is not None:
            b_here, behind[c, 0, g], behind[c, 1, g] = first_row(c, g, b_here, behind[c, 0, g], behind[c, 1, g])
        leaving = coef[c, 0, rows, :] + coef[c, 3, rows, :] + coef[c, 1, rows_at(g - 1), :] + b_here
        coef[c, 4, rows, :] = jnp.where(depth_at(c, g) > threshold(c), 1.0 - leaving, 0.0)
        for t in range(2):
            q1[c, t, rows, :] = combine(q0, c, t, g, ahead[c, t, g], behind[c, t, g])
    ahead, behind = shifted(q1)
    for c, g in parts:
        yield c, g, *(combine(q1, c, t, g, ahead[c, t, g], behind[c, t, g]) for t in range(2))


def halo_depth(levels, low, high, depth):
    for g in GROUPS:
        r = g - LOW
        if r < EDGE:
            value = low[4 * KL]
        elif r >= WIDE - EDGE:
            value = high[4 * KL]
        else:
            value = levels[rows_at(r - EDGE), :].astype(F32)
        depth[rows_at(g), :] = value
    for outside in OUTSIDE:
        depth[rows_at(outside), :] = jnp.zeros((8, 128), F32)


LEVELS = 2
END_LEVELS = 4


def set_faces(groups, depth, face):
    lane = lanes()
    ahead = {g: ahead_one(depth[rows_at(g), :]) for g in groups}
    for g in groups:
        rows = rows_at(g)
        here = depth[rows, :]
        face[0, rows, :] = jnp.minimum(here, depth[rows_at(g + 1), :])
        face[1, rows, :] = jnp.where(lane == 127, 0.0, jnp.minimum(here, ahead[g]))


def block_kernel(
    tracers, east, north, levels, after, own, first_pair, second_pair, new, total, depth, face, q0, q1, flow, coef
):
    del after
    pack_block(tracers, east, north, levels, own, first_pair, second_pair)
    blank = jnp.zeros((8, 128), F32)
    for g in INNER:
        depth[rows_at(g), :] = levels[rows_at(g - PAD), :].astype(F32)
        total[rows_at(g), :] = blank
    for g in (GROUPS[0], GROUPS[-1]):
        depth[rows_at(g), :] = blank
        total[rows_at(g), :] = blank
        for c in range(LEVELS):
            for i in range(2):
                coef[c, i, rows_at(g), :] = blank
                q0[c, i, rows_at(g), :] = blank
                q1[c, i, rows_at(g), :] = blank
    set_faces(INNER, depth, face)

    def some_levels(i, carry):
        for c in range(LEVELS):
            k = LEVELS * i + c
            for t in range(2):
                q0[c, t, PAD : PAD + SX, :] = tracers[t, k]
            flow[c, 0, PAD : PAD + SX, :] = east[k].astype(F32)
            flow[c, 1, PAD : PAD + SX, :] = north[k].astype(F32)
        for c, g, temperature, salinity in two_steps(
            LEVELS,
            INNER,
            lambda c: (LEVELS * i + c).astype(F32),
            lambda c, g: depth[rows_at(g), :],
            lambda c, g: (face[0, rows_at(g), :], face[1, rows_at(g), :]),
            flow,
            coef,
            q0,
            q1,
        ):
            new[0, LEVELS * i + c, rows_at(g - PAD), :] = temperature
            new[1, LEVELS * i + c, rows_at(g - PAD), :] = salinity
            total[rows_at(g), :] += temperature - 0.8 * salinity
        return carry

    lax.fori_loop(0, KL // LEVELS, some_levels, 0)


def level_scratch(rows, copies):
    shapes = ((), (2,), (copies, 2), (copies, 2), (copies, 2), (copies, 5))
    return [pltpu.VMEM(shape + (rows, 128), F32) for shape in shapes]


def block(tracers, east, north, levels, after):
    sent = pltpu.VMEM((SENT, SX, 128), F32)
    return pl.pallas_call(
        block_kernel,
        in_specs=[pl.BlockSpec(memory_space=pltpu.VMEM)] * 4 + [pl.BlockSpec(memory_space=pl.ANY)],
        out_shape=[
            pltpu.VMEM((2, 5, SX, 128), F32),
            sent,
            sent,
            pltpu.VMEM(tracers.shape, F32),
            pltpu.VMEM((ROWS, 128), F32),
        ],
        scratch_shapes=level_scratch(ROWS, LEVELS),
        compiler_params=params(),
        cost_estimate=pl.CostEstimate(flops=20_000_000, bytes_accessed=24_000_000, transcendentals=0),
        name="block",
    )(tracers, east, north, levels, after)


def ends_kernel(tracers, east, north, levels, low, high, new, total, depth, face, q0, q1, flow, coef):
    blank = jnp.zeros((8, 128), F32)
    for g in range(0, END_ROWS, 8):
        rows = rows_at(g)
        depth[rows, :] = blank
        total[rows, :] = blank
        if g not in END_GROUPS:
            for c in range(END_LEVELS):
                for i in range(2):
                    coef[c, i, rows, :] = blank
                    q0[c, i, rows, :] = blank
                    q1[c, i, rows, :] = blank
    depth[8:12, :] = low[4 * KL, 4:8, :]
    depth[12:16, :] = levels[0:8, :].astype(F32)[0:4]
    depth[24:32, :] = levels[SX - 8 : SX, :].astype(F32)
    depth[32:40, :] = high[4 * KL]
    set_faces(END_GROUPS, depth, face)

    def some_levels(i, carry):
        for c in range(END_LEVELS):
            k = END_LEVELS * i + c
            for t in range(2):
                q0[c, t, 8:12, :] = low[KL * t + k, 4:8, :]
                q0[c, t, 12:16, :] = tracers[t, k, 0:4, :]
                q0[c, t, 24:32, :] = tracers[t, k, SX - 8 : SX, :]
                q0[c, t, 32:40, :] = high[KL * t + k]
            for t, field in enumerate((east, north)):
                flow[c, t, 8:12, :] = low[KL * (2 + t) + k, 4:8, :]
                flow[c, t, 12:16, :] = field[k, 0:16, :].astype(F32)[0:4]
                flow[c, t, 24:32, :] = field[k, SX - 16 : SX, :].astype(F32)[8:16]
                flow[c, t, 32:40, :] = high[KL * (2 + t) + k]
        for c, g, temperature, salinity in two_steps(
            END_LEVELS,
            END_GROUPS,
            lambda c: (END_LEVELS * i + c).astype(F32),
            lambda c, g: depth[rows_at(g), :],
            lambda c, g: (face[0, rows_at(g), :], face[1, rows_at(g), :]),
            flow,
            coef,
            q0,
            q1,
        ):
            if g < 32:
                rows = rows_at(0 if g == 8 else 8)
                new[0, END_LEVELS * i + c, rows, :] = temperature
                new[1, END_LEVELS * i + c, rows, :] = salinity
            total[rows_at(g), :] += temperature - 0.8 * salinity
        return carry

    lax.fori_loop(0, KL // END_LEVELS, some_levels, 0)


def end_levels(tracers, east, north, levels, low, high):
    return pl.pallas_call(
        ends_kernel,
        out_shape=[pltpu.VMEM((2, KL, 16, SY), F32), pltpu.VMEM((END_ROWS, 128), F32)],
        scratch_shapes=level_scratch(END_ROWS, END_LEVELS),
        compiler_params=params(),
        cost_estimate=pl.CostEstimate(flops=5_000_000, bytes_accessed=6_000_000, transcendentals=0),
        name="end_levels",
    )(tracers, east, north, levels, low, high)


def operator_kernel(
    levels, low, high, own_rows, own_edges, first_rows, second_rows, first_edges, second_edges,
    blocked, ends, wall_total, ends_total,
    new, fields, sums,
    depth, q0, q1, strip_depth, strip_face, strip_flow, strip_total, first_q, coef, wall, total, field, grid, staged, sems,
    *, count,
):
    lane = lanes()
    member = lane % 8
    blank = jnp.zeros((8, 128), F32)
    strip_level = (lane // 8).astype(F32)
    first = lax.axis_index("gy") == 0
    last = lax.axis_index("gy") == count - 1

    def own(which, a, g):
        r = g - LOW
        if r < EDGE:
            return own_edges[which, a, rows_at(0), :]
        if r >= WIDE - EDGE:
            return own_edges[which, a, rows_at(8), :]
        return own_rows[which, a, rows_at(r - EDGE), :]

    even = is_even("gy")

    def sent(g):
        r = g - LOW
        if r < EDGE:
            refs, rows = (first_edges, second_edges), rows_at(0)
        elif r >= WIDE - EDGE:
            refs, rows = (first_edges, second_edges), rows_at(8)
        else:
            refs, rows = (first_rows, second_rows), rows_at(r - EDGE)
        pairs = [(refs[0][a, rows, :], refs[1][a, rows, :]) for a in range(SENT)]
        return [jnp.where(even, b, a) for a, b in pairs], [jnp.where(even, a, b) for a, b in pairs]

    halo_depth(levels, low, high, depth)
    parts = {}
    for g in GROUPS:
        from_low, from_high = sent(g)
        parts[g] = list(split_one(*from_low)), list(split_two(*from_high))
    for g in GROUPS:
        rows = rows_at(g)
        from_low, from_high = parts[g]
        from_low[4] = jnp.where(first, 0.0, from_low[4])
        from_high[4] = jnp.where(last, 0.0, from_high[4])
        for a in range(5):
            low_strip = jnp.where(member < 4, from_low[a], own(0, a, g))
            high_strip = jnp.where(member >= 3, from_high[a], own(1, a, g))
            for side, value in enumerate((low_strip, high_strip)):
                if a < 2:
                    q0[side, a, rows, :] = value
                elif a < 4:
                    strip_flow[side, a - 2, rows, :] = value
                else:
                    strip_depth[side, rows, :] = value
    for outside in OUTSIDE:
        for side in range(2):
            strip_depth[side, rows_at(outside), :] = blank

    ahead = {
        (side, g): ahead_one(strip_depth[side, rows_at(g), :]) for side in range(2) for g in GROUPS
    }
    for (side, g), value in ahead.items():
        strip_face[side, rows_at(g), :] = jnp.minimum(strip_depth[side, rows_at(g), :], value)

    for side in range(2):
        for i in range(2):
            coef[side, i, rows_at(LOW - 8), :] = blank

    def first_row(side, g, b_south, *behind):
        if side == 0:
            return b_south, *behind
        face = jnp.minimum(own(0, 4, g), own(1, 4, g))
        a_first, b_first = face_weights(face, own(0, 3, g), strip_level)
        return (
            jnp.where(member == 0, b_first, b_south),
            *(jnp.where(member == 0, a_first * own(0, t, g), behind[t]) for t in range(2)),
        )

    for side, g, temperature, salinity in two_steps(
        2,
        GROUPS,
        lambda side: strip_level,
        lambda side, g: strip_depth[side, rows_at(g), :],
        lambda side, g: (
            jnp.minimum(strip_depth[side, rows_at(g), :], strip_depth[side, rows_at(g + 1), :]),
            strip_face[side, rows_at(g), :],
        ),
        strip_flow,
        coef,
        q0,
        q1,
        first_row,
    ):
        rows = rows_at(g)
        q0[side, 0, rows, :] = temperature
        q0[side, 1, rows, :] = salinity
        strip_total[side, rows, :] = temperature - 0.8 * salinity
    for turn in (8, 16, 32, 64):
        values = {}
        for side in range(2):
            for g in GROUPS:
                value = strip_total[side, rows_at(g), :]
                values[side, g] = value + pltpu.roll(value, turn, 1)
        for (side, g), value in values.items():
            strip_total[side, rows_at(g), :] = value

    for tracer in range(2):
        for g in range(PAD, PAD + SX, 8):
            rows = rows_at(g)
            high_value = pltpu.roll(q0[1, tracer, rows, :], 1, 1)
            first_q[tracer, rows, :] = jnp.where(member >= 4, q0[0, tracer, rows, :], high_value)
    from_strip = (lane < 2) | (lane >= 126)
    row = lax.broadcasted_iota(jnp.int32, (8, 128), 0)

    def place(k, carry):
        turn = 124 - 8 * k
        for tracer in range(2):
            values = {g: pltpu.roll(first_q[tracer, rows_at(g + PAD), :], turn, 1) for g in range(0, SX, 8)}
            for g, value in values.items():
                rows = rows_at(g)
                here = blocked[tracer, k, rows, :]
                if g == 0:
                    here = jnp.where(row < 2, ends[tracer, k, rows_at(4), :], here)
                elif g == SX - 8:
                    here = jnp.where(row >= 6, ends[tracer, k, rows_at(8), :], here)
                staged[tracer, k, rows, :] = jnp.where(from_strip, value, here)
        for tracer in range(2):
            pltpu.make_async_copy(staged.at[tracer, k], new.at[tracer, k], sems.at[0]).start()
        return carry

    lax.fori_loop(0, KL, place, 0)

    def beside(low_value, high_value):
        return jnp.where(lane >= 64, pltpu.roll(low_value, 4, 1), pltpu.roll(high_value, 5, 1))

    def northward(main, side):
        a, b = ahead_one(main), ahead_one(side)
        return jnp.where(lane == 127, b, a), jnp.where(lane == 127, a, b)

    def southward(main, side):
        a, b = back_one(main), back_one(side)
        return jnp.where(lane == 0, b, a), jnp.where(lane == 0, a, b)

    for g in GROUPS:
        wall[rows_at(g), :] = wall_total[rows_at(g), :]
    wall[PAD - 2 : PAD + 2, :] = ends_total[10:14, :]
    wall[PAD + SX - 2 : PAD + SX + 3, :] = ends_total[30:35, :]
    for g in GROUPS + OUTSIDE:
        rows = rows_at(g)
        grid[0, 0, rows, :] = depth[rows, :]
        grid[0, 1, rows, :] = beside(strip_depth[0, rows, :], strip_depth[1, rows, :])
    for g in GROUPS:
        rows = rows_at(g)
        both = grid[0, 0, rows, :], grid[0, 1, rows, :]
        further = northward(*both)
        for part in range(2):
            grid[1, part, rows, :] = jnp.minimum(both[part], grid[0, part, rows_at(g + 1), :])
            grid[2, part, rows, :] = jnp.minimum(both[part], further[part])
        low_total = pltpu.roll(strip_total[0, rows, :], 4, 1)
        high_total = pltpu.roll(strip_total[1, rows, :], 5, 1)
        edge_total = jnp.where(lane < 64, low_total, high_total)
        total[0, rows, :] = jnp.where(from_strip, edge_total, wall[rows, :])
        total[1, rows, :] = jnp.where(lane >= 64, low_total, high_total)
    for part in range(2):
        grid[1, part, rows_at(LOW - 8), :] = blank
        for outside in OUTSIDE:
            for i in range(3):
                field[i, part, rows_at(outside), :] = blank
    scale = 1.0 / KL
    for g in GROUPS:
        rows = rows_at(g)
        souths = southward(grid[2, 0, rows, :], grid[2, 1, rows, :])
        for part in range(2):
            here = grid[0, part, rows, :]
            own_part = ALPHA * scale * here + jnp.where(here == 0.0, 1.0, 0.0)
            faces = grid[1, part, rows, :] + grid[1, part, rows_at(g - 1), :] + grid[2, part, rows, :] + souths[part]
            diagonal = own_part + scale * faces
            inverse = 1.0 / diagonal
            grid[3, part, rows, :] = inverse
            grid[4, part, rows, :] = own_part
            grid[5, part, rows, :] = diagonal
            field[0, part, rows, :] = 0.25 * total[part, rows, :] * inverse

    moments = [blank] * 6
    for i in range(3):
        for g in GROUPS:
            rows = rows_at(g)
            both = field[i, 0, rows, :], field[i, 1, rows, :]
            norths = northward(*both)
            souths = southward(*both)
            south_faces = southward(grid[2, 0, rows, :], grid[2, 1, rows, :])
            for part in range(2):
                if i == 2 and part == 1:
                    continue
                here = both[part]
                east_gap = here - field[i, part, rows_at(g + 1), :]
                north_gap = here - norths[part]
                east_face = scale * grid[1, part, rows, :]
                north_face = scale * grid[2, part, rows, :]
                own_part = grid[4, part, rows, :]
                if part == 0 and PAD <= g < PAD + SX:
                    moments[2 * i] += grid[5, 0, rows, :] * here * here
                    moments[2 * i + 1] += (
                        own_part * here * here + east_face * east_gap * east_gap + north_face * north_gap * north_gap
                    )
                if i < 2:
                    image = (
                        own_part * here
                        + east_face * east_gap
                        + scale * grid[1, part, rows_at(g - 1), :] * (here - field[i, part, rows_at(g - 1), :])
                        + north_face * north_gap
                        + scale * south_faces[part] * (here - souths[part])
                    )
                    field[i + 1, part, rows, :] = image * grid[3, part, rows, :]
        pltpu.make_async_copy(field.at[i, 0, PAD : PAD + SX, :], fields.at[i], sems.at[1]).start()
    sums_row = jnp.zeros((8, 128), F32)
    for i in range(6):
        value = jnp.sum(jnp.sum(moments[i], axis=0, keepdims=True), axis=1, keepdims=True)
        sums_row = jnp.where(lane == i, value, sums_row)
    for g in range(0, 128, 8):
        sums[rows_at(g), :] = sums_row
    pltpu.make_async_copy(field.at[:, 0, PAD : PAD + SX, :], fields, sems.at[1]).wait()
    pltpu.make_async_copy(staged, new, sems.at[0]).wait()


def operator(*arrays, count):
    tall = (ROWS, 128)
    scratch = (
        (),
        (2, 2),
        (2, 2),
        (2,),
        (2,),
        (2, 2),
        (2,),
        (2,),
        (2, 5),
        (),
        (2,),
        (3, 2),
        (6, 2),
    )
    return pl.pallas_call(
        functools.partial(operator_kernel, count=count),
        out_shape=[
            jax.ShapeDtypeStruct((2, KL, SX, SY), F32),
            pltpu.HBM((3, SX, SY), F32),
            jax.ShapeDtypeStruct((128, 128), F32),
        ],
        out_specs=[
            pl.BlockSpec(memory_space=pltpu.HBM),
            pl.BlockSpec(memory_space=pltpu.HBM),
            pl.BlockSpec(memory_space=pltpu.VMEM),
        ],
        scratch_shapes=[pltpu.VMEM(s + tall, F32) for s in scratch]
        + [pltpu.VMEM((2, KL, SX, SY), F32), pltpu.SemaphoreType.DMA((2,))],
        compiler_params=params(),
        name="operator",
    )(*arrays)


def finish_kernel(sums_in, fields_in, out, sums, fields, sems):
    first_copy = pltpu.make_async_copy(sums_in, sums, sems.at[0])
    copy = pltpu.make_async_copy(fields_in, fields, sems.at[1])
    first_copy.start()
    copy.start()
    first_copy.wait()
    value = sums[0:8, :]
    for g in range(8, 128, 8):
        value = value + sums[rows_at(g), :]
    value = jnp.sum(value, axis=0, keepdims=True)
    lane = lanes((1, 128))
    m0, m1, m2, m3, m4, m5 = (
        jnp.sum(jnp.where(lane == i, value, 0.0), axis=1, keepdims=True) for i in range(6)
    )
    floor = 4e-7
    l10 = m2 / m1
    l20 = m3 / m1
    d1 = m3 - l10 * m2
    t = m4 - l20 * m2
    has1 = d1 > floor * m3
    l21 = jnp.where(has1, t / d1, 0.0)
    d2 = m5 - l20 * m3 - l21 * t
    has2 = has1 & (d2 > floor * m5)
    y1 = m1 - l10 * m0
    y2 = m2 - l20 * m0 - l21 * y1
    c2 = jnp.where(has2, y2 / d2, 0.0)
    c1 = jnp.where(has1, y1 / d1, 0.0) - l21 * c2
    c0 = m0 / m1 - l10 * c1 - l20 * c2
    copy.wait()
    for g in range(0, SX, 8):
        rows = rows_at(g)
        out[rows, :] = c0 * fields[0, rows, :] + c1 * fields[1, rows, :] + c2 * fields[2, rows, :]


def finish(sums, fields):
    return pl.pallas_call(
        finish_kernel,
        in_specs=[pl.BlockSpec(memory_space=pl.ANY)] * 2,
        out_shape=jax.ShapeDtypeStruct((SX, SY), F32),
        scratch_shapes=[
            pltpu.VMEM((128, 128), F32),
            pltpu.VMEM((3, SX, SY), F32),
            pltpu.SemaphoreType.DMA((2,)),
        ],
        name="finish",
    )(sums, pltpu.with_memory_space_constraint(fields, pltpu.HBM))


def first_pairs(array, axis):
    return lax.ppermute(array, axis, [(i, i ^ 1) for i in range(lax.axis_size(axis))])


def second_pairs(array, axis, around):
    count = lax.axis_size(axis)
    pairs = [] if around else [(0, 0), (count - 1, count - 1)]
    for i in range(1, count if around else count - 1, 2):
        pairs += [(i, (i + 1) % count), ((i + 1) % count, i)]
    return lax.ppermute(array, axis, pairs)


def on_device(tracers, east, north, levels):
    to_first, to_second = edges(tracers, east, north, levels)
    first = first_pairs(to_first, "gx")
    second = second_pairs(to_second, "gx", True)
    own_rows, one, two, blocked, total = block(tracers, east, north, levels, to_first)
    one, two, first, second = lax.optimization_barrier((one, two, first, second))
    first_rows = first_pairs(one, "gy")
    second_rows = second_pairs(two, "gy", False)
    own_edges, one, two, low, high = pack_edges(first, second, total)
    first_edges = first_pairs(one, "gy")
    second_edges = second_pairs(two, "gy", False)
    ends, ends_total = end_levels(tracers, east, north, levels, low, high)
    new, fields, sums = operator(
        levels, low, high, own_rows, own_edges, first_rows, second_rows, first_edges, second_edges,
        blocked, ends, total, ends_total, count=lax.axis_size("gy"),
    )
    sums = lax.all_to_all(sums, ("gx", "gy"), split_axis=0, concat_axis=0, tiled=True)
    return new, finish(sums, fields)


def solution(mesh):
    placed = (P(None, None, "gx", "gy"), P(None, "gx", "gy"), P(None, "gx", "gy"), P("gx", "gy"))
    return jax.shard_map(
        on_device,
        mesh=mesh,
        in_specs=placed,
        out_specs=(P(None, None, "gx", "gy"), P("gx", "gy")),
        check_vma=False,
    )
```

```python
import functools

import jax
import jax.numpy as jnp
from jax import lax
from jax.experimental import pallas as pl
from jax.experimental.pallas import tpu as pltpu
from jax.sharding import PartitionSpec as P

KAPPA = 0.08
ALPHA = 0.05
F32 = jnp.float32

SX = 128
SY = 128
KL = 16
EDGE = 8
PAD = 16
ROWS = SX + 2 * PAD
WIDE = SX + 2 * EDGE
LOW = PAD - EDGE
ARRAYS = 2 * KL + 2 * KL + 1
VMEM = 40 * 1024 * 1024
GROUPS = tuple(range(LOW, LOW + WIDE, 8))
OUTSIDE = (LOW - 8, LOW + WIDE)
INNER = GROUPS[1:-1]
END_GROUPS = (8, 24, 32)
END_ROWS = 48
SENT = 3


def params():
    return pltpu.CompilerParams(vmem_limit_bytes=VMEM)


def is_even(axis):
    return lax.rem(lax.axis_index(axis), 2) == 0


def rows_at(row):
    return slice(row, row + 8)


def lanes(shape=(8, 128)):
    return lax.broadcasted_iota(jnp.int32, shape, len(shape) - 1)


def ahead_one(value):
    return pltpu.roll(value, 127, 1)


def back_one(value):
    return pltpu.roll(value, 1, 1)


def offsets(counts):
    starts, at = [], 8
    for a in range(4):
        starts.append(at)
        at += KL * counts[a]
    return starts, at


NEXT = (4, 4, 4, 4)
BEFORE = (5, 5, 4, 4)
NEXT_AT, NEXT_ROWS = offsets(NEXT)
BEFORE_AT, BEFORE_ROWS = offsets(BEFORE)
BEFORE_ROWS += 8
assert NEXT_ROWS <= BEFORE_ROWS


def edges_kernel(t, e, n, d, first_pair, second_pair, tiles, flows, depths, sems):
    copies = []
    for side, at in enumerate((0, SX - 8)):
        at16 = 0 if side == 0 else SX - 16
        copies += [
            (t.at[0, :, at : at + 8, :], tiles.at[side, 0]),
            (t.at[1, :, at : at + 8, :], tiles.at[side, 1]),
            (e.at[:, at16 : at16 + 16, :], flows.at[side, 0]),
            (n.at[:, at16 : at16 + 16, :], flows.at[side, 1]),
            (d.at[at : at + 8, :], depths.at[side]),
        ]
    copies = [pltpu.make_async_copy(src, dst, sems.at[i]) for i, (src, dst) in enumerate(copies)]
    for copy in copies:
        copy.start()
    for copy in copies:
        copy.wait()

    def write(before, after):
        for side, (out, starts, counts) in enumerate(((before, BEFORE_AT, BEFORE), (after, NEXT_AT, NEXT))):
            out[0:8, :] = depths[side].astype(F32)
            for a in range(4):
                for k in range(KL):
                    value = tiles[side, a, k] if a < 2 else flows[side, a - 2, k].astype(F32)[8 * side : 8 * side + 8]
                    from_row = 0 if side == 0 else 8 - counts[a]
                    at = starts[a] + counts[a] * k
                    out[at : at + counts[a], :] = value[from_row : from_row + counts[a]]
        before[BEFORE_ROWS - 8 : BEFORE_ROWS, :] = jnp.zeros((8, 128), F32)
        after[NEXT_ROWS:BEFORE_ROWS, :] = jnp.zeros((BEFORE_ROWS - NEXT_ROWS, 128), F32)

    @pl.when(is_even("gx"))
    def _():
        write(second_pair, first_pair)

    @pl.when(~is_even("gx"))
    def _():
        write(first_pair, second_pair)


def edges(tracers, east, north, levels):
    return pl.pallas_call(
        edges_kernel,
        in_specs=[pl.BlockSpec(memory_space=pltpu.HBM)] * 4,
        out_shape=[pltpu.VMEM((BEFORE_ROWS, SY), F32)] * 2,
        scratch_shapes=[
            pltpu.VMEM((2, 2, KL, 8, SY), F32),
            pltpu.VMEM((2, 2, KL, 16, SY), jnp.bfloat16),
            pltpu.VMEM((2, 8, SY), jnp.int32),
            pltpu.SemaphoreType.DMA((10,)),
        ],
        compiler_params=params(),
        name="edges",
    )(*(pltpu.with_memory_space_constraint(x, pltpu.HBM) for x in (tracers, east, north, levels)))


def low_tile(ref, a, k):
    if a == 4:
        return ref[0:8, :]
    at = NEXT_AT[a] + NEXT[a] * (k + 1) - 8
    return ref[at : at + 8, :]


def high_tile(ref, a, k):
    if a == 4:
        return ref[0:8, :]
    at = BEFORE_AT[a] + BEFORE[a] * k
    return ref[at : at + 8, :]


def pack(source, rows, last):
    group = lanes((rows, 128)) // 8
    one = jnp.zeros((rows, 128), F32)
    beyond = jnp.zeros((rows, 128), F32)
    for k in range(KL):
        value = source(k)
        one = jnp.where(group == k, pltpu.roll(value, (8 * k - 124) % 128, 1), one)
        if last:
            beyond = jnp.where(group == k, pltpu.roll(value, (8 * k + 3) % 128, 1), beyond)
    two = pltpu.roll(one, 127, 1)
    if last:
        two = jnp.where(lanes((rows, 128)) % 8 == 7, beyond, two)
    return one, two


def pack_depth(sources):
    lane = lanes(sources[0].shape)
    values = [pltpu.roll(x, turn, 1) for turn in (4, 3) for x in sources]
    values = [jnp.where(lane < 8, x, 0.0) for x in values]
    for turn in (8, 16, 32, 64):
        values = [x + pltpu.roll(x, turn, 1) for x in values]
    return list(zip(values[: len(sources)], values[len(sources) :], strict=True))


def merge_one(t0, t1, e, n, d):
    member = lanes(t0.shape) % 8
    return (
        jnp.where(member < 4, t0, pltpu.roll(n, 4, 1)),
        jnp.where(member < 4, t1, pltpu.roll(e, 4, 1)),
        d,
    )


def split_one(a, b, c):
    return a, b, pltpu.roll(b, 124, 1), pltpu.roll(a, 124, 1), c


def merge_two(t0, t1, e, n, d):
    member = lanes(t0.shape) % 8
    return (
        jnp.where(member < 3, pltpu.roll(d, 125, 1), t0),
        jnp.where(member < 2, pltpu.roll(d, 122, 1), t1),
        jnp.where((member >= 3) & (member < 7), n, pltpu.roll(e, 4, 1)),
    )


def split_two(a, b, c):
    member = lanes(a.shape) % 8
    depth = jnp.where(member < 6, pltpu.roll(a, 3, 1), pltpu.roll(b, 6, 1))
    return a, b, pltpu.roll(c, 124, 1), c, depth


def pack_all(sources, depths, rows, own, own_rows, first_pair, second_pair, sent_rows):
    packed = [pack(source, rows, a < 2) for a, source in enumerate(sources)] + [depths]
    for which in range(2):
        for a in range(5):
            own[which, a, own_rows, :] = packed[a][which]
    even = is_even("gy")
    ones = merge_one(*(p[0] for p in packed))
    twos = merge_two(*(p[1] for p in packed))
    for a in range(SENT):
        first_pair[a, sent_rows, :] = jnp.where(even, ones[a], twos[a])
        second_pair[a, sent_rows, :] = jnp.where(even, twos[a], ones[a])


def pack_block(t, e, n, d, own, one, two):
    chunk = 32
    groups = range(0, SX, 8)
    for g, pair in zip(groups, pack_depth([d[rows_at(g), :].astype(F32) for g in groups]), strict=True):
        for which in range(2):
            own[which, 4, rows_at(g), :] = pair[which]

    def body(i, carry):
        rows = pl.ds(pl.multiple_of(i * chunk, chunk), chunk)
        sources = (
            lambda k: t[0, k, rows, :],
            lambda k: t[1, k, rows, :],
            lambda k: e[k, rows, :].astype(F32),
            lambda k: n[k, rows, :].astype(F32),
        )
        depths = own[0, 4, rows, :], own[1, 4, rows, :]
        pack_all(sources, depths, chunk, own, rows, one, two, rows)
        return carry

    lax.fori_loop(0, SX // chunk, body, 0)


def pack_edges_kernel(first_pair, second_pair, first_rows, second_rows, own, one, two, low, high, low_in, high_in):
    for g in range(0, SX, 8):
        for a in range(SENT):
            one[a, rows_at(g + EDGE), :] = first_rows[a, rows_at(g), :]
            two[a, rows_at(g + EDGE), :] = second_rows[a, rows_at(g), :]
    even = is_even("gx")
    for at in range(0, BEFORE_ROWS, 8):
        rows = rows_at(at)
        value, other = first_pair[rows, :], second_pair[rows, :]
        low_in[rows, :] = jnp.where(even, other, value)
        high_in[rows, :] = jnp.where(even, value, other)
    for a in range(5):
        for k in range(KL if a < 4 else 1):
            low[KL * a + k] = low_tile(low_in, a, k)
            high[KL * a + k] = high_tile(high_in, a, k)
    depths = pack_depth([low_tile(low_in, 4, 0), high_tile(high_in, 4, 0)])
    for side, (ref, tile) in enumerate(((low_in, low_tile), (high_in, high_tile))):
        sources = [functools.partial(tile, ref, a) for a in range(4)]
        at = 0 if side == 0 else WIDE - EDGE
        pack_all(sources, depths[side], 8, own, rows_at(8 * side), one, two, rows_at(at))


def pack_edges(first, second, first_rows, second_rows):
    sent = jax.ShapeDtypeStruct((SENT, WIDE, 128), F32)
    halo = jax.ShapeDtypeStruct((ARRAYS, EDGE, SY), F32)
    return pl.pallas_call(
        pack_edges_kernel,
        out_shape=[jax.ShapeDtypeStruct((2, 5, 2 * EDGE, 128), F32), sent, sent, halo, halo],
        scratch_shapes=[pltpu.VMEM((BEFORE_ROWS, SY), F32)] * 2,
        compiler_params=params(),
        name="pack_edges",
    )(first, second, first_rows, second_rows)


def face_weights(face, flow_value, threshold):
    is_open = face > threshold
    ahead = jnp.where(is_open, KAPPA + jnp.maximum(flow_value, 0.0), 0.0)
    back = jnp.where(is_open, KAPPA - jnp.minimum(flow_value, 0.0), 0.0)
    return ahead, back


def two_steps(copies, groups, threshold, depth_at, faces, flow, coef, q0, q1, first_row=None):
    parts = [(c, g) for c in range(copies) for g in groups]
    every = [(c, t, g) for c, g in parts for t in range(2)]
    for c, g in parts:
        rows = rows_at(g)
        east, north = faces(c, g)
        coef[c, 0, rows, :], coef[c, 1, rows, :] = face_weights(east, flow[c, 0, rows, :], threshold(c))
        coef[c, 3, rows, :], coef[c, 2, rows, :] = face_weights(north, flow[c, 1, rows, :], threshold(c))
    b_south = {(c, g): back_one(coef[c, 2, rows_at(g), :]) for c, g in parts}

    def shifted(source):
        ahead = {(c, t, g): ahead_one(source[c, t, rows_at(g), :]) for c, t, g in every}
        behind = {
            (c, t, g): back_one(coef[c, 3, rows_at(g), :] * source[c, t, rows_at(g), :]) for c, t, g in every
        }
        return ahead, behind

    def combine(source, c, t, g, ahead, behind):
        rows = rows_at(g)
        return (
            coef[c, 4, rows, :] * source[c, t, rows, :]
            + coef[c, 1, rows, :] * source[c, t, rows_at(g + 1), :]
            + coef[c, 0, rows_at(g - 1), :] * source[c, t, rows_at(g - 1), :]
            + coef[c, 2, rows, :] * ahead
            + behind
        )

    ahead, behind = shifted(q0)
    for c, g in parts:
        rows = rows_at(g)
        b_here = b_south[c, g]
        if first_row is not None:
            b_here, behind[c, 0, g], behind[c, 1, g] = first_row(c, g, b_here, behind[c, 0, g], behind[c, 1, g])
        leaving = coef[c, 0, rows, :] + coef[c, 3, rows, :] + coef[c, 1, rows_at(g - 1), :] + b_here
        coef[c, 4, rows, :] = jnp.where(depth_at(c, g) > threshold(c), 1.0 - leaving, 0.0)
        for t in range(2):
            q1[c, t, rows, :] = combine(q0, c, t, g, ahead[c, t, g], behind[c, t, g])
    ahead, behind = shifted(q1)
    for c, g in parts:
        yield c, g, *(combine(q1, c, t, g, ahead[c, t, g], behind[c, t, g]) for t in range(2))


def halo_depth(levels, low, high, depth):
    for g in GROUPS:
        r = g - LOW
        if r < EDGE:
            value = low[4 * KL]
        elif r >= WIDE - EDGE:
            value = high[4 * KL]
        else:
            value = levels[rows_at(r - EDGE), :].astype(F32)
        depth[rows_at(g), :] = value
    for outside in OUTSIDE:
        depth[rows_at(outside), :] = jnp.zeros((8, 128), F32)


LEVELS = 2
END_LEVELS = 4
PLACED = 8


def set_faces(groups, depth, face):
    lane = lanes()
    ahead = {g: ahead_one(depth[rows_at(g), :]) for g in groups}
    for g in groups:
        rows = rows_at(g)
        here = depth[rows, :]
        face[0, rows, :] = jnp.minimum(here, depth[rows_at(g + 1), :])
        face[1, rows, :] = jnp.where(lane == 127, 0.0, jnp.minimum(here, ahead[g]))


def block_kernel(
    tracers, east, north, levels, after, own, first_pair, second_pair, new, total, depth, face, q0, q1, flow, coef
):
    del after
    pack_block(tracers, east, north, levels, own, first_pair, second_pair)
    blank = jnp.zeros((8, 128), F32)
    for g in INNER:
        depth[rows_at(g), :] = levels[rows_at(g - PAD), :].astype(F32)
        total[rows_at(g), :] = blank
    for g in (GROUPS[0], GROUPS[-1]):
        depth[rows_at(g), :] = blank
        total[rows_at(g), :] = blank
        for c in range(LEVELS):
            for i in range(2):
                coef[c, i, rows_at(g), :] = blank
                q0[c, i, rows_at(g), :] = blank
                q1[c, i, rows_at(g), :] = blank
    set_faces(INNER, depth, face)

    def some_levels(i, carry):
        for c in range(LEVELS):
            k = LEVELS * i + c
            for t in range(2):
                q0[c, t, PAD : PAD + SX, :] = tracers[t, k]
            flow[c, 0, PAD : PAD + SX, :] = east[k].astype(F32)
            flow[c, 1, PAD : PAD + SX, :] = north[k].astype(F32)
        for c, g, temperature, salinity in two_steps(
            LEVELS,
            INNER,
            lambda c: (LEVELS * i + c).astype(F32),
            lambda c, g: depth[rows_at(g), :],
            lambda c, g: (face[0, rows_at(g), :], face[1, rows_at(g), :]),
            flow,
            coef,
            q0,
            q1,
        ):
            new[0, LEVELS * i + c, rows_at(g - PAD), :] = temperature
            new[1, LEVELS * i + c, rows_at(g - PAD), :] = salinity
            total[rows_at(g), :] += temperature - 0.8 * salinity
        return carry

    lax.fori_loop(0, KL // LEVELS, some_levels, 0)


def level_scratch(rows, copies):
    shapes = ((), (2,), (copies, 2), (copies, 2), (copies, 2), (copies, 5))
    return [pltpu.VMEM(shape + (rows, 128), F32) for shape in shapes]


def block(tracers, east, north, levels, after):
    sent = pltpu.VMEM((SENT, SX, 128), F32)
    return pl.pallas_call(
        block_kernel,
        in_specs=[pl.BlockSpec(memory_space=pltpu.VMEM)] * 4 + [pl.BlockSpec(memory_space=pl.ANY)],
        out_shape=[
            pltpu.VMEM((2, 5, SX, 128), F32),
            sent,
            sent,
            pltpu.VMEM(tracers.shape, F32),
            pltpu.VMEM((ROWS, 128), F32),
        ],
        scratch_shapes=level_scratch(ROWS, LEVELS),
        compiler_params=params(),
        cost_estimate=pl.CostEstimate(flops=20_000_000, bytes_accessed=24_000_000, transcendentals=0),
        name="block",
    )(tracers, east, north, levels, after)


def ends_kernel(tracers, east, north, levels, low, high, new, total, depth, face, q0, q1, flow, coef):
    blank = jnp.zeros((8, 128), F32)
    for g in range(0, END_ROWS, 8):
        rows = rows_at(g)
        depth[rows, :] = blank
        total[rows, :] = blank
        if g not in END_GROUPS:
            for c in range(END_LEVELS):
                for i in range(2):
                    coef[c, i, rows, :] = blank
                    q0[c, i, rows, :] = blank
                    q1[c, i, rows, :] = blank
    depth[8:12, :] = low[4 * KL, 4:8, :]
    depth[12:16, :] = levels[0:8, :].astype(F32)[0:4]
    depth[24:32, :] = levels[SX - 8 : SX, :].astype(F32)
    depth[32:40, :] = high[4 * KL]
    set_faces(END_GROUPS, depth, face)

    def some_levels(i, carry):
        for c in range(END_LEVELS):
            k = END_LEVELS * i + c
            for t in range(2):
                q0[c, t, 8:12, :] = low[KL * t + k, 4:8, :]
                q0[c, t, 12:16, :] = tracers[t, k, 0:4, :]
                q0[c, t, 24:32, :] = tracers[t, k, SX - 8 : SX, :]
                q0[c, t, 32:40, :] = high[KL * t + k]
            for t, field in enumerate((east, north)):
                flow[c, t, 8:12, :] = low[KL * (2 + t) + k, 4:8, :]
                flow[c, t, 12:16, :] = field[k, 0:16, :].astype(F32)[0:4]
                flow[c, t, 24:32, :] = field[k, SX - 16 : SX, :].astype(F32)[8:16]
                flow[c, t, 32:40, :] = high[KL * (2 + t) + k]
        for c, g, temperature, salinity in two_steps(
            END_LEVELS,
            END_GROUPS,
            lambda c: (END_LEVELS * i + c).astype(F32),
            lambda c, g: depth[rows_at(g), :],
            lambda c, g: (face[0, rows_at(g), :], face[1, rows_at(g), :]),
            flow,
            coef,
            q0,
            q1,
        ):
            if g < 32:
                rows = rows_at(0 if g == 8 else 8)
                new[0, END_LEVELS * i + c, rows, :] = temperature
                new[1, END_LEVELS * i + c, rows, :] = salinity
            total[rows_at(g), :] += temperature - 0.8 * salinity
        return carry

    lax.fori_loop(0, KL // END_LEVELS, some_levels, 0)


def end_levels(tracers, east, north, levels, low, high):
    return pl.pallas_call(
        ends_kernel,
        out_shape=[pltpu.VMEM((2, KL, 16, SY), F32), pltpu.VMEM((END_ROWS, 128), F32)],
        scratch_shapes=level_scratch(END_ROWS, END_LEVELS),
        compiler_params=params(),
        cost_estimate=pl.CostEstimate(flops=5_000_000, bytes_accessed=6_000_000, transcendentals=0),
        name="end_levels",
    )(tracers, east, north, levels, low, high)


def operator_kernel(
    levels, low, high, own_rows, own_edges, first_pair, second_pair, blocked, ends, wall_total, ends_total,
    new, fields, sums,
    depth, q0, q1, strip_depth, strip_face, strip_flow, strip_total, first_q, coef, wall, total, field, grid, staged, sems,
    *, count,
):
    lane = lanes()
    member = lane % 8
    blank = jnp.zeros((8, 128), F32)
    strip_level = (lane // 8).astype(F32)
    first = lax.axis_index("gy") == 0
    last = lax.axis_index("gy") == count - 1

    def own(which, a, g):
        r = g - LOW
        if r < EDGE:
            return own_edges[which, a, rows_at(0), :]
        if r >= WIDE - EDGE:
            return own_edges[which, a, rows_at(8), :]
        return own_rows[which, a, rows_at(r - EDGE), :]

    even = is_even("gy")

    def sent(g):
        rows = rows_at(g - LOW)
        pairs = [(first_pair[a, rows, :], second_pair[a, rows, :]) for a in range(SENT)]
        return [jnp.where(even, b, a) for a, b in pairs], [jnp.where(even, a, b) for a, b in pairs]

    halo_depth(levels, low, high, depth)
    parts = {}
    for g in GROUPS:
        from_low, from_high = sent(g)
        parts[g] = list(split_one(*from_low)), list(split_two(*from_high))
    for g in GROUPS:
        rows = rows_at(g)
        from_low, from_high = parts[g]
        from_low[4] = jnp.where(first, 0.0, from_low[4])
        from_high[4] = jnp.where(last, 0.0, from_high[4])
        for a in range(5):
            low_strip = jnp.where(member < 4, from_low[a], own(0, a, g))
            high_strip = jnp.where(member >= 3, from_high[a], own(1, a, g))
            for side, value in enumerate((low_strip, high_strip)):
                if a < 2:
                    q0[side, a, rows, :] = value
                elif a < 4:
                    strip_flow[side, a - 2, rows, :] = value
                else:
                    strip_depth[side, rows, :] = value
    for outside in OUTSIDE:
        for side in range(2):
            strip_depth[side, rows_at(outside), :] = blank

    ahead = {
        (side, g): ahead_one(strip_depth[side, rows_at(g), :]) for side in range(2) for g in GROUPS
    }
    for (side, g), value in ahead.items():
        strip_face[side, rows_at(g), :] = jnp.minimum(strip_depth[side, rows_at(g), :], value)

    for side in range(2):
        for i in range(2):
            coef[side, i, rows_at(LOW - 8), :] = blank

    def first_row(side, g, b_south, *behind):
        if side == 0:
            return b_south, *behind
        face = jnp.minimum(own(0, 4, g), own(1, 4, g))
        a_first, b_first = face_weights(face, own(0, 3, g), strip_level)
        return (
            jnp.where(member == 0, b_first, b_south),
            *(jnp.where(member == 0, a_first * own(0, t, g), behind[t]) for t in range(2)),
        )

    for side, g, temperature, salinity in two_steps(
        2,
        GROUPS,
        lambda side: strip_level,
        lambda side, g: strip_depth[side, rows_at(g), :],
        lambda side, g: (
            jnp.minimum(strip_depth[side, rows_at(g), :], strip_depth[side, rows_at(g + 1), :]),
            strip_face[side, rows_at(g), :],
        ),
        strip_flow,
        coef,
        q0,
        q1,
        first_row,
    ):
        rows = rows_at(g)
        q0[side, 0, rows, :] = temperature
        q0[side, 1, rows, :] = salinity
        strip_total[side, rows, :] = temperature - 0.8 * salinity
    for turn in (8, 16, 32, 64):
        values = {}
        for side in range(2):
            for g in GROUPS:
                value = strip_total[side, rows_at(g), :]
                values[side, g] = value + pltpu.roll(value, turn, 1)
        for (side, g), value in values.items():
            strip_total[side, rows_at(g), :] = value

    for tracer in range(2):
        high_values = {g: back_one(q0[1, tracer, rows_at(g), :]) for g in INNER}
        for g in INNER:
            rows = rows_at(g)
            first_q[tracer, rows, :] = jnp.where(member >= 4, q0[0, tracer, rows, :], high_values[g])
    from_strip = (lane < 2) | (lane >= 126)
    row = lax.broadcasted_iota(jnp.int32, (8, 128), 0)

    def place(i, carry):
        slots = [(t, PLACED * i + c, c, g) for c in range(PLACED) for t in range(2) for g in range(0, SX, 8)]
        turned = {
            (t, c, g): pltpu.roll(first_q[t, rows_at(g + PAD), :], 124 - 8 * k, 1) for t, k, c, g in slots
        }
        for t, k, c, g in slots:
            rows = rows_at(g)
            here = blocked[t, k, rows, :]
            if g == 0:
                here = jnp.where(row < 2, ends[t, k, rows_at(4), :], here)
            elif g == SX - 8:
                here = jnp.where(row >= 6, ends[t, k, rows_at(8), :], here)
            staged[t, k, rows, :] = jnp.where(from_strip, turned[t, c, g], here)
        at = pl.ds(PLACED * i, PLACED)
        for t in range(2):
            pltpu.make_async_copy(staged.at[t, at], new.at[t, at], sems.at[0]).start()
        return carry

    lax.fori_loop(0, KL // PLACED, place, 0)

    def beside(low_value, high_value):
        return jnp.where(lane >= 64, pltpu.roll(low_value, 4, 1), pltpu.roll(high_value, 5, 1))

    def northward(main, side):
        a, b = ahead_one(main), ahead_one(side)
        return jnp.where(lane == 127, b, a), jnp.where(lane == 127, a, b)

    def southward(main, side):
        a, b = back_one(main), back_one(side)
        return jnp.where(lane == 0, b, a), jnp.where(lane == 0, a, b)

    for g in GROUPS:
        wall[rows_at(g), :] = wall_total[rows_at(g), :]
    wall[PAD - 2 : PAD + 2, :] = ends_total[10:14, :]
    wall[PAD + SX - 2 : PAD + SX + 3, :] = ends_total[30:35, :]
    for g in GROUPS + OUTSIDE:
        rows = rows_at(g)
        grid[0, 0, rows, :] = depth[rows, :]
        grid[0, 1, rows, :] = beside(strip_depth[0, rows, :], strip_depth[1, rows, :])
    further_all = {g: northward(grid[0, 0, rows_at(g), :], grid[0, 1, rows_at(g), :]) for g in GROUPS}
    strip_sums = {
        g: (pltpu.roll(strip_total[0, rows_at(g), :], 4, 1), pltpu.roll(strip_total[1, rows_at(g), :], 5, 1))
        for g in GROUPS
    }
    for g in GROUPS:
        rows = rows_at(g)
        both = grid[0, 0, rows, :], grid[0, 1, rows, :]
        further = further_all[g]
        for part in range(2):
            grid[1, part, rows, :] = jnp.minimum(both[part], grid[0, part, rows_at(g + 1), :])
            grid[2, part, rows, :] = jnp.minimum(both[part], further[part])
        low_total, high_total = strip_sums[g]
        edge_total = jnp.where(lane < 64, low_total, high_total)
        total[0, rows, :] = jnp.where(from_strip, edge_total, wall[rows, :])
        total[1, rows, :] = jnp.where(lane >= 64, low_total, high_total)
    for part in range(2):
        grid[1, part, rows_at(LOW - 8), :] = blank
        for outside in OUTSIDE:
            for i in range(3):
                field[i, part, rows_at(outside), :] = blank
    scale = 1.0 / KL
    south_faces = {g: southward(grid[2, 0, rows_at(g), :], grid[2, 1, rows_at(g), :]) for g in GROUPS}
    for g in GROUPS:
        rows = rows_at(g)
        souths = south_faces[g]
        for part in range(2):
            grid[6, part, rows, :] = souths[part]
            here = grid[0, part, rows, :]
            own_part = ALPHA * scale * here + jnp.where(here == 0.0, 1.0, 0.0)
            faces = grid[1, part, rows, :] + grid[1, part, rows_at(g - 1), :] + grid[2, part, rows, :] + souths[part]
            diagonal = own_part + scale * faces
            inverse = 1.0 / diagonal
            grid[3, part, rows, :] = inverse
            grid[4, part, rows, :] = own_part
            grid[5, part, rows, :] = diagonal
            field[0, part, rows, :] = 0.25 * total[part, rows, :] * inverse

    moments = [blank] * 6
    for i in range(3):
        groups = GROUPS if i < 2 else INNER
        pairs = {g: (field[i, 0, rows_at(g), :], field[i, 1, rows_at(g), :]) for g in groups}
        all_norths = {g: northward(*pairs[g]) for g in groups}
        all_souths = {g: southward(*pairs[g]) for g in groups} if i < 2 else {}
        for g in groups:
            rows = rows_at(g)
            both = pairs[g]
            norths = all_norths[g]
            for part in range(2):
                if i == 2 and part == 1:
                    continue
                here = both[part]
                east_gap = here - field[i, part, rows_at(g + 1), :]
                north_gap = here - norths[part]
                east_face = scale * grid[1, part, rows, :]
                north_face = scale * grid[2, part, rows, :]
                own_part = grid[4, part, rows, :]
                if part == 0 and PAD <= g < PAD + SX:
                    moments[2 * i] += grid[5, 0, rows, :] * here * here
                    moments[2 * i + 1] += (
                        own_part * here * here + east_face * east_gap * east_gap + north_face * north_gap * north_gap
                    )
                if i < 2:
                    image = (
                        own_part * here
                        + east_face * east_gap
                        + scale * grid[1, part, rows_at(g - 1), :] * (here - field[i, part, rows_at(g - 1), :])
                        + north_face * north_gap
                        + scale * grid[6, part, rows, :] * (here - all_souths[g][part])
                    )
                    field[i + 1, part, rows, :] = image * grid[3, part, rows, :]
        pltpu.make_async_copy(field.at[i, 0, PAD : PAD + SX, :], fields.at[i], sems.at[1]).start()
    sums_row = jnp.zeros((8, 128), F32)
    for i in range(6):
        value = jnp.sum(jnp.sum(moments[i], axis=0, keepdims=True), axis=1, keepdims=True)
        sums_row = jnp.where(lane == i, value, sums_row)
    for g in range(0, 128, 8):
        sums[rows_at(g), :] = sums_row
    pltpu.make_async_copy(field.at[:, 0, PAD : PAD + SX, :], fields, sems.at[1]).wait()
    pltpu.make_async_copy(staged, new, sems.at[0]).wait()


def operator(*arrays, count):
    tall = (ROWS, 128)
    scratch = (
        (),
        (2, 2),
        (2, 2),
        (2,),
        (2,),
        (2, 2),
        (2,),
        (2,),
        (2, 5),
        (),
        (2,),
        (3, 2),
        (7, 2),
    )
    return pl.pallas_call(
        functools.partial(operator_kernel, count=count),
        out_shape=[
            jax.ShapeDtypeStruct((2, KL, SX, SY), F32),
            pltpu.HBM((3, SX, SY), F32),
            jax.ShapeDtypeStruct((128, 128), F32),
        ],
        out_specs=[
            pl.BlockSpec(memory_space=pltpu.HBM),
            pl.BlockSpec(memory_space=pltpu.HBM),
            pl.BlockSpec(memory_space=pltpu.VMEM),
        ],
        scratch_shapes=[pltpu.VMEM(s + tall, F32) for s in scratch]
        + [pltpu.VMEM((2, KL, SX, SY), F32), pltpu.SemaphoreType.DMA((2,))],
        compiler_params=params(),
        name="operator",
    )(*arrays)


def finish_kernel(sums_in, fields_in, out, sums, fields, sems):
    first_copy = pltpu.make_async_copy(sums_in, sums, sems.at[0])
    copy = pltpu.make_async_copy(fields_in, fields, sems.at[1])
    first_copy.start()
    copy.start()
    first_copy.wait()
    value = sums[0:8, :]
    for g in range(8, 128, 8):
        value = value + sums[rows_at(g), :]
    value = jnp.sum(value, axis=0, keepdims=True)
    lane = lanes((1, 128))
    m0, m1, m2, m3, m4, m5 = (
        jnp.sum(jnp.where(lane == i, value, 0.0), axis=1, keepdims=True) for i in range(6)
    )
    floor = 4e-7
    l10 = m2 / m1
    l20 = m3 / m1
    d1 = m3 - l10 * m2
    t = m4 - l20 * m2
    has1 = d1 > floor * m3
    l21 = jnp.where(has1, t / d1, 0.0)
    d2 = m5 - l20 * m3 - l21 * t
    has2 = has1 & (d2 > floor * m5)
    y1 = m1 - l10 * m0
    y2 = m2 - l20 * m0 - l21 * y1
    c2 = jnp.where(has2, y2 / d2, 0.0)
    c1 = jnp.where(has1, y1 / d1, 0.0) - l21 * c2
    c0 = m0 / m1 - l10 * c1 - l20 * c2
    copy.wait()
    for g in range(0, SX, 8):
        rows = rows_at(g)
        out[rows, :] = c0 * fields[0, rows, :] + c1 * fields[1, rows, :] + c2 * fields[2, rows, :]


def finish(sums, fields):
    return pl.pallas_call(
        finish_kernel,
        in_specs=[pl.BlockSpec(memory_space=pl.ANY)] * 2,
        out_shape=jax.ShapeDtypeStruct((SX, SY), F32),
        scratch_shapes=[
            pltpu.VMEM((128, 128), F32),
            pltpu.VMEM((3, SX, SY), F32),
            pltpu.SemaphoreType.DMA((2,)),
        ],
        name="finish",
    )(sums, pltpu.with_memory_space_constraint(fields, pltpu.HBM))


def first_pairs(array, axis):
    return lax.ppermute(array, axis, [(i, i ^ 1) for i in range(lax.axis_size(axis))])


def second_pairs(array, axis, around):
    count = lax.axis_size(axis)
    pairs = [] if around else [(0, 0), (count - 1, count - 1)]
    for i in range(1, count if around else count - 1, 2):
        pairs += [(i, (i + 1) % count), ((i + 1) % count, i)]
    return lax.ppermute(array, axis, pairs)


def on_device(tracers, east, north, levels):
    to_first, to_second = edges(tracers, east, north, levels)
    second = second_pairs(to_second, "gx", True)
    first = first_pairs(to_first, "gx")
    own_rows, one, two, blocked, total = block(tracers, east, north, levels, to_first)
    own_edges, one, two, low, high = pack_edges(first, second, one, two)
    first = first_pairs(one, "gy")
    second = second_pairs(two, "gy", False)
    ends, ends_total = end_levels(tracers, east, north, levels, low, high)
    new, fields, sums = operator(
        levels, low, high, own_rows, own_edges, first, second, blocked, ends, total, ends_total, count=lax.axis_size("gy")
    )
    sums = lax.all_to_all(sums, ("gx", "gy"), split_axis=0, concat_axis=0, tiled=True)
    return new, finish(sums, fields)


def solution(mesh):
    placed = (P(None, None, "gx", "gy"), P(None, "gx", "gy"), P(None, "gx", "gy"), P("gx", "gy"))
    return jax.shard_map(
        on_device,
        mesh=mesh,
        in_specs=placed,
        out_specs=(P(None, None, "gx", "gy"), P("gx", "gy")),
        check_vma=False,
    )
```

```python
import functools

import jax
import jax.numpy as jnp
from jax import lax
from jax.experimental import pallas as pl
from jax.experimental.pallas import tpu as pltpu
from jax.sharding import PartitionSpec as P

KAPPA = 0.08
ALPHA = 0.05
F32 = jnp.float32

SX = 128
SY = 128
KL = 16
EDGE = 8
PAD = 16
ROWS = SX + 2 * PAD
WIDE = SX + 2 * EDGE
LOW = PAD - EDGE
ARRAYS = 2 * KL + 2 * KL + 1
VMEM = 40 * 1024 * 1024
GROUPS = tuple(range(LOW, LOW + WIDE, 8))
OUTSIDE = (LOW - 8, LOW + WIDE)
INNER = GROUPS[1:-1]
END_GROUPS = (8, 24, 32)
END_ROWS = 48
SENT = 3


def params():
    return pltpu.CompilerParams(vmem_limit_bytes=VMEM)


def is_even(axis):
    return lax.rem(lax.axis_index(axis), 2) == 0


def rows_at(row):
    return slice(row, row + 8)


def lanes(shape=(8, 128)):
    return lax.broadcasted_iota(jnp.int32, shape, len(shape) - 1)


def ahead_one(value):
    return pltpu.roll(value, 127, 1)


def back_one(value):
    return pltpu.roll(value, 1, 1)


def offsets(counts):
    starts, at = [], 8
    for a in range(4):
        starts.append(at)
        at += KL * counts[a]
    return starts, at


NEXT = (4, 4, 4, 4)
BEFORE = (5, 5, 4, 4)
NEXT_AT, NEXT_ROWS = offsets(NEXT)
BEFORE_AT, BEFORE_ROWS = offsets(BEFORE)
BEFORE_ROWS += 8
assert NEXT_ROWS <= BEFORE_ROWS


def edges_kernel(t, e, n, d, first_pair, second_pair, tiles, flows, depths, sems):
    copies = []
    for side, at in enumerate((0, SX - 8)):
        at16 = 0 if side == 0 else SX - 16
        copies += [
            (t.at[0, :, at : at + 8, :], tiles.at[side, 0]),
            (t.at[1, :, at : at + 8, :], tiles.at[side, 1]),
            (e.at[:, at16 : at16 + 16, :], flows.at[side, 0]),
            (n.at[:, at16 : at16 + 16, :], flows.at[side, 1]),
            (d.at[at : at + 8, :], depths.at[side]),
        ]
    copies = [pltpu.make_async_copy(src, dst, sems.at[i]) for i, (src, dst) in enumerate(copies)]
    for copy in copies:
        copy.start()
    for copy in copies:
        copy.wait()

    def write(before, after):
        for side, (out, starts, counts) in enumerate(((before, BEFORE_AT, BEFORE), (after, NEXT_AT, NEXT))):
            out[0:8, :] = depths[side].astype(F32)
            for a in range(4):
                for k in range(KL):
                    value = tiles[side, a, k] if a < 2 else flows[side, a - 2, k].astype(F32)[8 * side : 8 * side + 8]
                    from_row = 0 if side == 0 else 8 - counts[a]
                    at = starts[a] + counts[a] * k
                    out[at : at + counts[a], :] = value[from_row : from_row + counts[a]]
        before[BEFORE_ROWS - 8 : BEFORE_ROWS, :] = jnp.zeros((8, 128), F32)
        after[NEXT_ROWS:BEFORE_ROWS, :] = jnp.zeros((BEFORE_ROWS - NEXT_ROWS, 128), F32)

    @pl.when(is_even("gx"))
    def _():
        write(second_pair, first_pair)

    @pl.when(~is_even("gx"))
    def _():
        write(first_pair, second_pair)


def edges(tracers, east, north, levels):
    return pl.pallas_call(
        edges_kernel,
        in_specs=[pl.BlockSpec(memory_space=pltpu.HBM)] * 4,
        out_shape=[pltpu.VMEM((BEFORE_ROWS, SY), F32)] * 2,
        scratch_shapes=[
            pltpu.VMEM((2, 2, KL, 8, SY), F32),
            pltpu.VMEM((2, 2, KL, 16, SY), jnp.bfloat16),
            pltpu.VMEM((2, 8, SY), jnp.int32),
            pltpu.SemaphoreType.DMA((10,)),
        ],
        compiler_params=params(),
        name="edges",
    )(*(pltpu.with_memory_space_constraint(x, pltpu.HBM) for x in (tracers, east, north, levels)))


def low_tile(ref, a, k):
    if a == 4:
        return ref[0:8, :]
    at = NEXT_AT[a] + NEXT[a] * (k + 1) - 8
    return ref[at : at + 8, :]


def high_tile(ref, a, k):
    if a == 4:
        return ref[0:8, :]
    at = BEFORE_AT[a] + BEFORE[a] * k
    return ref[at : at + 8, :]


def pack(source, rows, last):
    group = lanes((rows, 128)) // 8
    one = jnp.zeros((rows, 128), F32)
    beyond = jnp.zeros((rows, 128), F32)
    for k in range(KL):
        value = source(k)
        one = jnp.where(group == k, pltpu.roll(value, (8 * k - 124) % 128, 1), one)
        if last:
            beyond = jnp.where(group == k, pltpu.roll(value, (8 * k + 3) % 128, 1), beyond)
    two = pltpu.roll(one, 127, 1)
    if last:
        two = jnp.where(lanes((rows, 128)) % 8 == 7, beyond, two)
    return one, two


def pack_depth(sources):
    lane = lanes(sources[0].shape)
    values = [pltpu.roll(x, turn, 1) for turn in (4, 3) for x in sources]
    values = [jnp.where(lane < 8, x, 0.0) for x in values]
    for turn in (8, 16, 32, 64):
        values = [x + pltpu.roll(x, turn, 1) for x in values]
    return list(zip(values[: len(sources)], values[len(sources) :], strict=True))


def merge_one(t0, t1, e, n, d):
    member = lanes(t0.shape) % 8
    return (
        jnp.where(member < 4, t0, pltpu.roll(n, 4, 1)),
        jnp.where(member < 4, t1, pltpu.roll(e, 4, 1)),
        d,
    )


def split_one(a, b, c):
    return a, b, pltpu.roll(b, 124, 1), pltpu.roll(a, 124, 1), c


def merge_two(t0, t1, e, n, d):
    member = lanes(t0.shape) % 8
    return (
        jnp.where(member < 3, pltpu.roll(d, 125, 1), t0),
        jnp.where(member < 2, pltpu.roll(d, 122, 1), t1),
        jnp.where((member >= 3) & (member < 7), n, pltpu.roll(e, 4, 1)),
    )


def split_two(a, b, c):
    member = lanes(a.shape) % 8
    depth = jnp.where(member < 6, pltpu.roll(a, 3, 1), pltpu.roll(b, 6, 1))
    return a, b, pltpu.roll(c, 124, 1), c, depth


def pack_all(sources, depths, rows, own, own_rows, first_pair, second_pair, sent_rows):
    packed = [pack(source, rows, a < 2) for a, source in enumerate(sources)] + [depths]
    for which in range(2):
        for a in range(5):
            own[which, a, own_rows, :] = packed[a][which]
    even = is_even("gy")
    ones = merge_one(*(p[0] for p in packed))
    twos = merge_two(*(p[1] for p in packed))
    for a in range(SENT):
        first_pair[a, sent_rows, :] = jnp.where(even, ones[a], twos[a])
        second_pair[a, sent_rows, :] = jnp.where(even, twos[a], ones[a])


def pack_block(t, e, n, d, own, one, two):
    chunk = 32
    groups = range(0, SX, 8)
    for g, pair in zip(groups, pack_depth([d[rows_at(g), :].astype(F32) for g in groups]), strict=True):
        for which in range(2):
            own[which, 4, rows_at(g), :] = pair[which]

    def body(i, carry):
        rows = pl.ds(pl.multiple_of(i * chunk, chunk), chunk)
        sources = (
            lambda k: t[0, k, rows, :],
            lambda k: t[1, k, rows, :],
            lambda k: e[k, rows, :].astype(F32),
            lambda k: n[k, rows, :].astype(F32),
        )
        depths = own[0, 4, rows, :], own[1, 4, rows, :]
        pack_all(sources, depths, chunk, own, rows, one, two, rows)
        return carry

    lax.fori_loop(0, SX // chunk, body, 0)


def pack_edges_kernel(first_pair, second_pair, first_rows, second_rows, own, one, two, low, high, low_in, high_in):
    for g in range(0, SX, 8):
        for a in range(SENT):
            one[a, rows_at(g + EDGE), :] = first_rows[a, rows_at(g), :]
            two[a, rows_at(g + EDGE), :] = second_rows[a, rows_at(g), :]
    even = is_even("gx")
    for at in range(0, BEFORE_ROWS, 8):
        rows = rows_at(at)
        value, other = first_pair[rows, :], second_pair[rows, :]
        low_in[rows, :] = jnp.where(even, other, value)
        high_in[rows, :] = jnp.where(even, value, other)
    for a in range(5):
        for k in range(KL if a < 4 else 1):
            low[KL * a + k] = low_tile(low_in, a, k)
            high[KL * a + k] = high_tile(high_in, a, k)
    depths = pack_depth([low_tile(low_in, 4, 0), high_tile(high_in, 4, 0)])
    for side, (ref, tile) in enumerate(((low_in, low_tile), (high_in, high_tile))):
        sources = [functools.partial(tile, ref, a) for a in range(4)]
        at = 0 if side == 0 else WIDE - EDGE
        pack_all(sources, depths[side], 8, own, rows_at(8 * side), one, two, rows_at(at))


def pack_edges(first, second, first_rows, second_rows):
    sent = jax.ShapeDtypeStruct((SENT, WIDE, 128), F32)
    halo = jax.ShapeDtypeStruct((ARRAYS, EDGE, SY), F32)
    return pl.pallas_call(
        pack_edges_kernel,
        out_shape=[jax.ShapeDtypeStruct((2, 5, 2 * EDGE, 128), F32), sent, sent, halo, halo],
        scratch_shapes=[pltpu.VMEM((BEFORE_ROWS, SY), F32)] * 2,
        compiler_params=params(),
        name="pack_edges",
    )(first, second, first_rows, second_rows)


def face_weights(face, flow_value, threshold):
    is_open = face > threshold
    ahead = jnp.where(is_open, KAPPA + jnp.maximum(flow_value, 0.0), 0.0)
    back = jnp.where(is_open, KAPPA - jnp.minimum(flow_value, 0.0), 0.0)
    return ahead, back


def two_steps(copies, groups, threshold, depth_at, faces, flow, coef, q0, q1, first_row=None):
    parts = [(c, g) for c in range(copies) for g in groups]
    every = [(c, t, g) for c, g in parts for t in range(2)]
    for c, g in parts:
        rows = rows_at(g)
        east, north = faces(c, g)
        coef[c, 0, rows, :], coef[c, 1, rows, :] = face_weights(east, flow[c, 0, rows, :], threshold(c))
        coef[c, 3, rows, :], coef[c, 2, rows, :] = face_weights(north, flow[c, 1, rows, :], threshold(c))
    b_south = {(c, g): back_one(coef[c, 2, rows_at(g), :]) for c, g in parts}

    def shifted(source):
        ahead = {(c, t, g): ahead_one(source[c, t, rows_at(g), :]) for c, t, g in every}
        behind = {
            (c, t, g): back_one(coef[c, 3, rows_at(g), :] * source[c, t, rows_at(g), :]) for c, t, g in every
        }
        return ahead, behind

    def combine(source, c, t, g, ahead, behind):
        rows = rows_at(g)
        return (
            coef[c, 4, rows, :] * source[c, t, rows, :]
            + coef[c, 1, rows, :] * source[c, t, rows_at(g + 1), :]
            + coef[c, 0, rows_at(g - 1), :] * source[c, t, rows_at(g - 1), :]
            + coef[c, 2, rows, :] * ahead
            + behind
        )

    ahead, behind = shifted(q0)
    for c, g in parts:
        rows = rows_at(g)
        b_here = b_south[c, g]
        if first_row is not None:
            b_here, behind[c, 0, g], behind[c, 1, g] = first_row(c, g, b_here, behind[c, 0, g], behind[c, 1, g])
        leaving = coef[c, 0, rows, :] + coef[c, 3, rows, :] + coef[c, 1, rows_at(g - 1), :] + b_here
        coef[c, 4, rows, :] = jnp.where(depth_at(c, g) > threshold(c), 1.0 - leaving, 0.0)
        for t in range(2):
            q1[c, t, rows, :] = combine(q0, c, t, g, ahead[c, t, g], behind[c, t, g])
    ahead, behind = shifted(q1)
    for c, g in parts:
        yield c, g, *(combine(q1, c, t, g, ahead[c, t, g], behind[c, t, g]) for t in range(2))


def halo_depth(levels, low, high, depth):
    for g in GROUPS:
        r = g - LOW
        if r < EDGE:
            value = low[4 * KL]
        elif r >= WIDE - EDGE:
            value = high[4 * KL]
        else:
            value = levels[rows_at(r - EDGE), :].astype(F32)
        depth[rows_at(g), :] = value
    for outside in OUTSIDE:
        depth[rows_at(outside), :] = jnp.zeros((8, 128), F32)


LEVELS = 2
END_LEVELS = 4
PLACED = 8
EARLY = 8


def set_faces(groups, depth, face):
    lane = lanes()
    ahead = {g: ahead_one(depth[rows_at(g), :]) for g in groups}
    for g in groups:
        rows = rows_at(g)
        here = depth[rows, :]
        face[0, rows, :] = jnp.minimum(here, depth[rows_at(g + 1), :])
        face[1, rows, :] = jnp.where(lane == 127, 0.0, jnp.minimum(here, ahead[g]))


def inner_levels(from_level, to_level, tracers, east, north, levels, new, total, depth, face, q0, q1, flow, coef):
    blank = jnp.zeros((8, 128), F32)
    for g in INNER:
        depth[rows_at(g), :] = levels[rows_at(g - PAD), :].astype(F32)
        total[rows_at(g), :] = blank
    for g in (GROUPS[0], GROUPS[-1]):
        depth[rows_at(g), :] = blank
        total[rows_at(g), :] = blank
        for c in range(LEVELS):
            for i in range(2):
                coef[c, i, rows_at(g), :] = blank
                q0[c, i, rows_at(g), :] = blank
                q1[c, i, rows_at(g), :] = blank
    set_faces(INNER, depth, face)

    def some_levels(i, carry):
        for c in range(LEVELS):
            k = from_level + LEVELS * i + c
            for t in range(2):
                q0[c, t, PAD : PAD + SX, :] = tracers[t, k]
            flow[c, 0, PAD : PAD + SX, :] = east[k].astype(F32)
            flow[c, 1, PAD : PAD + SX, :] = north[k].astype(F32)
        for c, g, temperature, salinity in two_steps(
            LEVELS,
            INNER,
            lambda c: (from_level + LEVELS * i + c).astype(F32),
            lambda c, g: depth[rows_at(g), :],
            lambda c, g: (face[0, rows_at(g), :], face[1, rows_at(g), :]),
            flow,
            coef,
            q0,
            q1,
        ):
            new[0, LEVELS * i + c, rows_at(g - PAD), :] = temperature
            new[1, LEVELS * i + c, rows_at(g - PAD), :] = salinity
            total[rows_at(g), :] += temperature - 0.8 * salinity
        return carry

    lax.fori_loop(0, (to_level - from_level) // LEVELS, some_levels, 0)


def block_kernel(tracers, east, north, levels, after, own, first_pair, second_pair, *rest):
    del after
    pack_block(tracers, east, north, levels, own, first_pair, second_pair)
    inner_levels(0, EARLY, tracers, east, north, levels, *rest)


def level_scratch(rows, copies):
    shapes = ((), (2,), (copies, 2), (copies, 2), (copies, 2), (copies, 5))
    return [pltpu.VMEM(shape + (rows, 128), F32) for shape in shapes]


def block(tracers, east, north, levels, after):
    sent = pltpu.VMEM((SENT, SX, 128), F32)
    return pl.pallas_call(
        block_kernel,
        in_specs=[pl.BlockSpec(memory_space=pltpu.VMEM)] * 4 + [pl.BlockSpec(memory_space=pl.ANY)],
        out_shape=[
            pltpu.VMEM((2, 5, SX, 128), F32),
            sent,
            sent,
            pltpu.VMEM((2, EARLY, SX, SY), F32),
            pltpu.VMEM((ROWS, 128), F32),
        ],
        scratch_shapes=level_scratch(ROWS, LEVELS),
        compiler_params=params(),
        cost_estimate=pl.CostEstimate(flops=20_000_000, bytes_accessed=24_000_000, transcendentals=0),
        name="block",
    )(tracers, east, north, levels, after)


def late_kernel(tracers, east, north, levels, low, high, new, total, ends_new, ends_total, *scratch):
    ends(tracers, east, north, levels, low, high, ends_new, ends_total, *scratch[6:])
    inner_levels(EARLY, KL, tracers, east, north, levels, new, total, *scratch[:6])


def ends(tracers, east, north, levels, low, high, new, total, depth, face, q0, q1, flow, coef):
    blank = jnp.zeros((8, 128), F32)
    for g in range(0, END_ROWS, 8):
        rows = rows_at(g)
        depth[rows, :] = blank
        total[rows, :] = blank
        if g not in END_GROUPS:
            for c in range(END_LEVELS):
                for i in range(2):
                    coef[c, i, rows, :] = blank
                    q0[c, i, rows, :] = blank
                    q1[c, i, rows, :] = blank
    depth[8:12, :] = low[4 * KL, 4:8, :]
    depth[12:16, :] = levels[0:8, :].astype(F32)[0:4]
    depth[24:32, :] = levels[SX - 8 : SX, :].astype(F32)
    depth[32:40, :] = high[4 * KL]
    set_faces(END_GROUPS, depth, face)

    def some_levels(i, carry):
        for c in range(END_LEVELS):
            k = END_LEVELS * i + c
            for t in range(2):
                q0[c, t, 8:12, :] = low[KL * t + k, 4:8, :]
                q0[c, t, 12:16, :] = tracers[t, k, 0:4, :]
                q0[c, t, 24:32, :] = tracers[t, k, SX - 8 : SX, :]
                q0[c, t, 32:40, :] = high[KL * t + k]
            for t, field in enumerate((east, north)):
                flow[c, t, 8:12, :] = low[KL * (2 + t) + k, 4:8, :]
                flow[c, t, 12:16, :] = field[k, 0:16, :].astype(F32)[0:4]
                flow[c, t, 24:32, :] = field[k, SX - 16 : SX, :].astype(F32)[8:16]
                flow[c, t, 32:40, :] = high[KL * (2 + t) + k]
        for c, g, temperature, salinity in two_steps(
            END_LEVELS,
            END_GROUPS,
            lambda c: (END_LEVELS * i + c).astype(F32),
            lambda c, g: depth[rows_at(g), :],
            lambda c, g: (face[0, rows_at(g), :], face[1, rows_at(g), :]),
            flow,
            coef,
            q0,
            q1,
        ):
            if g < 32:
                rows = rows_at(0 if g == 8 else 8)
                new[0, END_LEVELS * i + c, rows, :] = temperature
                new[1, END_LEVELS * i + c, rows, :] = salinity
            total[rows_at(g), :] += temperature - 0.8 * salinity
        return carry

    lax.fori_loop(0, KL // END_LEVELS, some_levels, 0)


def late_levels(tracers, east, north, levels, low, high):
    return pl.pallas_call(
        late_kernel,
        out_shape=[
            pltpu.VMEM((2, KL - EARLY, SX, SY), F32),
            pltpu.VMEM((ROWS, 128), F32),
            pltpu.VMEM((2, KL, 16, SY), F32),
            pltpu.VMEM((END_ROWS, 128), F32),
        ],
        scratch_shapes=level_scratch(ROWS, LEVELS) + level_scratch(END_ROWS, END_LEVELS),
        compiler_params=params(),
        cost_estimate=pl.CostEstimate(flops=5_000_000, bytes_accessed=6_000_000, transcendentals=0),
        name="late_levels",
    )(tracers, east, north, levels, low, high)


def operator_kernel(
    levels, low, high, own_rows, own_edges, first_pair, second_pair, early, early_total,
    late, late_total, ends, ends_total,
    new, fields, sums,
    depth, q0, q1, strip_depth, strip_face, strip_flow, strip_total, first_q, coef, wall, total, field, grid, staged, sems,
    *, count,
):
    lane = lanes()
    member = lane % 8
    blank = jnp.zeros((8, 128), F32)
    strip_level = (lane // 8).astype(F32)
    first = lax.axis_index("gy") == 0
    last = lax.axis_index("gy") == count - 1

    def own(which, a, g):
        r = g - LOW
        if r < EDGE:
            return own_edges[which, a, rows_at(0), :]
        if r >= WIDE - EDGE:
            return own_edges[which, a, rows_at(8), :]
        return own_rows[which, a, rows_at(r - EDGE), :]

    even = is_even("gy")

    def sent(g):
        rows = rows_at(g - LOW)
        pairs = [(first_pair[a, rows, :], second_pair[a, rows, :]) for a in range(SENT)]
        return [jnp.where(even, b, a) for a, b in pairs], [jnp.where(even, a, b) for a, b in pairs]

    halo_depth(levels, low, high, depth)
    parts = {}
    for g in GROUPS:
        from_low, from_high = sent(g)
        parts[g] = list(split_one(*from_low)), list(split_two(*from_high))
    for g in GROUPS:
        rows = rows_at(g)
        from_low, from_high = parts[g]
        from_low[4] = jnp.where(first, 0.0, from_low[4])
        from_high[4] = jnp.where(last, 0.0, from_high[4])
        for a in range(5):
            low_strip = jnp.where(member < 4, from_low[a], own(0, a, g))
            high_strip = jnp.where(member >= 3, from_high[a], own(1, a, g))
            for side, value in enumerate((low_strip, high_strip)):
                if a < 2:
                    q0[side, a, rows, :] = value
                elif a < 4:
                    strip_flow[side, a - 2, rows, :] = value
                else:
                    strip_depth[side, rows, :] = value
    for outside in OUTSIDE:
        for side in range(2):
            strip_depth[side, rows_at(outside), :] = blank

    ahead = {
        (side, g): ahead_one(strip_depth[side, rows_at(g), :]) for side in range(2) for g in GROUPS
    }
    for (side, g), value in ahead.items():
        strip_face[side, rows_at(g), :] = jnp.minimum(strip_depth[side, rows_at(g), :], value)

    for side in range(2):
        for i in range(2):
            coef[side, i, rows_at(LOW - 8), :] = blank

    def first_row(side, g, b_south, *behind):
        if side == 0:
            return b_south, *behind
        face = jnp.minimum(own(0, 4, g), own(1, 4, g))
        a_first, b_first = face_weights(face, own(0, 3, g), strip_level)
        return (
            jnp.where(member == 0, b_first, b_south),
            *(jnp.where(member == 0, a_first * own(0, t, g), behind[t]) for t in range(2)),
        )

    for side, g, temperature, salinity in two_steps(
        2,
        GROUPS,
        lambda side: strip_level,
        lambda side, g: strip_depth[side, rows_at(g), :],
        lambda side, g: (
            jnp.minimum(strip_depth[side, rows_at(g), :], strip_depth[side, rows_at(g + 1), :]),
            strip_face[side, rows_at(g), :],
        ),
        strip_flow,
        coef,
        q0,
        q1,
        first_row,
    ):
        rows = rows_at(g)
        q0[side, 0, rows, :] = temperature
        q0[side, 1, rows, :] = salinity
        strip_total[side, rows, :] = temperature - 0.8 * salinity
    for turn in (8, 16, 32, 64):
        values = {}
        for side in range(2):
            for g in GROUPS:
                value = strip_total[side, rows_at(g), :]
                values[side, g] = value + pltpu.roll(value, turn, 1)
        for (side, g), value in values.items():
            strip_total[side, rows_at(g), :] = value

    for tracer in range(2):
        high_values = {g: back_one(q0[1, tracer, rows_at(g), :]) for g in INNER}
        for g in INNER:
            rows = rows_at(g)
            first_q[tracer, rows, :] = jnp.where(member >= 4, q0[0, tracer, rows, :], high_values[g])
    from_strip = (lane < 2) | (lane >= 126)
    row = lax.broadcasted_iota(jnp.int32, (8, 128), 0)

    def place(blocked, first_level):
        slots = [(t, first_level + c, c, g) for c in range(PLACED) for t in range(2) for g in range(0, SX, 8)]
        turned = {
            (t, c, g): pltpu.roll(first_q[t, rows_at(g + PAD), :], 124 - 8 * k, 1) for t, k, c, g in slots
        }
        for t, k, c, g in slots:
            rows = rows_at(g)
            here = blocked[t, c, rows, :]
            if g == 0:
                here = jnp.where(row < 2, ends[t, k, rows_at(4), :], here)
            elif g == SX - 8:
                here = jnp.where(row >= 6, ends[t, k, rows_at(8), :], here)
            staged[t, k, rows, :] = jnp.where(from_strip, turned[t, c, g], here)
        at = slice(first_level, first_level + PLACED)
        for t in range(2):
            pltpu.make_async_copy(staged.at[t, at], new.at[t, at], sems.at[0]).start()

    for first_level in range(0, KL, PLACED):
        for start, blocked in ((0, early), (EARLY, late)):
            if start <= first_level < (EARLY if start == 0 else KL):
                place(blocked.at[:, first_level - start : first_level - start + PLACED], first_level)

    def beside(low_value, high_value):
        return jnp.where(lane >= 64, pltpu.roll(low_value, 4, 1), pltpu.roll(high_value, 5, 1))

    def northward(main, side):
        a, b = ahead_one(main), ahead_one(side)
        return jnp.where(lane == 127, b, a), jnp.where(lane == 127, a, b)

    def southward(main, side):
        a, b = back_one(main), back_one(side)
        return jnp.where(lane == 0, b, a), jnp.where(lane == 0, a, b)

    for g in GROUPS:
        wall[rows_at(g), :] = early_total[rows_at(g), :] + late_total[rows_at(g), :]
    wall[PAD - 2 : PAD + 2, :] = ends_total[10:14, :]
    wall[PAD + SX - 2 : PAD + SX + 3, :] = ends_total[30:35, :]
    for g in GROUPS + OUTSIDE:
        rows = rows_at(g)
        grid[0, 0, rows, :] = depth[rows, :]
        grid[0, 1, rows, :] = beside(strip_depth[0, rows, :], strip_depth[1, rows, :])
    further_all = {g: northward(grid[0, 0, rows_at(g), :], grid[0, 1, rows_at(g), :]) for g in GROUPS}
    strip_sums = {
        g: (pltpu.roll(strip_total[0, rows_at(g), :], 4, 1), pltpu.roll(strip_total[1, rows_at(g), :], 5, 1))
        for g in GROUPS
    }
    for g in GROUPS:
        rows = rows_at(g)
        both = grid[0, 0, rows, :], grid[0, 1, rows, :]
        further = further_all[g]
        for part in range(2):
            grid[1, part, rows, :] = jnp.minimum(both[part], grid[0, part, rows_at(g + 1), :])
            grid[2, part, rows, :] = jnp.minimum(both[part], further[part])
        low_total, high_total = strip_sums[g]
        edge_total = jnp.where(lane < 64, low_total, high_total)
        total[0, rows, :] = jnp.where(from_strip, edge_total, wall[rows, :])
        total[1, rows, :] = jnp.where(lane >= 64, low_total, high_total)
    for part in range(2):
        grid[1, part, rows_at(LOW - 8), :] = blank
        for outside in OUTSIDE:
            for i in range(3):
                field[i, part, rows_at(outside), :] = blank
    scale = 1.0 / KL
    south_faces = {g: southward(grid[2, 0, rows_at(g), :], grid[2, 1, rows_at(g), :]) for g in GROUPS}
    for g in GROUPS:
        rows = rows_at(g)
        souths = south_faces[g]
        for part in range(2):
            grid[6, part, rows, :] = souths[part]
            here = grid[0, part, rows, :]
            own_part = ALPHA * scale * here + jnp.where(here == 0.0, 1.0, 0.0)
            faces = grid[1, part, rows, :] + grid[1, part, rows_at(g - 1), :] + grid[2, part, rows, :] + souths[part]
            diagonal = own_part + scale * faces
            inverse = 1.0 / diagonal
            grid[3, part, rows, :] = inverse
            grid[4, part, rows, :] = own_part
            grid[5, part, rows, :] = diagonal
            field[0, part, rows, :] = 0.25 * total[part, rows, :] * inverse

    moments = [blank] * 6
    for i in range(3):
        groups = GROUPS if i < 2 else INNER
        pairs = {g: (field[i, 0, rows_at(g), :], field[i, 1, rows_at(g), :]) for g in groups}
        all_norths = {g: northward(*pairs[g]) for g in groups}
        all_souths = {g: southward(*pairs[g]) for g in groups} if i < 2 else {}
        for g in groups:
            rows = rows_at(g)
            both = pairs[g]
            norths = all_norths[g]
            for part in range(2):
                if i == 2 and part == 1:
                    continue
                here = both[part]
                east_gap = here - field[i, part, rows_at(g + 1), :]
                north_gap = here - norths[part]
                east_face = scale * grid[1, part, rows, :]
                north_face = scale * grid[2, part, rows, :]
                own_part = grid[4, part, rows, :]
                if part == 0 and PAD <= g < PAD + SX:
                    moments[2 * i] += grid[5, 0, rows, :] * here * here
                    moments[2 * i + 1] += (
                        own_part * here * here + east_face * east_gap * east_gap + north_face * north_gap * north_gap
                    )
                if i < 2:
                    image = (
                        own_part * here
                        + east_face * east_gap
                        + scale * grid[1, part, rows_at(g - 1), :] * (here - field[i, part, rows_at(g - 1), :])
                        + north_face * north_gap
                        + scale * grid[6, part, rows, :] * (here - all_souths[g][part])
                    )
                    field[i + 1, part, rows, :] = image * grid[3, part, rows, :]
        pltpu.make_async_copy(field.at[i, 0, PAD : PAD + SX, :], fields.at[i], sems.at[1]).start()
    sums_row = jnp.zeros((8, 128), F32)
    for i in range(6):
        value = jnp.sum(jnp.sum(moments[i], axis=0, keepdims=True), axis=1, keepdims=True)
        sums_row = jnp.where(lane == i, value, sums_row)
    for g in range(0, 128, 8):
        sums[rows_at(g), :] = sums_row
    pltpu.make_async_copy(field.at[:, 0, PAD : PAD + SX, :], fields, sems.at[1]).wait()
    pltpu.make_async_copy(staged, new, sems.at[0]).wait()


def operator(*arrays, count):
    tall = (ROWS, 128)
    scratch = (
        (),
        (2, 2),
        (2, 2),
        (2,),
        (2,),
        (2, 2),
        (2,),
        (2,),
        (2, 5),
        (),
        (2,),
        (3, 2),
        (7, 2),
    )
    return pl.pallas_call(
        functools.partial(operator_kernel, count=count),
        out_shape=[
            jax.ShapeDtypeStruct((2, KL, SX, SY), F32),
            pltpu.HBM((3, SX, SY), F32),
            jax.ShapeDtypeStruct((128, 128), F32),
        ],
        out_specs=[
            pl.BlockSpec(memory_space=pltpu.HBM),
            pl.BlockSpec(memory_space=pltpu.HBM),
            pl.BlockSpec(memory_space=pltpu.VMEM),
        ],
        scratch_shapes=[pltpu.VMEM(s + tall, F32) for s in scratch]
        + [pltpu.VMEM((2, KL, SX, SY), F32), pltpu.SemaphoreType.DMA((2,))],
        compiler_params=params(),
        name="operator",
    )(*arrays)


def finish_kernel(sums_in, fields_in, out, sums, fields, sems):
    first_copy = pltpu.make_async_copy(sums_in, sums, sems.at[0])
    copy = pltpu.make_async_copy(fields_in, fields, sems.at[1])
    first_copy.start()
    copy.start()
    first_copy.wait()
    value = sums[0:8, :]
    for g in range(8, 128, 8):
        value = value + sums[rows_at(g), :]
    value = jnp.sum(value, axis=0, keepdims=True)
    lane = lanes((1, 128))
    m0, m1, m2, m3, m4, m5 = (
        jnp.sum(jnp.where(lane == i, value, 0.0), axis=1, keepdims=True) for i in range(6)
    )
    floor = 4e-7
    l10 = m2 / m1
    l20 = m3 / m1
    d1 = m3 - l10 * m2
    t = m4 - l20 * m2
    has1 = d1 > floor * m3
    l21 = jnp.where(has1, t / d1, 0.0)
    d2 = m5 - l20 * m3 - l21 * t
    has2 = has1 & (d2 > floor * m5)
    y1 = m1 - l10 * m0
    y2 = m2 - l20 * m0 - l21 * y1
    c2 = jnp.where(has2, y2 / d2, 0.0)
    c1 = jnp.where(has1, y1 / d1, 0.0) - l21 * c2
    c0 = m0 / m1 - l10 * c1 - l20 * c2
    copy.wait()
    for g in range(0, SX, 8):
        rows = rows_at(g)
        out[rows, :] = c0 * fields[0, rows, :] + c1 * fields[1, rows, :] + c2 * fields[2, rows, :]


def finish(sums, fields):
    return pl.pallas_call(
        finish_kernel,
        in_specs=[pl.BlockSpec(memory_space=pl.ANY)] * 2,
        out_shape=jax.ShapeDtypeStruct((SX, SY), F32),
        scratch_shapes=[
            pltpu.VMEM((128, 128), F32),
            pltpu.VMEM((3, SX, SY), F32),
            pltpu.SemaphoreType.DMA((2,)),
        ],
        name="finish",
    )(sums, pltpu.with_memory_space_constraint(fields, pltpu.HBM))


def first_pairs(array, axis):
    return lax.ppermute(array, axis, [(i, i ^ 1) for i in range(lax.axis_size(axis))])


def second_pairs(array, axis, around):
    count = lax.axis_size(axis)
    pairs = [] if around else [(0, 0), (count - 1, count - 1)]
    for i in range(1, count if around else count - 1, 2):
        pairs += [(i, (i + 1) % count), ((i + 1) % count, i)]
    return lax.ppermute(array, axis, pairs)


def on_device(tracers, east, north, levels):
    to_first, to_second = edges(tracers, east, north, levels)
    second = second_pairs(to_second, "gx", True)
    first = first_pairs(to_first, "gx")
    own_rows, one, two, early, early_total = block(tracers, east, north, levels, to_first)
    own_edges, one, two, low, high = pack_edges(first, second, one, two)
    second = second_pairs(two, "gy", False)
    first = first_pairs(one, "gy")
    later = late_levels(tracers, east, north, levels, low, high)
    new, fields, sums = operator(
        levels, low, high, own_rows, own_edges, first, second, early, early_total, *later, count=lax.axis_size("gy")
    )
    sums = lax.all_to_all(sums, ("gx", "gy"), split_axis=0, concat_axis=0, tiled=True)
    return new, finish(sums, fields)


def solution(mesh):
    placed = (P(None, None, "gx", "gy"), P(None, "gx", "gy"), P(None, "gx", "gy"), P("gx", "gy"))
    return jax.shard_map(
        on_device,
        mesh=mesh,
        in_specs=placed,
        out_specs=(P(None, None, "gx", "gy"), P("gx", "gy")),
        check_vma=False,
    )
```

```python
import functools

import jax
import jax.numpy as jnp
from jax import lax
from jax.experimental import pallas as pl
from jax.experimental.pallas import tpu as pltpu
from jax.sharding import PartitionSpec as P

KAPPA = 0.08
ALPHA = 0.05
F32 = jnp.float32

SX = 128
SY = 128
KL = 16
EDGE = 8
PAD = 16
ROWS = SX + 2 * PAD
WIDE = SX + 2 * EDGE
LOW = PAD - EDGE
ARRAYS = 2 * KL + 2 * KL + 1
VMEM = 40 * 1024 * 1024
GROUPS = tuple(range(LOW, LOW + WIDE, 8))
OUTSIDE = (LOW - 8, LOW + WIDE)
INNER = GROUPS[1:-1]
END_GROUPS = (8, 24, 32)
END_ROWS = 48
SENT = 3


def params():
    return pltpu.CompilerParams(vmem_limit_bytes=VMEM)


def is_even(axis):
    return lax.rem(lax.axis_index(axis), 2) == 0


def rows_at(row):
    return slice(row, row + 8)


def lanes(shape=(8, 128)):
    return lax.broadcasted_iota(jnp.int32, shape, len(shape) - 1)


def ahead_one(value):
    return pltpu.roll(value, 127, 1)


def back_one(value):
    return pltpu.roll(value, 1, 1)


def offsets(counts):
    starts, at = [], 8
    for a in range(4):
        starts.append(at)
        at += KL * counts[a]
    return starts, at


NEXT = (4, 4, 4, 4)
BEFORE = (5, 5, 4, 4)
NEXT_AT, NEXT_ROWS = offsets(NEXT)
BEFORE_AT, BEFORE_ROWS = offsets(BEFORE)
BEFORE_ROWS += 8
assert NEXT_ROWS <= BEFORE_ROWS


def edges_kernel(t, e, n, d, first_pair, second_pair, tiles, flows, depths, sems):
    copies = []
    for side, at in enumerate((0, SX - 8)):
        at16 = 0 if side == 0 else SX - 16
        copies += [
            (t.at[0, :, at : at + 8, :], tiles.at[side, 0]),
            (t.at[1, :, at : at + 8, :], tiles.at[side, 1]),
            (e.at[:, at16 : at16 + 16, :], flows.at[side, 0]),
            (n.at[:, at16 : at16 + 16, :], flows.at[side, 1]),
            (d.at[at : at + 8, :], depths.at[side]),
        ]
    copies = [pltpu.make_async_copy(src, dst, sems.at[i]) for i, (src, dst) in enumerate(copies)]
    for copy in copies:
        copy.start()
    for copy in copies:
        copy.wait()

    def write(before, after):
        for side, (out, starts, counts) in enumerate(((before, BEFORE_AT, BEFORE), (after, NEXT_AT, NEXT))):
            out[0:8, :] = depths[side].astype(F32)
            for a in range(4):
                for k in range(KL):
                    value = tiles[side, a, k] if a < 2 else flows[side, a - 2, k].astype(F32)[8 * side : 8 * side + 8]
                    from_row = 0 if side == 0 else 8 - counts[a]
                    at = starts[a] + counts[a] * k
                    out[at : at + counts[a], :] = value[from_row : from_row + counts[a]]
        before[BEFORE_ROWS - 8 : BEFORE_ROWS, :] = jnp.zeros((8, 128), F32)
        after[NEXT_ROWS:BEFORE_ROWS, :] = jnp.zeros((BEFORE_ROWS - NEXT_ROWS, 128), F32)

    @pl.when(is_even("gx"))
    def _():
        write(second_pair, first_pair)

    @pl.when(~is_even("gx"))
    def _():
        write(first_pair, second_pair)


def edges(tracers, east, north, levels):
    return pl.pallas_call(
        edges_kernel,
        in_specs=[pl.BlockSpec(memory_space=pltpu.HBM)] * 4,
        out_shape=[pltpu.VMEM((BEFORE_ROWS, SY), F32)] * 2,
        scratch_shapes=[
            pltpu.VMEM((2, 2, KL, 8, SY), F32),
            pltpu.VMEM((2, 2, KL, 16, SY), jnp.bfloat16),
            pltpu.VMEM((2, 8, SY), jnp.int32),
            pltpu.SemaphoreType.DMA((10,)),
        ],
        compiler_params=params(),
        name="edges",
    )(*(pltpu.with_memory_space_constraint(x, pltpu.HBM) for x in (tracers, east, north, levels)))


def low_tile(ref, a, k):
    if a == 4:
        return ref[0:8, :]
    at = NEXT_AT[a] + NEXT[a] * (k + 1) - 8
    return ref[at : at + 8, :]


def high_tile(ref, a, k):
    if a == 4:
        return ref[0:8, :]
    at = BEFORE_AT[a] + BEFORE[a] * k
    return ref[at : at + 8, :]


def pack(source, rows, last):
    group = lanes((rows, 128)) // 8
    one = jnp.zeros((rows, 128), F32)
    beyond = jnp.zeros((rows, 128), F32)
    for k in range(KL):
        value = source(k)
        one = jnp.where(group == k, pltpu.roll(value, (8 * k - 124) % 128, 1), one)
        if last:
            beyond = jnp.where(group == k, pltpu.roll(value, (8 * k + 3) % 128, 1), beyond)
    two = pltpu.roll(one, 127, 1)
    if last:
        two = jnp.where(lanes((rows, 128)) % 8 == 7, beyond, two)
    return one, two


def pack_depth(sources):
    lane = lanes(sources[0].shape)
    values = [pltpu.roll(x, turn, 1) for turn in (4, 3) for x in sources]
    values = [jnp.where(lane < 8, x, 0.0) for x in values]
    for turn in (8, 16, 32, 64):
        values = [x + pltpu.roll(x, turn, 1) for x in values]
    return list(zip(values[: len(sources)], values[len(sources) :], strict=True))


def merge_one(t0, t1, e, n, d):
    member = lanes(t0.shape) % 8
    return (
        jnp.where(member < 4, t0, pltpu.roll(n, 4, 1)),
        jnp.where(member < 4, t1, pltpu.roll(e, 4, 1)),
        d,
    )


def split_one(a, b, c):
    return a, b, pltpu.roll(b, 124, 1), pltpu.roll(a, 124, 1), c


def merge_two(t0, t1, e, n, d):
    member = lanes(t0.shape) % 8
    return (
        jnp.where(member < 3, pltpu.roll(d, 125, 1), t0),
        jnp.where(member < 2, pltpu.roll(d, 122, 1), t1),
        jnp.where((member >= 3) & (member < 7), n, pltpu.roll(e, 4, 1)),
    )


def split_two(a, b, c):
    member = lanes(a.shape) % 8
    depth = jnp.where(member < 6, pltpu.roll(a, 3, 1), pltpu.roll(b, 6, 1))
    return a, b, pltpu.roll(c, 124, 1), c, depth


def pack_all(sources, depths, rows, own, own_rows, first_pair, second_pair, sent_rows):
    packed = [pack(source, rows, a < 2) for a, source in enumerate(sources)] + [depths]
    for which in range(2):
        for a in range(5):
            own[which, a, own_rows, :] = packed[a][which]
    even = is_even("gy")
    ones = merge_one(*(p[0] for p in packed))
    twos = merge_two(*(p[1] for p in packed))
    for a in range(SENT):
        first_pair[a, sent_rows, :] = jnp.where(even, ones[a], twos[a])
        second_pair[a, sent_rows, :] = jnp.where(even, twos[a], ones[a])


def pack_block(t, e, n, d, own, one, two):
    chunk = 32
    groups = range(0, SX, 8)
    for g, pair in zip(groups, pack_depth([d[rows_at(g), :].astype(F32) for g in groups]), strict=True):
        for which in range(2):
            own[which, 4, rows_at(g), :] = pair[which]

    def body(i, carry):
        rows = pl.ds(pl.multiple_of(i * chunk, chunk), chunk)
        sources = (
            lambda k: t[0, k, rows, :],
            lambda k: t[1, k, rows, :],
            lambda k: e[k, rows, :].astype(F32),
            lambda k: n[k, rows, :].astype(F32),
        )
        depths = own[0, 4, rows, :], own[1, 4, rows, :]
        pack_all(sources, depths, chunk, own, rows, one, two, rows)
        return carry

    lax.fori_loop(0, SX // chunk, body, 0)


def pack_edges_kernel(first_pair, second_pair, first_rows, second_rows, own, one, two, low, high, low_in, high_in):
    for g in range(0, SX, 8):
        for a in range(SENT):
            one[a, rows_at(g + EDGE), :] = first_rows[a, rows_at(g), :]
            two[a, rows_at(g + EDGE), :] = second_rows[a, rows_at(g), :]
    even = is_even("gx")
    for at in range(0, BEFORE_ROWS, 8):
        rows = rows_at(at)
        value, other = first_pair[rows, :], second_pair[rows, :]
        low_in[rows, :] = jnp.where(even, other, value)
        high_in[rows, :] = jnp.where(even, value, other)
    for a in range(5):
        for k in range(KL if a < 4 else 1):
            low[KL * a + k] = low_tile(low_in, a, k)
            high[KL * a + k] = high_tile(high_in, a, k)
    depths = pack_depth([low_tile(low_in, 4, 0), high_tile(high_in, 4, 0)])
    for side, (ref, tile) in enumerate(((low_in, low_tile), (high_in, high_tile))):
        sources = [functools.partial(tile, ref, a) for a in range(4)]
        at = 0 if side == 0 else WIDE - EDGE
        pack_all(sources, depths[side], 8, own, rows_at(8 * side), one, two, rows_at(at))


def pack_edges(first, second, first_rows, second_rows):
    sent = jax.ShapeDtypeStruct((SENT, WIDE, 128), F32)
    halo = jax.ShapeDtypeStruct((ARRAYS, EDGE, SY), F32)
    return pl.pallas_call(
        pack_edges_kernel,
        out_shape=[jax.ShapeDtypeStruct((2, 5, 2 * EDGE, 128), F32), sent, sent, halo, halo],
        scratch_shapes=[pltpu.VMEM((BEFORE_ROWS, SY), F32)] * 2,
        compiler_params=params(),
        name="pack_edges",
    )(first, second, first_rows, second_rows)


def face_weights(face, flow_value, threshold):
    is_open = face > threshold
    ahead = jnp.where(is_open, KAPPA + jnp.maximum(flow_value, 0.0), 0.0)
    back = jnp.where(is_open, KAPPA - jnp.minimum(flow_value, 0.0), 0.0)
    return ahead, back


def two_steps(copies, groups, threshold, depth_at, faces, flow, coef, q0, q1, first_row=None):
    parts = [(c, g) for c in range(copies) for g in groups]
    every = [(c, t, g) for c, g in parts for t in range(2)]
    for c, g in parts:
        rows = rows_at(g)
        east, north = faces(c, g)
        coef[c, 0, rows, :], coef[c, 1, rows, :] = face_weights(east, flow[c, 0, rows, :], threshold(c))
        coef[c, 3, rows, :], coef[c, 2, rows, :] = face_weights(north, flow[c, 1, rows, :], threshold(c))
    b_south = {(c, g): back_one(coef[c, 2, rows_at(g), :]) for c, g in parts}

    def shifted(source):
        ahead = {(c, t, g): ahead_one(source[c, t, rows_at(g), :]) for c, t, g in every}
        behind = {
            (c, t, g): back_one(coef[c, 3, rows_at(g), :] * source[c, t, rows_at(g), :]) for c, t, g in every
        }
        return ahead, behind

    def combine(source, c, t, g, ahead, behind):
        rows = rows_at(g)
        return (
            coef[c, 4, rows, :] * source[c, t, rows, :]
            + coef[c, 1, rows, :] * source[c, t, rows_at(g + 1), :]
            + coef[c, 0, rows_at(g - 1), :] * source[c, t, rows_at(g - 1), :]
            + coef[c, 2, rows, :] * ahead
            + behind
        )

    ahead, behind = shifted(q0)
    for c, g in parts:
        rows = rows_at(g)
        b_here = b_south[c, g]
        if first_row is not None:
            b_here, behind[c, 0, g], behind[c, 1, g] = first_row(c, g, b_here, behind[c, 0, g], behind[c, 1, g])
        leaving = coef[c, 0, rows, :] + coef[c, 3, rows, :] + coef[c, 1, rows_at(g - 1), :] + b_here
        coef[c, 4, rows, :] = jnp.where(depth_at(c, g) > threshold(c), 1.0 - leaving, 0.0)
        for t in range(2):
            q1[c, t, rows, :] = combine(q0, c, t, g, ahead[c, t, g], behind[c, t, g])
    ahead, behind = shifted(q1)
    for c, g in parts:
        yield c, g, *(combine(q1, c, t, g, ahead[c, t, g], behind[c, t, g]) for t in range(2))


def halo_depth(levels, low, high, depth):
    for g in GROUPS:
        r = g - LOW
        if r < EDGE:
            value = low[4 * KL]
        elif r >= WIDE - EDGE:
            value = high[4 * KL]
        else:
            value = levels[rows_at(r - EDGE), :].astype(F32)
        depth[rows_at(g), :] = value
    for outside in OUTSIDE:
        depth[rows_at(outside), :] = jnp.zeros((8, 128), F32)


LEVELS = 2
END_LEVELS = 4
PLACED = 8
EARLY = 8


def set_faces(groups, depth, face):
    lane = lanes()
    ahead = {g: ahead_one(depth[rows_at(g), :]) for g in groups}
    for g in groups:
        rows = rows_at(g)
        here = depth[rows, :]
        face[0, rows, :] = jnp.minimum(here, depth[rows_at(g + 1), :])
        face[1, rows, :] = jnp.where(lane == 127, 0.0, jnp.minimum(here, ahead[g]))


def inner_levels(from_level, to_level, tracers, east, north, levels, new, total, depth, face, q0, q1, flow, coef):
    blank = jnp.zeros((8, 128), F32)
    for g in INNER:
        depth[rows_at(g), :] = levels[rows_at(g - PAD), :].astype(F32)
        total[rows_at(g), :] = blank
    for g in (GROUPS[0], GROUPS[-1]):
        depth[rows_at(g), :] = blank
        total[rows_at(g), :] = blank
        for c in range(LEVELS):
            for i in range(2):
                coef[c, i, rows_at(g), :] = blank
                q0[c, i, rows_at(g), :] = blank
                q1[c, i, rows_at(g), :] = blank
    set_faces(INNER, depth, face)

    def some_levels(i, carry):
        for c in range(LEVELS):
            k = from_level + LEVELS * i + c
            for t in range(2):
                q0[c, t, PAD : PAD + SX, :] = tracers[t, k]
            flow[c, 0, PAD : PAD + SX, :] = east[k].astype(F32)
            flow[c, 1, PAD : PAD + SX, :] = north[k].astype(F32)
        for c, g, temperature, salinity in two_steps(
            LEVELS,
            INNER,
            lambda c: (from_level + LEVELS * i + c).astype(F32),
            lambda c, g: depth[rows_at(g), :],
            lambda c, g: (face[0, rows_at(g), :], face[1, rows_at(g), :]),
            flow,
            coef,
            q0,
            q1,
        ):
            new[0, LEVELS * i + c, rows_at(g - PAD), :] = temperature
            new[1, LEVELS * i + c, rows_at(g - PAD), :] = salinity
            total[rows_at(g), :] += temperature - 0.8 * salinity
        return carry

    lax.fori_loop(0, (to_level - from_level) // LEVELS, some_levels, 0)


def block_kernel(tracers, east, north, levels, after, own, first_pair, second_pair, *rest):
    del after
    pack_block(tracers, east, north, levels, own, first_pair, second_pair)
    inner_levels(0, EARLY, tracers, east, north, levels, *rest)


def level_scratch(rows, copies):
    shapes = ((), (2,), (copies, 2), (copies, 2), (copies, 2), (copies, 5))
    return [pltpu.VMEM(shape + (rows, 128), F32) for shape in shapes]


def block(tracers, east, north, levels, after):
    sent = pltpu.VMEM((SENT, SX, 128), F32)
    return pl.pallas_call(
        block_kernel,
        in_specs=[pl.BlockSpec(memory_space=pltpu.VMEM)] * 4 + [pl.BlockSpec(memory_space=pl.ANY)],
        out_shape=[
            pltpu.VMEM((2, 5, SX, 128), F32),
            sent,
            sent,
            pltpu.VMEM((2, EARLY, SX, SY), F32),
            pltpu.VMEM((ROWS, 128), F32),
        ],
        scratch_shapes=level_scratch(ROWS, LEVELS),
        compiler_params=params(),
        cost_estimate=pl.CostEstimate(flops=20_000_000, bytes_accessed=24_000_000, transcendentals=0),
        name="block",
    )(tracers, east, north, levels, after)


def late_kernel(tracers, east, north, levels, low, high, new, total, ends_new, ends_total, *scratch):
    ends(tracers, east, north, levels, low, high, ends_new, ends_total, *scratch[6:])
    inner_levels(EARLY, KL, tracers, east, north, levels, new, total, *scratch[:6])


def ends(tracers, east, north, levels, low, high, new, total, depth, face, q0, q1, flow, coef):
    blank = jnp.zeros((8, 128), F32)
    for g in range(0, END_ROWS, 8):
        rows = rows_at(g)
        depth[rows, :] = blank
        total[rows, :] = blank
        if g not in END_GROUPS:
            for c in range(END_LEVELS):
                for i in range(2):
                    coef[c, i, rows, :] = blank
                    q0[c, i, rows, :] = blank
                    q1[c, i, rows, :] = blank
    depth[8:12, :] = low[4 * KL, 4:8, :]
    depth[12:16, :] = levels[0:8, :].astype(F32)[0:4]
    depth[24:32, :] = levels[SX - 8 : SX, :].astype(F32)
    depth[32:40, :] = high[4 * KL]
    set_faces(END_GROUPS, depth, face)

    def some_levels(i, carry):
        for c in range(END_LEVELS):
            k = END_LEVELS * i + c
            for t in range(2):
                q0[c, t, 8:12, :] = low[KL * t + k, 4:8, :]
                q0[c, t, 12:16, :] = tracers[t, k, 0:4, :]
                q0[c, t, 24:32, :] = tracers[t, k, SX - 8 : SX, :]
                q0[c, t, 32:40, :] = high[KL * t + k]
            for t, field in enumerate((east, north)):
                flow[c, t, 8:12, :] = low[KL * (2 + t) + k, 4:8, :]
                flow[c, t, 12:16, :] = field[k, 0:16, :].astype(F32)[0:4]
                flow[c, t, 24:32, :] = field[k, SX - 16 : SX, :].astype(F32)[8:16]
                flow[c, t, 32:40, :] = high[KL * (2 + t) + k]
        for c, g, temperature, salinity in two_steps(
            END_LEVELS,
            END_GROUPS,
            lambda c: (END_LEVELS * i + c).astype(F32),
            lambda c, g: depth[rows_at(g), :],
            lambda c, g: (face[0, rows_at(g), :], face[1, rows_at(g), :]),
            flow,
            coef,
            q0,
            q1,
        ):
            if g < 32:
                rows = rows_at(0 if g == 8 else 8)
                new[0, END_LEVELS * i + c, rows, :] = temperature
                new[1, END_LEVELS * i + c, rows, :] = salinity
            total[rows_at(g), :] += temperature - 0.8 * salinity
        return carry

    lax.fori_loop(0, KL // END_LEVELS, some_levels, 0)


def late_levels(tracers, east, north, levels, low, high):
    return pl.pallas_call(
        late_kernel,
        out_shape=[
            pltpu.VMEM((2, KL - EARLY, SX, SY), F32),
            pltpu.VMEM((ROWS, 128), F32),
            pltpu.VMEM((2, KL, 16, SY), F32),
            pltpu.VMEM((END_ROWS, 128), F32),
        ],
        scratch_shapes=level_scratch(ROWS, LEVELS) + level_scratch(END_ROWS, END_LEVELS),
        compiler_params=params(),
        cost_estimate=pl.CostEstimate(flops=5_000_000, bytes_accessed=6_000_000, transcendentals=0),
        name="late_levels",
    )(tracers, east, north, levels, low, high)


def operator_kernel(
    levels, low, high, own_rows, own_edges, first_pair, second_pair, early, early_total,
    late, late_total, ends, ends_total,
    new, fields, sums,
    depth, q0, q1, strip_depth, strip_face, strip_flow, strip_total, first_q, coef, wall, total, field, grid, staged, sems,
    *, count,
):
    lane = lanes()
    member = lane % 8
    blank = jnp.zeros((8, 128), F32)
    strip_level = (lane // 8).astype(F32)
    first = lax.axis_index("gy") == 0
    last = lax.axis_index("gy") == count - 1

    def own(which, a, g):
        r = g - LOW
        if r < EDGE:
            return own_edges[which, a, rows_at(0), :]
        if r >= WIDE - EDGE:
            return own_edges[which, a, rows_at(8), :]
        return own_rows[which, a, rows_at(r - EDGE), :]

    even = is_even("gy")

    def sent(g):
        rows = rows_at(g - LOW)
        pairs = [(first_pair[a, rows, :], second_pair[a, rows, :]) for a in range(SENT)]
        return [jnp.where(even, b, a) for a, b in pairs], [jnp.where(even, a, b) for a, b in pairs]

    halo_depth(levels, low, high, depth)
    parts = {}
    for g in GROUPS:
        from_low, from_high = sent(g)
        parts[g] = list(split_one(*from_low)), list(split_two(*from_high))
    for g in GROUPS:
        rows = rows_at(g)
        from_low, from_high = parts[g]
        from_low[4] = jnp.where(first, 0.0, from_low[4])
        from_high[4] = jnp.where(last, 0.0, from_high[4])
        for a in range(5):
            low_strip = jnp.where(member < 4, from_low[a], own(0, a, g))
            high_strip = jnp.where(member >= 3, from_high[a], own(1, a, g))
            for side, value in enumerate((low_strip, high_strip)):
                if a < 2:
                    q0[side, a, rows, :] = value
                elif a < 4:
                    strip_flow[side, a - 2, rows, :] = value
                else:
                    strip_depth[side, rows, :] = value
    for outside in OUTSIDE:
        for side in range(2):
            strip_depth[side, rows_at(outside), :] = blank

    ahead = {
        (side, g): ahead_one(strip_depth[side, rows_at(g), :]) for side in range(2) for g in GROUPS
    }
    for (side, g), value in ahead.items():
        strip_face[side, rows_at(g), :] = jnp.minimum(strip_depth[side, rows_at(g), :], value)

    for side in range(2):
        for i in range(2):
            coef[side, i, rows_at(LOW - 8), :] = blank

    def first_row(side, g, b_south, *behind):
        if side == 0:
            return b_south, *behind
        face = jnp.minimum(own(0, 4, g), own(1, 4, g))
        a_first, b_first = face_weights(face, own(0, 3, g), strip_level)
        return (
            jnp.where(member == 0, b_first, b_south),
            *(jnp.where(member == 0, a_first * own(0, t, g), behind[t]) for t in range(2)),
        )

    for side, g, temperature, salinity in two_steps(
        2,
        GROUPS,
        lambda side: strip_level,
        lambda side, g: strip_depth[side, rows_at(g), :],
        lambda side, g: (
            jnp.minimum(strip_depth[side, rows_at(g), :], strip_depth[side, rows_at(g + 1), :]),
            strip_face[side, rows_at(g), :],
        ),
        strip_flow,
        coef,
        q0,
        q1,
        first_row,
    ):
        rows = rows_at(g)
        q0[side, 0, rows, :] = temperature
        q0[side, 1, rows, :] = salinity
        strip_total[side, rows, :] = temperature - 0.8 * salinity
    for turn in (8, 16, 32, 64):
        values = {}
        for side in range(2):
            for g in GROUPS:
                value = strip_total[side, rows_at(g), :]
                values[side, g] = value + pltpu.roll(value, turn, 1)
        for (side, g), value in values.items():
            strip_total[side, rows_at(g), :] = value

    for tracer in range(2):
        high_values = {g: back_one(q0[1, tracer, rows_at(g), :]) for g in INNER}
        for g in INNER:
            rows = rows_at(g)
            first_q[tracer, rows, :] = jnp.where(member >= 4, q0[0, tracer, rows, :], high_values[g])
    from_strip = (lane < 2) | (lane >= 126)
    row = lax.broadcasted_iota(jnp.int32, (8, 128), 0)

    def place(blocked, first_level):
        slots = [(t, first_level + c, c, g) for c in range(PLACED) for t in range(2) for g in range(0, SX, 8)]
        turned = {
            (t, c, g): pltpu.roll(first_q[t, rows_at(g + PAD), :], 124 - 8 * k, 1) for t, k, c, g in slots
        }
        for t, k, c, g in slots:
            rows = rows_at(g)
            here = blocked[t, c, rows, :]
            if g == 0:
                here = jnp.where(row < 2, ends[t, k, rows_at(4), :], here)
            elif g == SX - 8:
                here = jnp.where(row >= 6, ends[t, k, rows_at(8), :], here)
            staged[t, k, rows, :] = jnp.where(from_strip, turned[t, c, g], here)
        at = slice(first_level, first_level + PLACED)
        for t in range(2):
            pltpu.make_async_copy(staged.at[t, at], new.at[t, at], sems.at[0]).start()

    for first_level in range(0, KL, PLACED):
        for start, blocked in ((0, early), (EARLY, late)):
            if start <= first_level < (EARLY if start == 0 else KL):
                place(blocked.at[:, first_level - start : first_level - start + PLACED], first_level)

    def beside(low_value, high_value):
        return jnp.where(lane >= 64, pltpu.roll(low_value, 4, 1), pltpu.roll(high_value, 5, 1))

    def northward(main, side):
        a, b = ahead_one(main), ahead_one(side)
        return jnp.where(lane == 127, b, a), jnp.where(lane == 127, a, b)

    def southward(main, side):
        a, b = back_one(main), back_one(side)
        return jnp.where(lane == 0, b, a), jnp.where(lane == 0, a, b)

    for g in GROUPS:
        wall[rows_at(g), :] = early_total[rows_at(g), :] + late_total[rows_at(g), :]
    wall[PAD - 2 : PAD + 2, :] = ends_total[10:14, :]
    wall[PAD + SX - 2 : PAD + SX + 3, :] = ends_total[30:35, :]
    for g in GROUPS + OUTSIDE:
        rows = rows_at(g)
        grid[0, 0, rows, :] = depth[rows, :]
        grid[0, 1, rows, :] = beside(strip_depth[0, rows, :], strip_depth[1, rows, :])
    further_all = {g: northward(grid[0, 0, rows_at(g), :], grid[0, 1, rows_at(g), :]) for g in GROUPS}
    strip_sums = {
        g: (pltpu.roll(strip_total[0, rows_at(g), :], 4, 1), pltpu.roll(strip_total[1, rows_at(g), :], 5, 1))
        for g in GROUPS
    }
    for g in GROUPS:
        rows = rows_at(g)
        both = grid[0, 0, rows, :], grid[0, 1, rows, :]
        further = further_all[g]
        for part in range(2):
            grid[1, part, rows, :] = jnp.minimum(both[part], grid[0, part, rows_at(g + 1), :])
            grid[2, part, rows, :] = jnp.minimum(both[part], further[part])
        low_total, high_total = strip_sums[g]
        edge_total = jnp.where(lane < 64, low_total, high_total)
        total[0, rows, :] = jnp.where(from_strip, edge_total, wall[rows, :])
        total[1, rows, :] = jnp.where(lane >= 64, low_total, high_total)
    for part in range(2):
        grid[1, part, rows_at(LOW - 8), :] = blank
        for outside in OUTSIDE:
            for i in range(3):
                field[i, part, rows_at(outside), :] = blank
    scale = 1.0 / KL
    south_faces = {g: southward(grid[2, 0, rows_at(g), :], grid[2, 1, rows_at(g), :]) for g in GROUPS}
    for g in GROUPS:
        rows = rows_at(g)
        souths = south_faces[g]
        for part in range(2):
            grid[6, part, rows, :] = souths[part]
            here = grid[0, part, rows, :]
            own_part = ALPHA * scale * here + jnp.where(here == 0.0, 1.0, 0.0)
            faces = grid[1, part, rows, :] + grid[1, part, rows_at(g - 1), :] + grid[2, part, rows, :] + souths[part]
            diagonal = own_part + scale * faces
            inverse = 1.0 / diagonal
            grid[3, part, rows, :] = inverse
            grid[4, part, rows, :] = own_part
            grid[5, part, rows, :] = diagonal
            field[0, part, rows, :] = 0.25 * total[part, rows, :] * inverse

    moments = [blank] * 6
    for i in range(3):
        groups = GROUPS if i < 2 else INNER
        pairs = {g: (field[i, 0, rows_at(g), :], field[i, 1, rows_at(g), :]) for g in groups}
        all_norths = {g: northward(*pairs[g]) for g in groups}
        all_souths = {g: southward(*pairs[g]) for g in groups} if i < 2 else {}
        for g in groups:
            rows = rows_at(g)
            both = pairs[g]
            norths = all_norths[g]
            for part in range(2):
                if i == 2 and part == 1:
                    continue
                here = both[part]
                east_gap = here - field[i, part, rows_at(g + 1), :]
                north_gap = here - norths[part]
                east_face = scale * grid[1, part, rows, :]
                north_face = scale * grid[2, part, rows, :]
                own_part = grid[4, part, rows, :]
                if part == 0 and PAD <= g < PAD + SX:
                    moments[2 * i] += grid[5, 0, rows, :] * here * here
                    moments[2 * i + 1] += (
                        own_part * here * here + east_face * east_gap * east_gap + north_face * north_gap * north_gap
                    )
                if i < 2:
                    image = (
                        own_part * here
                        + east_face * east_gap
                        + scale * grid[1, part, rows_at(g - 1), :] * (here - field[i, part, rows_at(g - 1), :])
                        + north_face * north_gap
                        + scale * grid[6, part, rows, :] * (here - all_souths[g][part])
                    )
                    field[i + 1, part, rows, :] = image * grid[3, part, rows, :]
        fields[i] = field[i, 0, PAD : PAD + SX, :]
    sums_row = jnp.zeros((8, 128), F32)
    for i in range(6):
        value = jnp.sum(jnp.sum(moments[i], axis=0, keepdims=True), axis=1, keepdims=True)
        sums_row = jnp.where(lane == i, value, sums_row)
    for g in range(0, 128, 8):
        sums[rows_at(g), :] = sums_row
    pltpu.make_async_copy(staged, new, sems.at[0]).wait()


def operator(*arrays, count):
    tall = (ROWS, 128)
    scratch = (
        (),
        (2, 2),
        (2, 2),
        (2,),
        (2,),
        (2, 2),
        (2,),
        (2,),
        (2, 5),
        (),
        (2,),
        (3, 2),
        (7, 2),
    )
    return pl.pallas_call(
        functools.partial(operator_kernel, count=count),
        out_shape=[
            jax.ShapeDtypeStruct((2, KL, SX, SY), F32),
            pltpu.VMEM((3, SX, SY), F32),
            jax.ShapeDtypeStruct((128, 128), F32),
        ],
        out_specs=[
            pl.BlockSpec(memory_space=pltpu.HBM),
            pl.BlockSpec(memory_space=pltpu.VMEM),
            pl.BlockSpec(memory_space=pltpu.VMEM),
        ],
        scratch_shapes=[pltpu.VMEM(s + tall, F32) for s in scratch]
        + [pltpu.VMEM((2, KL, SX, SY), F32), pltpu.SemaphoreType.DMA((2,))],
        compiler_params=params(),
        name="operator",
    )(*arrays)


def finish_kernel(sums, fields, out):
    value = sums[0:8, :]
    for g in range(8, 128, 8):
        value = value + sums[rows_at(g), :]
    value = jnp.sum(value, axis=0, keepdims=True)
    lane = lanes((1, 128))
    m0, m1, m2, m3, m4, m5 = (
        jnp.sum(jnp.where(lane == i, value, 0.0), axis=1, keepdims=True) for i in range(6)
    )
    floor = 4e-7
    l10 = m2 / m1
    l20 = m3 / m1
    d1 = m3 - l10 * m2
    t = m4 - l20 * m2
    has1 = d1 > floor * m3
    l21 = jnp.where(has1, t / d1, 0.0)
    d2 = m5 - l20 * m3 - l21 * t
    has2 = has1 & (d2 > floor * m5)
    y1 = m1 - l10 * m0
    y2 = m2 - l20 * m0 - l21 * y1
    c2 = jnp.where(has2, y2 / d2, 0.0)
    c1 = jnp.where(has1, y1 / d1, 0.0) - l21 * c2
    c0 = m0 / m1 - l10 * c1 - l20 * c2
    for g in range(0, SX, 8):
        rows = rows_at(g)
        out[rows, :] = c0 * fields[0, rows, :] + c1 * fields[1, rows, :] + c2 * fields[2, rows, :]


def finish(sums, fields):
    return pl.pallas_call(
        finish_kernel,
        out_shape=jax.ShapeDtypeStruct((SX, SY), F32),
        name="finish",
    )(*(pltpu.with_memory_space_constraint(x, pltpu.VMEM) for x in (sums, fields)))


def first_pairs(array, axis):
    return lax.ppermute(array, axis, [(i, i ^ 1) for i in range(lax.axis_size(axis))])


def second_pairs(array, axis, around):
    count = lax.axis_size(axis)
    pairs = [] if around else [(0, 0), (count - 1, count - 1)]
    for i in range(1, count if around else count - 1, 2):
        pairs += [(i, (i + 1) % count), ((i + 1) % count, i)]
    return lax.ppermute(array, axis, pairs)


def on_device(tracers, east, north, levels):
    to_first, to_second = edges(tracers, east, north, levels)
    second = second_pairs(to_second, "gx", True)
    first = first_pairs(to_first, "gx")
    own_rows, one, two, early, early_total = block(tracers, east, north, levels, to_first)
    own_edges, one, two, low, high = pack_edges(first, second, one, two)
    second = second_pairs(two, "gy", False)
    first = first_pairs(one, "gy")
    later = late_levels(tracers, east, north, levels, low, high)
    new, fields, sums = operator(
        levels, low, high, own_rows, own_edges, first, second, early, early_total, *later, count=lax.axis_size("gy")
    )
    sums = lax.all_to_all(sums, ("gx", "gy"), split_axis=0, concat_axis=0, tiled=True)
    return new, finish(sums, fields)


def solution(mesh):
    placed = (P(None, None, "gx", "gy"), P(None, "gx", "gy"), P(None, "gx", "gy"), P("gx", "gy"))
    return jax.shard_map(
        on_device,
        mesh=mesh,
        in_specs=placed,
        out_specs=(P(None, None, "gx", "gy"), P("gx", "gy")),
        check_vma=False,
    )
```

```python
import functools

import jax
import jax.numpy as jnp
from jax import lax
from jax.experimental import pallas as pl
from jax.experimental.pallas import tpu as pltpu
from jax.sharding import PartitionSpec as P

KAPPA = 0.08
ALPHA = 0.05
F32 = jnp.float32

SX = 128
SY = 128
KL = 16
EDGE = 8
PAD = 16
ROWS = SX + 2 * PAD
WIDE = SX + 2 * EDGE
LOW = PAD - EDGE
ARRAYS = 2 * KL + 2 * KL + 1
VMEM = 40 * 1024 * 1024
GROUPS = tuple(range(LOW, LOW + WIDE, 8))
OUTSIDE = (LOW - 8, LOW + WIDE)
INNER = GROUPS[1:-1]
END_GROUPS = (8, 24, 32)
END_ROWS = 48
SENT = 3


def params():
    return pltpu.CompilerParams(vmem_limit_bytes=VMEM)


def is_even(axis):
    return lax.rem(lax.axis_index(axis), 2) == 0


def rows_at(row):
    return slice(row, row + 8)


def lanes(shape=(8, 128)):
    return lax.broadcasted_iota(jnp.int32, shape, len(shape) - 1)


def ahead_one(value):
    return pltpu.roll(value, 127, 1)


def back_one(value):
    return pltpu.roll(value, 1, 1)


def offsets(counts):
    starts, at = [], 8
    for a in range(4):
        starts.append(at)
        at += KL * counts[a]
    return starts, at


NEXT = (4, 4, 4, 4)
BEFORE = (5, 5, 4, 4)
NEXT_AT, NEXT_ROWS = offsets(NEXT)
BEFORE_AT, BEFORE_ROWS = offsets(BEFORE)
BEFORE_ROWS += 8
assert NEXT_ROWS <= BEFORE_ROWS


def edges_kernel(t, e, n, d, first_pair, second_pair, tiles, flows, depths, sems):
    copies = []
    for side, at in enumerate((0, SX - 8)):
        at16 = 0 if side == 0 else SX - 16
        copies += [
            (t.at[0, :, at : at + 8, :], tiles.at[side, 0]),
            (t.at[1, :, at : at + 8, :], tiles.at[side, 1]),
            (e.at[:, at16 : at16 + 16, :], flows.at[side, 0]),
            (n.at[:, at16 : at16 + 16, :], flows.at[side, 1]),
            (d.at[at : at + 8, :], depths.at[side]),
        ]
    copies = [pltpu.make_async_copy(src, dst, sems.at[i]) for i, (src, dst) in enumerate(copies)]
    for copy in copies:
        copy.start()
    for copy in copies:
        copy.wait()

    def write(before, after):
        for side, (out, starts, counts) in enumerate(((before, BEFORE_AT, BEFORE), (after, NEXT_AT, NEXT))):
            out[0:8, :] = depths[side].astype(F32)
            for a in range(4):
                for k in range(KL):
                    value = tiles[side, a, k] if a < 2 else flows[side, a - 2, k].astype(F32)[8 * side : 8 * side + 8]
                    from_row = 0 if side == 0 else 8 - counts[a]
                    at = starts[a] + counts[a] * k
                    out[at : at + counts[a], :] = value[from_row : from_row + counts[a]]
        before[BEFORE_ROWS - 8 : BEFORE_ROWS, :] = jnp.zeros((8, 128), F32)
        after[NEXT_ROWS:BEFORE_ROWS, :] = jnp.zeros((BEFORE_ROWS - NEXT_ROWS, 128), F32)

    @pl.when(is_even("gx"))
    def _():
        write(second_pair, first_pair)

    @pl.when(~is_even("gx"))
    def _():
        write(first_pair, second_pair)


def edges(tracers, east, north, levels):
    return pl.pallas_call(
        edges_kernel,
        in_specs=[pl.BlockSpec(memory_space=pltpu.HBM)] * 4,
        out_shape=[pltpu.VMEM((BEFORE_ROWS, SY), F32)] * 2,
        scratch_shapes=[
            pltpu.VMEM((2, 2, KL, 8, SY), F32),
            pltpu.VMEM((2, 2, KL, 16, SY), jnp.bfloat16),
            pltpu.VMEM((2, 8, SY), jnp.int32),
            pltpu.SemaphoreType.DMA((10,)),
        ],
        compiler_params=params(),
        name="edges",
    )(*(pltpu.with_memory_space_constraint(x, pltpu.HBM) for x in (tracers, east, north, levels)))


def low_tile(ref, a, k):
    if a == 4:
        return ref[0:8, :]
    at = NEXT_AT[a] + NEXT[a] * (k + 1) - 8
    return ref[at : at + 8, :]


def high_tile(ref, a, k):
    if a == 4:
        return ref[0:8, :]
    at = BEFORE_AT[a] + BEFORE[a] * k
    return ref[at : at + 8, :]


def pack(source, rows, last):
    group = lanes((rows, 128)) // 8
    one = jnp.zeros((rows, 128), F32)
    beyond = jnp.zeros((rows, 128), F32)
    for k in range(KL):
        value = source(k)
        one = jnp.where(group == k, pltpu.roll(value, (8 * k - 124) % 128, 1), one)
        if last:
            beyond = jnp.where(group == k, pltpu.roll(value, (8 * k + 3) % 128, 1), beyond)
    two = pltpu.roll(one, 127, 1)
    if last:
        two = jnp.where(lanes((rows, 128)) % 8 == 7, beyond, two)
    return one, two


def pack_depth(sources):
    lane = lanes(sources[0].shape)
    values = [pltpu.roll(x, turn, 1) for turn in (4, 3) for x in sources]
    values = [jnp.where(lane < 8, x, 0.0) for x in values]
    for turn in (8, 16, 32, 64):
        values = [x + pltpu.roll(x, turn, 1) for x in values]
    return list(zip(values[: len(sources)], values[len(sources) :], strict=True))


def merge_one(t0, t1, e, n, d):
    member = lanes(t0.shape) % 8
    return (
        jnp.where(member < 4, t0, pltpu.roll(n, 4, 1)),
        jnp.where(member < 4, t1, pltpu.roll(e, 4, 1)),
        d,
    )


def split_one(a, b, c):
    return a, b, pltpu.roll(b, 124, 1), pltpu.roll(a, 124, 1), c


def merge_two(t0, t1, e, n, d):
    member = lanes(t0.shape) % 8
    return (
        jnp.where(member < 3, pltpu.roll(d, 125, 1), t0),
        jnp.where(member < 2, pltpu.roll(d, 122, 1), t1),
        jnp.where((member >= 3) & (member < 7), n, pltpu.roll(e, 4, 1)),
    )


def split_two(a, b, c):
    member = lanes(a.shape) % 8
    depth = jnp.where(member < 6, pltpu.roll(a, 3, 1), pltpu.roll(b, 6, 1))
    return a, b, pltpu.roll(c, 124, 1), c, depth


def pack_all(sources, depths, rows, own, own_rows, first_pair, second_pair, sent_rows):
    packed = [pack(source, rows, a < 2) for a, source in enumerate(sources)] + [depths]
    for which in range(2):
        for a in range(5):
            own[which, a, own_rows, :] = packed[a][which]
    even = is_even("gy")
    ones = merge_one(*(p[0] for p in packed))
    twos = merge_two(*(p[1] for p in packed))
    for a in range(SENT):
        first_pair[a, sent_rows, :] = jnp.where(even, ones[a], twos[a])
        second_pair[a, sent_rows, :] = jnp.where(even, twos[a], ones[a])


def pack_block(t, e, n, d, own, one, two):
    chunk = 32
    groups = range(0, SX, 8)
    for g, pair in zip(groups, pack_depth([d[rows_at(g), :].astype(F32) for g in groups]), strict=True):
        for which in range(2):
            own[which, 4, rows_at(g), :] = pair[which]

    def body(i, carry):
        rows = pl.ds(pl.multiple_of(i * chunk, chunk), chunk)
        sources = (
            lambda k: t[0, k, rows, :],
            lambda k: t[1, k, rows, :],
            lambda k: e[k, rows, :].astype(F32),
            lambda k: n[k, rows, :].astype(F32),
        )
        depths = own[0, 4, rows, :], own[1, 4, rows, :]
        pack_all(sources, depths, chunk, own, rows, one, two, rows)
        return carry

    lax.fori_loop(0, SX // chunk, body, 0)


def pack_edges_kernel(first_pair, second_pair, first_rows, second_rows, own, one, two, low, high, low_in, high_in):
    for g in range(0, SX, 8):
        for a in range(SENT):
            one[a, rows_at(g + EDGE), :] = first_rows[a, rows_at(g), :]
            two[a, rows_at(g + EDGE), :] = second_rows[a, rows_at(g), :]
    even = is_even("gx")
    for at in range(0, BEFORE_ROWS, 8):
        rows = rows_at(at)
        value, other = first_pair[rows, :], second_pair[rows, :]
        low_in[rows, :] = jnp.where(even, other, value)
        high_in[rows, :] = jnp.where(even, value, other)
    for a in range(5):
        for k in range(KL if a < 4 else 1):
            low[KL * a + k] = low_tile(low_in, a, k)
            high[KL * a + k] = high_tile(high_in, a, k)
    depths = pack_depth([low_tile(low_in, 4, 0), high_tile(high_in, 4, 0)])
    for side, (ref, tile) in enumerate(((low_in, low_tile), (high_in, high_tile))):
        sources = [functools.partial(tile, ref, a) for a in range(4)]
        at = 0 if side == 0 else WIDE - EDGE
        pack_all(sources, depths[side], 8, own, rows_at(8 * side), one, two, rows_at(at))


def pack_edges(first, second, first_rows, second_rows):
    sent = jax.ShapeDtypeStruct((SENT, WIDE, 128), F32)
    halo = jax.ShapeDtypeStruct((ARRAYS, EDGE, SY), F32)
    return pl.pallas_call(
        pack_edges_kernel,
        out_shape=[jax.ShapeDtypeStruct((2, 5, 2 * EDGE, 128), F32), sent, sent, halo, halo],
        scratch_shapes=[pltpu.VMEM((BEFORE_ROWS, SY), F32)] * 2,
        compiler_params=params(),
        name="pack_edges",
    )(first, second, first_rows, second_rows)


def face_weights(face, flow_value, threshold):
    is_open = face > threshold
    ahead = jnp.where(is_open, KAPPA + jnp.maximum(flow_value, 0.0), 0.0)
    back = jnp.where(is_open, KAPPA - jnp.minimum(flow_value, 0.0), 0.0)
    return ahead, back


def two_steps(copies, groups, threshold, depth_at, faces, flow, coef, q0, q1, first_row=None):
    parts = [(c, g) for c in range(copies) for g in groups]
    every = [(c, t, g) for c, g in parts for t in range(2)]
    for c, g in parts:
        rows = rows_at(g)
        east, north = faces(c, g)
        coef[c, 0, rows, :], coef[c, 1, rows, :] = face_weights(east, flow[c, 0, rows, :], threshold(c))
        coef[c, 3, rows, :], coef[c, 2, rows, :] = face_weights(north, flow[c, 1, rows, :], threshold(c))
    b_south = {(c, g): back_one(coef[c, 2, rows_at(g), :]) for c, g in parts}

    def shifted(source):
        ahead = {(c, t, g): ahead_one(source[c, t, rows_at(g), :]) for c, t, g in every}
        behind = {
            (c, t, g): back_one(coef[c, 3, rows_at(g), :] * source[c, t, rows_at(g), :]) for c, t, g in every
        }
        return ahead, behind

    def combine(source, c, t, g, ahead, behind):
        rows = rows_at(g)
        return (
            coef[c, 4, rows, :] * source[c, t, rows, :]
            + coef[c, 1, rows, :] * source[c, t, rows_at(g + 1), :]
            + coef[c, 0, rows_at(g - 1), :] * source[c, t, rows_at(g - 1), :]
            + coef[c, 2, rows, :] * ahead
            + behind
        )

    ahead, behind = shifted(q0)
    for c, g in parts:
        rows = rows_at(g)
        b_here = b_south[c, g]
        if first_row is not None:
            b_here, behind[c, 0, g], behind[c, 1, g] = first_row(c, g, b_here, behind[c, 0, g], behind[c, 1, g])
        leaving = coef[c, 0, rows, :] + coef[c, 3, rows, :] + coef[c, 1, rows_at(g - 1), :] + b_here
        coef[c, 4, rows, :] = jnp.where(depth_at(c, g) > threshold(c), 1.0 - leaving, 0.0)
        for t in range(2):
            q1[c, t, rows, :] = combine(q0, c, t, g, ahead[c, t, g], behind[c, t, g])
    ahead, behind = shifted(q1)
    for c, g in parts:
        yield c, g, *(combine(q1, c, t, g, ahead[c, t, g], behind[c, t, g]) for t in range(2))


def halo_depth(levels, low, high, depth):
    for g in GROUPS:
        r = g - LOW
        if r < EDGE:
            value = low[4 * KL]
        elif r >= WIDE - EDGE:
            value = high[4 * KL]
        else:
            value = levels[rows_at(r - EDGE), :].astype(F32)
        depth[rows_at(g), :] = value
    for outside in OUTSIDE:
        depth[rows_at(outside), :] = jnp.zeros((8, 128), F32)


LEVELS = 2
END_LEVELS = 4
PLACED = 8
EARLY = 8


def set_faces(groups, depth, face):
    lane = lanes()
    ahead = {g: ahead_one(depth[rows_at(g), :]) for g in groups}
    for g in groups:
        rows = rows_at(g)
        here = depth[rows, :]
        face[0, rows, :] = jnp.minimum(here, depth[rows_at(g + 1), :])
        face[1, rows, :] = jnp.where(lane == 127, 0.0, jnp.minimum(here, ahead[g]))


def inner_levels(from_level, to_level, tracers, east, north, levels, new, total, depth, face, q0, q1, flow, coef):
    blank = jnp.zeros((8, 128), F32)
    for g in INNER:
        depth[rows_at(g), :] = levels[rows_at(g - PAD), :].astype(F32)
        total[rows_at(g), :] = blank
    for g in (GROUPS[0], GROUPS[-1]):
        depth[rows_at(g), :] = blank
        total[rows_at(g), :] = blank
        for c in range(LEVELS):
            for i in range(2):
                coef[c, i, rows_at(g), :] = blank
                q0[c, i, rows_at(g), :] = blank
                q1[c, i, rows_at(g), :] = blank
    set_faces(INNER, depth, face)

    def some_levels(i, carry):
        for c in range(LEVELS):
            k = from_level + LEVELS * i + c
            for t in range(2):
                q0[c, t, PAD : PAD + SX, :] = tracers[t, k]
            flow[c, 0, PAD : PAD + SX, :] = east[k].astype(F32)
            flow[c, 1, PAD : PAD + SX, :] = north[k].astype(F32)
        for c, g, temperature, salinity in two_steps(
            LEVELS,
            INNER,
            lambda c: (from_level + LEVELS * i + c).astype(F32),
            lambda c, g: depth[rows_at(g), :],
            lambda c, g: (face[0, rows_at(g), :], face[1, rows_at(g), :]),
            flow,
            coef,
            q0,
            q1,
        ):
            new[0, LEVELS * i + c, rows_at(g - PAD), :] = temperature
            new[1, LEVELS * i + c, rows_at(g - PAD), :] = salinity
            total[rows_at(g), :] += temperature - 0.8 * salinity
        return carry

    lax.fori_loop(0, (to_level - from_level) // LEVELS, some_levels, 0)


def block_kernel(tracers, east, north, levels, after, own, first_pair, second_pair, *rest):
    del after
    pack_block(tracers, east, north, levels, own, first_pair, second_pair)
    inner_levels(0, EARLY, tracers, east, north, levels, *rest)


def level_scratch(rows, copies):
    shapes = ((), (2,), (copies, 2), (copies, 2), (copies, 2), (copies, 5))
    return [pltpu.VMEM(shape + (rows, 128), F32) for shape in shapes]


def block(tracers, east, north, levels, after):
    sent = pltpu.VMEM((SENT, SX, 128), F32)
    return pl.pallas_call(
        block_kernel,
        in_specs=[pl.BlockSpec(memory_space=pltpu.VMEM)] * 4 + [pl.BlockSpec(memory_space=pl.ANY)],
        out_shape=[
            pltpu.VMEM((2, 5, SX, 128), F32),
            sent,
            sent,
            pltpu.VMEM((2, EARLY, SX, SY), F32),
            pltpu.VMEM((ROWS, 128), F32),
        ],
        scratch_shapes=level_scratch(ROWS, LEVELS),
        compiler_params=params(),
        cost_estimate=pl.CostEstimate(flops=20_000_000, bytes_accessed=24_000_000, transcendentals=0),
        name="block",
    )(tracers, east, north, levels, after)


def late_kernel(tracers, east, north, levels, low, high, new, total, ends_new, ends_total, *scratch):
    ends(tracers, east, north, levels, low, high, ends_new, ends_total, *scratch[6:])
    inner_levels(EARLY, KL, tracers, east, north, levels, new, total, *scratch[:6])


def ends(tracers, east, north, levels, low, high, new, total, depth, face, q0, q1, flow, coef):
    blank = jnp.zeros((8, 128), F32)
    for g in range(0, END_ROWS, 8):
        rows = rows_at(g)
        depth[rows, :] = blank
        total[rows, :] = blank
        if g not in END_GROUPS:
            for c in range(END_LEVELS):
                for i in range(2):
                    coef[c, i, rows, :] = blank
                    q0[c, i, rows, :] = blank
                    q1[c, i, rows, :] = blank
    depth[8:12, :] = low[4 * KL, 4:8, :]
    depth[12:16, :] = levels[0:8, :].astype(F32)[0:4]
    depth[24:32, :] = levels[SX - 8 : SX, :].astype(F32)
    depth[32:40, :] = high[4 * KL]
    set_faces(END_GROUPS, depth, face)

    def some_levels(i, carry):
        for c in range(END_LEVELS):
            k = END_LEVELS * i + c
            for t in range(2):
                q0[c, t, 8:12, :] = low[KL * t + k, 4:8, :]
                q0[c, t, 12:16, :] = tracers[t, k, 0:4, :]
                q0[c, t, 24:32, :] = tracers[t, k, SX - 8 : SX, :]
                q0[c, t, 32:40, :] = high[KL * t + k]
            for t, field in enumerate((east, north)):
                flow[c, t, 8:12, :] = low[KL * (2 + t) + k, 4:8, :]
                flow[c, t, 12:16, :] = field[k, 0:16, :].astype(F32)[0:4]
                flow[c, t, 24:32, :] = field[k, SX - 16 : SX, :].astype(F32)[8:16]
                flow[c, t, 32:40, :] = high[KL * (2 + t) + k]
        for c, g, temperature, salinity in two_steps(
            END_LEVELS,
            END_GROUPS,
            lambda c: (END_LEVELS * i + c).astype(F32),
            lambda c, g: depth[rows_at(g), :],
            lambda c, g: (face[0, rows_at(g), :], face[1, rows_at(g), :]),
            flow,
            coef,
            q0,
            q1,
        ):
            if g < 32:
                rows = rows_at(0 if g == 8 else 8)
                new[0, END_LEVELS * i + c, rows, :] = temperature
                new[1, END_LEVELS * i + c, rows, :] = salinity
            total[rows_at(g), :] += temperature - 0.8 * salinity
        return carry

    lax.fori_loop(0, KL // END_LEVELS, some_levels, 0)


def late_levels(tracers, east, north, levels, low, high):
    return pl.pallas_call(
        late_kernel,
        out_shape=[
            pltpu.VMEM((2, KL - EARLY, SX, SY), F32),
            pltpu.VMEM((ROWS, 128), F32),
            pltpu.VMEM((2, KL, 16, SY), F32),
            pltpu.VMEM((END_ROWS, 128), F32),
        ],
        scratch_shapes=level_scratch(ROWS, LEVELS) + level_scratch(END_ROWS, END_LEVELS),
        compiler_params=params(),
        cost_estimate=pl.CostEstimate(flops=5_000_000, bytes_accessed=6_000_000, transcendentals=0),
        name="late_levels",
    )(tracers, east, north, levels, low, high)


def operator_kernel(
    levels, low, high, own_rows, own_edges, first_pair, second_pair, early_total, late_total, ends_total,
    from_strips, fields, sums,
    depth, q0, q1, strip_depth, strip_face, strip_flow, strip_total, coef, wall, total, field, grid, *, count,
):
    lane = lanes()
    member = lane % 8
    blank = jnp.zeros((8, 128), F32)
    strip_level = (lane // 8).astype(F32)
    first = lax.axis_index("gy") == 0
    last = lax.axis_index("gy") == count - 1

    def own(which, a, g):
        r = g - LOW
        if r < EDGE:
            return own_edges[which, a, rows_at(0), :]
        if r >= WIDE - EDGE:
            return own_edges[which, a, rows_at(8), :]
        return own_rows[which, a, rows_at(r - EDGE), :]

    even = is_even("gy")

    def sent(g):
        rows = rows_at(g - LOW)
        pairs = [(first_pair[a, rows, :], second_pair[a, rows, :]) for a in range(SENT)]
        return [jnp.where(even, b, a) for a, b in pairs], [jnp.where(even, a, b) for a, b in pairs]

    halo_depth(levels, low, high, depth)
    parts = {}
    for g in GROUPS:
        from_low, from_high = sent(g)
        parts[g] = list(split_one(*from_low)), list(split_two(*from_high))
    for g in GROUPS:
        rows = rows_at(g)
        from_low, from_high = parts[g]
        from_low[4] = jnp.where(first, 0.0, from_low[4])
        from_high[4] = jnp.where(last, 0.0, from_high[4])
        for a in range(5):
            low_strip = jnp.where(member < 4, from_low[a], own(0, a, g))
            high_strip = jnp.where(member >= 3, from_high[a], own(1, a, g))
            for side, value in enumerate((low_strip, high_strip)):
                if a < 2:
                    q0[side, a, rows, :] = value
                elif a < 4:
                    strip_flow[side, a - 2, rows, :] = value
                else:
                    strip_depth[side, rows, :] = value
    for outside in OUTSIDE:
        for side in range(2):
            strip_depth[side, rows_at(outside), :] = blank

    ahead = {
        (side, g): ahead_one(strip_depth[side, rows_at(g), :]) for side in range(2) for g in GROUPS
    }
    for (side, g), value in ahead.items():
        strip_face[side, rows_at(g), :] = jnp.minimum(strip_depth[side, rows_at(g), :], value)

    for side in range(2):
        for i in range(2):
            coef[side, i, rows_at(LOW - 8), :] = blank

    def first_row(side, g, b_south, *behind):
        if side == 0:
            return b_south, *behind
        face = jnp.minimum(own(0, 4, g), own(1, 4, g))
        a_first, b_first = face_weights(face, own(0, 3, g), strip_level)
        return (
            jnp.where(member == 0, b_first, b_south),
            *(jnp.where(member == 0, a_first * own(0, t, g), behind[t]) for t in range(2)),
        )

    for side, g, temperature, salinity in two_steps(
        2,
        GROUPS,
        lambda side: strip_level,
        lambda side, g: strip_depth[side, rows_at(g), :],
        lambda side, g: (
            jnp.minimum(strip_depth[side, rows_at(g), :], strip_depth[side, rows_at(g + 1), :]),
            strip_face[side, rows_at(g), :],
        ),
        strip_flow,
        coef,
        q0,
        q1,
        first_row,
    ):
        rows = rows_at(g)
        q0[side, 0, rows, :] = temperature
        q0[side, 1, rows, :] = salinity
        strip_total[side, rows, :] = temperature - 0.8 * salinity
    for turn in (8, 16, 32, 64):
        values = {}
        for side in range(2):
            for g in GROUPS:
                value = strip_total[side, rows_at(g), :]
                values[side, g] = value + pltpu.roll(value, turn, 1)
        for (side, g), value in values.items():
            strip_total[side, rows_at(g), :] = value

    for tracer in range(2):
        high_values = {g: back_one(q0[1, tracer, rows_at(g), :]) for g in INNER}
        for g in INNER:
            rows = rows_at(g)
            from_strips[tracer, rows, :] = jnp.where(member >= 4, q0[0, tracer, rows, :], high_values[g])
    from_strip = (lane < 2) | (lane >= 126)

    def beside(low_value, high_value):
        return jnp.where(lane >= 64, pltpu.roll(low_value, 4, 1), pltpu.roll(high_value, 5, 1))

    def northward(main, side):
        a, b = ahead_one(main), ahead_one(side)
        return jnp.where(lane == 127, b, a), jnp.where(lane == 127, a, b)

    def southward(main, side):
        a, b = back_one(main), back_one(side)
        return jnp.where(lane == 0, b, a), jnp.where(lane == 0, a, b)

    for g in GROUPS:
        wall[rows_at(g), :] = early_total[rows_at(g), :] + late_total[rows_at(g), :]
    wall[PAD - 2 : PAD + 2, :] = ends_total[10:14, :]
    wall[PAD + SX - 2 : PAD + SX + 3, :] = ends_total[30:35, :]
    for g in GROUPS + OUTSIDE:
        rows = rows_at(g)
        grid[0, 0, rows, :] = depth[rows, :]
        grid[0, 1, rows, :] = beside(strip_depth[0, rows, :], strip_depth[1, rows, :])
    further_all = {g: northward(grid[0, 0, rows_at(g), :], grid[0, 1, rows_at(g), :]) for g in GROUPS}
    strip_sums = {
        g: (pltpu.roll(strip_total[0, rows_at(g), :], 4, 1), pltpu.roll(strip_total[1, rows_at(g), :], 5, 1))
        for g in GROUPS
    }
    for g in GROUPS:
        rows = rows_at(g)
        both = grid[0, 0, rows, :], grid[0, 1, rows, :]
        further = further_all[g]
        for part in range(2):
            grid[1, part, rows, :] = jnp.minimum(both[part], grid[0, part, rows_at(g + 1), :])
            grid[2, part, rows, :] = jnp.minimum(both[part], further[part])
        low_total, high_total = strip_sums[g]
        edge_total = jnp.where(lane < 64, low_total, high_total)
        total[0, rows, :] = jnp.where(from_strip, edge_total, wall[rows, :])
        total[1, rows, :] = jnp.where(lane >= 64, low_total, high_total)
    for part in range(2):
        grid[1, part, rows_at(LOW - 8), :] = blank
        for outside in OUTSIDE:
            for i in range(3):
                field[i, part, rows_at(outside), :] = blank
    scale = 1.0 / KL
    south_faces = {g: southward(grid[2, 0, rows_at(g), :], grid[2, 1, rows_at(g), :]) for g in GROUPS}
    for g in GROUPS:
        rows = rows_at(g)
        souths = south_faces[g]
        for part in range(2):
            grid[6, part, rows, :] = souths[part]
            here = grid[0, part, rows, :]
            own_part = ALPHA * scale * here + jnp.where(here == 0.0, 1.0, 0.0)
            faces = grid[1, part, rows, :] + grid[1, part, rows_at(g - 1), :] + grid[2, part, rows, :] + souths[part]
            diagonal = own_part + scale * faces
            inverse = 1.0 / diagonal
            grid[3, part, rows, :] = inverse
            grid[4, part, rows, :] = own_part
            grid[5, part, rows, :] = diagonal
            field[0, part, rows, :] = 0.25 * total[part, rows, :] * inverse

    moments = [blank] * 6
    for i in range(3):
        groups = GROUPS if i < 2 else INNER
        pairs = {g: (field[i, 0, rows_at(g), :], field[i, 1, rows_at(g), :]) for g in groups}
        all_norths = {g: northward(*pairs[g]) for g in groups}
        all_souths = {g: southward(*pairs[g]) for g in groups} if i < 2 else {}
        for g in groups:
            rows = rows_at(g)
            both = pairs[g]
            norths = all_norths[g]
            for part in range(2):
                if i == 2 and part == 1:
                    continue
                here = both[part]
                east_gap = here - field[i, part, rows_at(g + 1), :]
                north_gap = here - norths[part]
                east_face = scale * grid[1, part, rows, :]
                north_face = scale * grid[2, part, rows, :]
                own_part = grid[4, part, rows, :]
                if part == 0 and PAD <= g < PAD + SX:
                    moments[2 * i] += grid[5, 0, rows, :] * here * here
                    moments[2 * i + 1] += (
                        own_part * here * here + east_face * east_gap * east_gap + north_face * north_gap * north_gap
                    )
                if i < 2:
                    image = (
                        own_part * here
                        + east_face * east_gap
                        + scale * grid[1, part, rows_at(g - 1), :] * (here - field[i, part, rows_at(g - 1), :])
                        + north_face * north_gap
                        + scale * grid[6, part, rows, :] * (here - all_souths[g][part])
                    )
                    field[i + 1, part, rows, :] = image * grid[3, part, rows, :]
        fields[i] = field[i, 0, PAD : PAD + SX, :]
    sums_row = jnp.zeros((8, 128), F32)
    for i in range(6):
        value = jnp.sum(jnp.sum(moments[i], axis=0, keepdims=True), axis=1, keepdims=True)
        sums_row = jnp.where(lane == i, value, sums_row)
    for g in range(0, 128, 8):
        sums[rows_at(g), :] = sums_row


def operator(*arrays, count):
    tall = (ROWS, 128)
    scratch = (
        (),
        (2, 2),
        (2, 2),
        (2,),
        (2,),
        (2, 2),
        (2,),
        (2, 5),
        (),
        (2,),
        (3, 2),
        (7, 2),
    )
    return pl.pallas_call(
        functools.partial(operator_kernel, count=count),
        out_shape=[
            pltpu.VMEM((2,) + tall, F32),
            pltpu.VMEM((3, SX, SY), F32),
            jax.ShapeDtypeStruct((128, 128), F32),
        ],
        scratch_shapes=[pltpu.VMEM(s + tall, F32) for s in scratch],
        compiler_params=params(),
        name="operator",
    )(*arrays)


def place_kernel(early, late, ends_new, from_strips, new, staged, sem):
    lane = lanes()
    row = lax.broadcasted_iota(jnp.int32, (8, 128), 0)
    from_strip = (lane < 2) | (lane >= 126)
    for first_level in range(0, KL, PLACED):
        blocked, start = (early, 0) if first_level < EARLY else (late, EARLY)
        slots = [(t, first_level + c, g) for c in range(PLACED) for t in range(2) for g in range(0, SX, 8)]
        turned = {
            (t, k, g): pltpu.roll(from_strips[t, rows_at(g + PAD), :], 124 - 8 * k, 1) for t, k, g in slots
        }
        for t, k, g in slots:
            rows = rows_at(g)
            here = blocked[t, k - start, rows, :]
            if g == 0:
                here = jnp.where(row < 2, ends_new[t, k, rows_at(4), :], here)
            elif g == SX - 8:
                here = jnp.where(row >= 6, ends_new[t, k, rows_at(8), :], here)
            staged[t, k, rows, :] = jnp.where(from_strip, turned[t, k, g], here)
        at = slice(first_level, first_level + PLACED)
        for t in range(2):
            pltpu.make_async_copy(staged.at[t, at], new.at[t, at], sem).start()
    pltpu.make_async_copy(staged, new, sem).wait()


def place(*arrays):
    whole = (2, KL, SX, SY)
    return pl.pallas_call(
        place_kernel,
        out_shape=jax.ShapeDtypeStruct(whole, F32),
        out_specs=pl.BlockSpec(memory_space=pltpu.HBM),
        scratch_shapes=[pltpu.VMEM(whole, F32), pltpu.SemaphoreType.DMA(())],
        compiler_params=params(),
        cost_estimate=pl.CostEstimate(flops=2_000_000, bytes_accessed=6_000_000, transcendentals=0),
        name="place",
    )(*arrays)


def finish_kernel(sums, fields, out):
    value = sums[0:8, :]
    for g in range(8, 128, 8):
        value = value + sums[rows_at(g), :]
    value = jnp.sum(value, axis=0, keepdims=True)
    lane = lanes((1, 128))
    m0, m1, m2, m3, m4, m5 = (
        jnp.sum(jnp.where(lane == i, value, 0.0), axis=1, keepdims=True) for i in range(6)
    )
    floor = 4e-7
    l10 = m2 / m1
    l20 = m3 / m1
    d1 = m3 - l10 * m2
    t = m4 - l20 * m2
    has1 = d1 > floor * m3
    l21 = jnp.where(has1, t / d1, 0.0)
    d2 = m5 - l20 * m3 - l21 * t
    has2 = has1 & (d2 > floor * m5)
    y1 = m1 - l10 * m0
    y2 = m2 - l20 * m0 - l21 * y1
    c2 = jnp.where(has2, y2 / d2, 0.0)
    c1 = jnp.where(has1, y1 / d1, 0.0) - l21 * c2
    c0 = m0 / m1 - l10 * c1 - l20 * c2
    for g in range(0, SX, 8):
        rows = rows_at(g)
        out[rows, :] = c0 * fields[0, rows, :] + c1 * fields[1, rows, :] + c2 * fields[2, rows, :]


def finish(sums, fields):
    return pl.pallas_call(
        finish_kernel,
        out_shape=jax.ShapeDtypeStruct((SX, SY), F32),
        name="finish",
    )(*(pltpu.with_memory_space_constraint(x, pltpu.VMEM) for x in (sums, fields)))


def first_pairs(array, axis):
    return lax.ppermute(array, axis, [(i, i ^ 1) for i in range(lax.axis_size(axis))])


def second_pairs(array, axis, around):
    count = lax.axis_size(axis)
    pairs = [] if around else [(0, 0), (count - 1, count - 1)]
    for i in range(1, count if around else count - 1, 2):
        pairs += [(i, (i + 1) % count), ((i + 1) % count, i)]
    return lax.ppermute(array, axis, pairs)


def on_device(tracers, east, north, levels):
    to_first, to_second = edges(tracers, east, north, levels)
    second = second_pairs(to_second, "gx", True)
    first = first_pairs(to_first, "gx")
    own_rows, one, two, early, early_total = block(tracers, east, north, levels, to_first)
    own_edges, one, two, low, high = pack_edges(first, second, one, two)
    second = second_pairs(two, "gy", False)
    first = first_pairs(one, "gy")
    late, late_total, ends_new, ends_total = late_levels(tracers, east, north, levels, low, high)
    from_strips, fields, sums = operator(
        levels, low, high, own_rows, own_edges, first, second, early_total, late_total, ends_total,
        count=lax.axis_size("gy"),
    )
    sums = lax.all_to_all(sums, ("gx", "gy"), split_axis=0, concat_axis=0, tiled=True)
    new = place(early, late, ends_new, from_strips)
    return new, finish(sums, fields)


def solution(mesh):
    placed = (P(None, None, "gx", "gy"), P(None, "gx", "gy"), P(None, "gx", "gy"), P("gx", "gy"))
    return jax.shard_map(
        on_device,
        mesh=mesh,
        in_specs=placed,
        out_specs=(P(None, None, "gx", "gy"), P("gx", "gy")),
        check_vma=False,
    )
```

```python
import functools

import jax
import jax.numpy as jnp
from jax import lax
from jax.experimental import pallas as pl
from jax.experimental.pallas import tpu as pltpu
from jax.sharding import PartitionSpec as P

KAPPA = 0.08
ALPHA = 0.05
F32 = jnp.float32

SX = 128
SY = 128
KL = 16
EDGE = 8
PAD = 16
ROWS = SX + 2 * PAD
WIDE = SX + 2 * EDGE
LOW = PAD - EDGE
ARRAYS = 2 * KL + 2 * KL + 1
VMEM = 40 * 1024 * 1024
GROUPS = tuple(range(LOW, LOW + WIDE, 8))
OUTSIDE = (LOW - 8, LOW + WIDE)
INNER = GROUPS[1:-1]
END_GROUPS = (8, 24, 32)
END_ROWS = 48
SENT = 3


def params():
    return pltpu.CompilerParams(vmem_limit_bytes=VMEM)


def is_even(axis):
    return lax.rem(lax.axis_index(axis), 2) == 0


def rows_at(row):
    return slice(row, row + 8)


def lanes(shape=(8, 128)):
    return lax.broadcasted_iota(jnp.int32, shape, len(shape) - 1)


def ahead_one(value):
    return pltpu.roll(value, 127, 1)


def back_one(value):
    return pltpu.roll(value, 1, 1)


def offsets(counts):
    starts, at = [], 8
    for a in range(4):
        starts.append(at)
        at += KL * counts[a]
    return starts, at


NEXT = (4, 4, 4, 4)
BEFORE = (5, 5, 4, 4)
NEXT_AT, NEXT_ROWS = offsets(NEXT)
BEFORE_AT, BEFORE_ROWS = offsets(BEFORE)
BEFORE_ROWS += 8
assert NEXT_ROWS <= BEFORE_ROWS


def edges_kernel(t, e, n, d, first_pair, second_pair, tiles, flows, depths, sems):
    copies = []
    for side, at in enumerate((0, SX - 8)):
        at16 = 0 if side == 0 else SX - 16
        copies += [
            (t.at[0, :, at : at + 8, :], tiles.at[side, 0]),
            (t.at[1, :, at : at + 8, :], tiles.at[side, 1]),
            (e.at[:, at16 : at16 + 16, :], flows.at[side, 0]),
            (n.at[:, at16 : at16 + 16, :], flows.at[side, 1]),
            (d.at[at : at + 8, :], depths.at[side]),
        ]
    copies = [pltpu.make_async_copy(src, dst, sems.at[i]) for i, (src, dst) in enumerate(copies)]
    for copy in copies:
        copy.start()
    for copy in copies:
        copy.wait()

    def write(before, after):
        for side, (out, starts, counts) in enumerate(((before, BEFORE_AT, BEFORE), (after, NEXT_AT, NEXT))):
            out[0:8, :] = depths[side].astype(F32)
            for a in range(4):
                for k in range(KL):
                    value = tiles[side, a, k] if a < 2 else flows[side, a - 2, k].astype(F32)[8 * side : 8 * side + 8]
                    from_row = 0 if side == 0 else 8 - counts[a]
                    at = starts[a] + counts[a] * k
                    out[at : at + counts[a], :] = value[from_row : from_row + counts[a]]
        before[BEFORE_ROWS - 8 : BEFORE_ROWS, :] = jnp.zeros((8, 128), F32)
        after[NEXT_ROWS:BEFORE_ROWS, :] = jnp.zeros((BEFORE_ROWS - NEXT_ROWS, 128), F32)

    @pl.when(is_even("gx"))
    def _():
        write(second_pair, first_pair)

    @pl.when(~is_even("gx"))
    def _():
        write(first_pair, second_pair)


def edges(tracers, east, north, levels):
    return pl.pallas_call(
        edges_kernel,
        in_specs=[pl.BlockSpec(memory_space=pltpu.HBM)] * 4,
        out_shape=[pltpu.VMEM((BEFORE_ROWS, SY), F32)] * 2,
        scratch_shapes=[
            pltpu.VMEM((2, 2, KL, 8, SY), F32),
            pltpu.VMEM((2, 2, KL, 16, SY), jnp.bfloat16),
            pltpu.VMEM((2, 8, SY), jnp.int32),
            pltpu.SemaphoreType.DMA((10,)),
        ],
        compiler_params=params(),
        name="edges",
    )(*(pltpu.with_memory_space_constraint(x, pltpu.HBM) for x in (tracers, east, north, levels)))


def low_tile(ref, a, k):
    if a == 4:
        return ref[0:8, :]
    at = NEXT_AT[a] + NEXT[a] * (k + 1) - 8
    return ref[at : at + 8, :]


def high_tile(ref, a, k):
    if a == 4:
        return ref[0:8, :]
    at = BEFORE_AT[a] + BEFORE[a] * k
    return ref[at : at + 8, :]


def pack(source, rows, last):
    group = lanes((rows, 128)) // 8
    one = jnp.zeros((rows, 128), F32)
    beyond = jnp.zeros((rows, 128), F32)
    for k in range(KL):
        value = source(k)
        one = jnp.where(group == k, pltpu.roll(value, (8 * k - 124) % 128, 1), one)
        if last:
            beyond = jnp.where(group == k, pltpu.roll(value, (8 * k + 3) % 128, 1), beyond)
    two = pltpu.roll(one, 127, 1)
    if last:
        two = jnp.where(lanes((rows, 128)) % 8 == 7, beyond, two)
    return one, two


def pack_depth(sources):
    lane = lanes(sources[0].shape)
    values = [pltpu.roll(x, turn, 1) for turn in (4, 3) for x in sources]
    values = [jnp.where(lane < 8, x, 0.0) for x in values]
    for turn in (8, 16, 32, 64):
        values = [x + pltpu.roll(x, turn, 1) for x in values]
    return list(zip(values[: len(sources)], values[len(sources) :], strict=True))


def merge_one(t0, t1, e, n, d):
    member = lanes(t0.shape) % 8
    return (
        jnp.where(member < 4, t0, pltpu.roll(n, 4, 1)),
        jnp.where(member < 4, t1, pltpu.roll(e, 4, 1)),
        d,
    )


def split_one(a, b, c):
    return a, b, pltpu.roll(b, 124, 1), pltpu.roll(a, 124, 1), c


def merge_two(t0, t1, e, n, d):
    member = lanes(t0.shape) % 8
    return (
        jnp.where(member < 3, pltpu.roll(d, 125, 1), t0),
        jnp.where(member < 2, pltpu.roll(d, 122, 1), t1),
        jnp.where((member >= 3) & (member < 7), n, pltpu.roll(e, 4, 1)),
    )


def split_two(a, b, c):
    member = lanes(a.shape) % 8
    depth = jnp.where(member < 6, pltpu.roll(a, 3, 1), pltpu.roll(b, 6, 1))
    return a, b, pltpu.roll(c, 124, 1), c, depth


def pack_all(sources, depths, rows, own, own_rows, first_pair, second_pair, sent_rows):
    packed = [pack(source, rows, a < 2) for a, source in enumerate(sources)] + [depths]
    for which in range(2):
        for a in range(5):
            own[which, a, own_rows, :] = packed[a][which]
    even = is_even("gy")
    ones = merge_one(*(p[0] for p in packed))
    twos = merge_two(*(p[1] for p in packed))
    for a in range(SENT):
        first_pair[a, sent_rows, :] = jnp.where(even, ones[a], twos[a])
        second_pair[a, sent_rows, :] = jnp.where(even, twos[a], ones[a])


def pack_block(t, e, n, d, own, one, two):
    chunk = 32
    groups = range(0, SX, 8)
    for g, pair in zip(groups, pack_depth([d[rows_at(g), :].astype(F32) for g in groups]), strict=True):
        for which in range(2):
            own[which, 4, rows_at(g), :] = pair[which]

    def body(i, carry):
        rows = pl.ds(pl.multiple_of(i * chunk, chunk), chunk)
        sources = (
            lambda k: t[0, k, rows, :],
            lambda k: t[1, k, rows, :],
            lambda k: e[k, rows, :].astype(F32),
            lambda k: n[k, rows, :].astype(F32),
        )
        depths = own[0, 4, rows, :], own[1, 4, rows, :]
        pack_all(sources, depths, chunk, own, rows, one, two, rows)
        return carry

    lax.fori_loop(0, SX // chunk, body, 0)


def pack_edges_kernel(first_pair, second_pair, first_rows, second_rows, own, one, two, low, high, low_in, high_in):
    for g in range(0, SX, 8):
        for a in range(SENT):
            one[a, rows_at(g + EDGE), :] = first_rows[a, rows_at(g), :]
            two[a, rows_at(g + EDGE), :] = second_rows[a, rows_at(g), :]
    even = is_even("gx")
    for at in range(0, BEFORE_ROWS, 8):
        rows = rows_at(at)
        value, other = first_pair[rows, :], second_pair[rows, :]
        low_in[rows, :] = jnp.where(even, other, value)
        high_in[rows, :] = jnp.where(even, value, other)
    for a in range(5):
        for k in range(KL if a < 4 else 1):
            low[KL * a + k] = low_tile(low_in, a, k)
            high[KL * a + k] = high_tile(high_in, a, k)
    depths = pack_depth([low_tile(low_in, 4, 0), high_tile(high_in, 4, 0)])
    for side, (ref, tile) in enumerate(((low_in, low_tile), (high_in, high_tile))):
        sources = [functools.partial(tile, ref, a) for a in range(4)]
        at = 0 if side == 0 else WIDE - EDGE
        pack_all(sources, depths[side], 8, own, rows_at(8 * side), one, two, rows_at(at))


def pack_edges(first, second, first_rows, second_rows):
    sent = jax.ShapeDtypeStruct((SENT, WIDE, 128), F32)
    halo = jax.ShapeDtypeStruct((ARRAYS, EDGE, SY), F32)
    return pl.pallas_call(
        pack_edges_kernel,
        out_shape=[jax.ShapeDtypeStruct((2, 5, 2 * EDGE, 128), F32), sent, sent, halo, halo],
        scratch_shapes=[pltpu.VMEM((BEFORE_ROWS, SY), F32)] * 2,
        compiler_params=params(),
        name="pack_edges",
    )(first, second, first_rows, second_rows)


def face_weights(face, flow_value, threshold):
    is_open = face > threshold
    ahead = jnp.where(is_open, KAPPA + jnp.maximum(flow_value, 0.0), 0.0)
    back = jnp.where(is_open, KAPPA - jnp.minimum(flow_value, 0.0), 0.0)
    return ahead, back


def two_steps(copies, groups, threshold, depth_at, faces, flow, coef, q0, q1, first_row=None):
    parts = [(c, g) for c in range(copies) for g in groups]
    every = [(c, t, g) for c, g in parts for t in range(2)]
    for c, g in parts:
        rows = rows_at(g)
        east, north = faces(c, g)
        coef[c, 0, rows, :], coef[c, 1, rows, :] = face_weights(east, flow[c, 0, rows, :], threshold(c))
        coef[c, 3, rows, :], coef[c, 2, rows, :] = face_weights(north, flow[c, 1, rows, :], threshold(c))
    b_south = {(c, g): back_one(coef[c, 2, rows_at(g), :]) for c, g in parts}

    def shifted(source):
        ahead = {(c, t, g): ahead_one(source[c, t, rows_at(g), :]) for c, t, g in every}
        behind = {
            (c, t, g): back_one(coef[c, 3, rows_at(g), :] * source[c, t, rows_at(g), :]) for c, t, g in every
        }
        return ahead, behind

    def combine(source, c, t, g, ahead, behind):
        rows = rows_at(g)
        return (
            coef[c, 4, rows, :] * source[c, t, rows, :]
            + coef[c, 1, rows, :] * source[c, t, rows_at(g + 1), :]
            + coef[c, 0, rows_at(g - 1), :] * source[c, t, rows_at(g - 1), :]
            + coef[c, 2, rows, :] * ahead
            + behind
        )

    ahead, behind = shifted(q0)
    for c, g in parts:
        rows = rows_at(g)
        b_here = b_south[c, g]
        if first_row is not None:
            b_here, behind[c, 0, g], behind[c, 1, g] = first_row(c, g, b_here, behind[c, 0, g], behind[c, 1, g])
        leaving = coef[c, 0, rows, :] + coef[c, 3, rows, :] + coef[c, 1, rows_at(g - 1), :] + b_here
        coef[c, 4, rows, :] = jnp.where(depth_at(c, g) > threshold(c), 1.0 - leaving, 0.0)
        for t in range(2):
            q1[c, t, rows, :] = combine(q0, c, t, g, ahead[c, t, g], behind[c, t, g])
    ahead, behind = shifted(q1)
    for c, g in parts:
        yield c, g, *(combine(q1, c, t, g, ahead[c, t, g], behind[c, t, g]) for t in range(2))


def halo_depth(levels, low, high, depth):
    for g in GROUPS:
        r = g - LOW
        if r < EDGE:
            value = low[4 * KL]
        elif r >= WIDE - EDGE:
            value = high[4 * KL]
        else:
            value = levels[rows_at(r - EDGE), :].astype(F32)
        depth[rows_at(g), :] = value
    for outside in OUTSIDE:
        depth[rows_at(outside), :] = jnp.zeros((8, 128), F32)


LEVELS = 2
END_LEVELS = 4
PLACED = 8
EARLY = 8


def set_faces(groups, depth, face):
    lane = lanes()
    ahead = {g: ahead_one(depth[rows_at(g), :]) for g in groups}
    for g in groups:
        rows = rows_at(g)
        here = depth[rows, :]
        face[0, rows, :] = jnp.minimum(here, depth[rows_at(g + 1), :])
        face[1, rows, :] = jnp.where(lane == 127, 0.0, jnp.minimum(here, ahead[g]))


def inner_levels(from_level, to_level, tracers, east, north, levels, new, total, depth, face, q0, q1, flow, coef):
    blank = jnp.zeros((8, 128), F32)
    for g in INNER:
        depth[rows_at(g), :] = levels[rows_at(g - PAD), :].astype(F32)
        total[rows_at(g), :] = blank
    for g in (GROUPS[0], GROUPS[-1]):
        depth[rows_at(g), :] = blank
        total[rows_at(g), :] = blank
        for c in range(LEVELS):
            for i in range(2):
                coef[c, i, rows_at(g), :] = blank
                q0[c, i, rows_at(g), :] = blank
                q1[c, i, rows_at(g), :] = blank
    set_faces(INNER, depth, face)

    def some_levels(i, carry):
        for c in range(LEVELS):
            k = from_level + LEVELS * i + c
            for t in range(2):
                q0[c, t, PAD : PAD + SX, :] = tracers[t, k]
            flow[c, 0, PAD : PAD + SX, :] = east[k].astype(F32)
            flow[c, 1, PAD : PAD + SX, :] = north[k].astype(F32)
        for c, g, temperature, salinity in two_steps(
            LEVELS,
            INNER,
            lambda c: (from_level + LEVELS * i + c).astype(F32),
            lambda c, g: depth[rows_at(g), :],
            lambda c, g: (face[0, rows_at(g), :], face[1, rows_at(g), :]),
            flow,
            coef,
            q0,
            q1,
        ):
            new[0, LEVELS * i + c, rows_at(g - PAD), :] = temperature
            new[1, LEVELS * i + c, rows_at(g - PAD), :] = salinity
            total[rows_at(g), :] += temperature - 0.8 * salinity
        return carry

    lax.fori_loop(0, (to_level - from_level) // LEVELS, some_levels, 0)


def block_kernel(tracers, east, north, levels, after, own, first_pair, second_pair, *rest):
    del after
    pack_block(tracers, east, north, levels, own, first_pair, second_pair)
    inner_levels(0, EARLY, tracers, east, north, levels, *rest)


def level_scratch(rows, copies):
    shapes = ((), (2,), (copies, 2), (copies, 2), (copies, 2), (copies, 5))
    return [pltpu.VMEM(shape + (rows, 128), F32) for shape in shapes]


def block(tracers, east, north, levels, after):
    sent = pltpu.VMEM((SENT, SX, 128), F32)
    return pl.pallas_call(
        block_kernel,
        in_specs=[pl.BlockSpec(memory_space=pltpu.VMEM)] * 4 + [pl.BlockSpec(memory_space=pl.ANY)],
        out_shape=[
            pltpu.VMEM((2, 5, SX, 128), F32),
            sent,
            sent,
            pltpu.VMEM((2, EARLY, SX, SY), F32),
            pltpu.VMEM((ROWS, 128), F32),
        ],
        scratch_shapes=level_scratch(ROWS, LEVELS),
        compiler_params=params(),
        cost_estimate=pl.CostEstimate(flops=20_000_000, bytes_accessed=24_000_000, transcendentals=0),
        name="block",
    )(tracers, east, north, levels, after)


def late_kernel(tracers, east, north, levels, low, high, new, total, ends_new, ends_total, *scratch):
    ends(tracers, east, north, levels, low, high, ends_new, ends_total, *scratch[6:])
    inner_levels(EARLY, KL, tracers, east, north, levels, new, total, *scratch[:6])


def ends(tracers, east, north, levels, low, high, new, total, depth, face, q0, q1, flow, coef):
    blank = jnp.zeros((8, 128), F32)
    for g in range(0, END_ROWS, 8):
        rows = rows_at(g)
        depth[rows, :] = blank
        total[rows, :] = blank
        if g not in END_GROUPS:
            for c in range(END_LEVELS):
                for i in range(2):
                    coef[c, i, rows, :] = blank
                    q0[c, i, rows, :] = blank
                    q1[c, i, rows, :] = blank
    depth[8:12, :] = low[4 * KL, 4:8, :]
    depth[12:16, :] = levels[0:8, :].astype(F32)[0:4]
    depth[24:32, :] = levels[SX - 8 : SX, :].astype(F32)
    depth[32:40, :] = high[4 * KL]
    set_faces(END_GROUPS, depth, face)

    def some_levels(i, carry):
        for c in range(END_LEVELS):
            k = END_LEVELS * i + c
            for t in range(2):
                q0[c, t, 8:12, :] = low[KL * t + k, 4:8, :]
                q0[c, t, 12:16, :] = tracers[t, k, 0:4, :]
                q0[c, t, 24:32, :] = tracers[t, k, SX - 8 : SX, :]
                q0[c, t, 32:40, :] = high[KL * t + k]
            for t, field in enumerate((east, north)):
                flow[c, t, 8:12, :] = low[KL * (2 + t) + k, 4:8, :]
                flow[c, t, 12:16, :] = field[k, 0:16, :].astype(F32)[0:4]
                flow[c, t, 24:32, :] = field[k, SX - 16 : SX, :].astype(F32)[8:16]
                flow[c, t, 32:40, :] = high[KL * (2 + t) + k]
        for c, g, temperature, salinity in two_steps(
            END_LEVELS,
            END_GROUPS,
            lambda c: (END_LEVELS * i + c).astype(F32),
            lambda c, g: depth[rows_at(g), :],
            lambda c, g: (face[0, rows_at(g), :], face[1, rows_at(g), :]),
            flow,
            coef,
            q0,
            q1,
        ):
            if g < 32:
                rows = rows_at(0 if g == 8 else 8)
                new[0, END_LEVELS * i + c, rows, :] = temperature
                new[1, END_LEVELS * i + c, rows, :] = salinity
            total[rows_at(g), :] += temperature - 0.8 * salinity
        return carry

    lax.fori_loop(0, KL // END_LEVELS, some_levels, 0)


def late_levels(tracers, east, north, levels, low, high):
    return pl.pallas_call(
        late_kernel,
        out_shape=[
            pltpu.VMEM((2, KL - EARLY, SX, SY), F32),
            pltpu.VMEM((ROWS, 128), F32),
            pltpu.VMEM((2, KL, 16, SY), F32),
            pltpu.VMEM((END_ROWS, 128), F32),
        ],
        scratch_shapes=level_scratch(ROWS, LEVELS) + level_scratch(END_ROWS, END_LEVELS),
        compiler_params=params(),
        cost_estimate=pl.CostEstimate(flops=5_000_000, bytes_accessed=6_000_000, transcendentals=0),
        name="late_levels",
    )(tracers, east, north, levels, low, high)


def operator_kernel(
    levels, low, high, own_rows, own_edges, first_pair, second_pair, early_total, late_total, ends_total,
    from_strips, fields, sums,
    depth, q0, q1, strip_depth, strip_face, strip_flow, strip_total, coef, wall, total, field, grid, *, count,
):
    lane = lanes()
    member = lane % 8
    blank = jnp.zeros((8, 128), F32)
    strip_level = (lane // 8).astype(F32)
    first = lax.axis_index("gy") == 0
    last = lax.axis_index("gy") == count - 1

    def own(which, a, g):
        r = g - LOW
        if r < EDGE:
            return own_edges[which, a, rows_at(0), :]
        if r >= WIDE - EDGE:
            return own_edges[which, a, rows_at(8), :]
        return own_rows[which, a, rows_at(r - EDGE), :]

    even = is_even("gy")

    def sent(g):
        rows = rows_at(g - LOW)
        pairs = [(first_pair[a, rows, :], second_pair[a, rows, :]) for a in range(SENT)]
        return [jnp.where(even, b, a) for a, b in pairs], [jnp.where(even, a, b) for a, b in pairs]

    halo_depth(levels, low, high, depth)
    parts = {}
    for g in GROUPS:
        from_low, from_high = sent(g)
        parts[g] = list(split_one(*from_low)), list(split_two(*from_high))
    for g in GROUPS:
        rows = rows_at(g)
        from_low, from_high = parts[g]
        from_low[4] = jnp.where(first, 0.0, from_low[4])
        from_high[4] = jnp.where(last, 0.0, from_high[4])
        for a in range(5):
            low_strip = jnp.where(member < 4, from_low[a], own(0, a, g))
            high_strip = jnp.where(member >= 3, from_high[a], own(1, a, g))
            for side, value in enumerate((low_strip, high_strip)):
                if a < 2:
                    q0[side, a, rows, :] = value
                elif a < 4:
                    strip_flow[side, a - 2, rows, :] = value
                else:
                    strip_depth[side, rows, :] = value
    for outside in OUTSIDE:
        for side in range(2):
            strip_depth[side, rows_at(outside), :] = blank

    ahead = {
        (side, g): ahead_one(strip_depth[side, rows_at(g), :]) for side in range(2) for g in GROUPS
    }
    for (side, g), value in ahead.items():
        strip_face[side, rows_at(g), :] = jnp.minimum(strip_depth[side, rows_at(g), :], value)

    for side in range(2):
        for i in range(2):
            coef[side, i, rows_at(LOW - 8), :] = blank

    def first_row(side, g, b_south, *behind):
        if side == 0:
            return b_south, *behind
        face = jnp.minimum(own(0, 4, g), own(1, 4, g))
        a_first, b_first = face_weights(face, own(0, 3, g), strip_level)
        return (
            jnp.where(member == 0, b_first, b_south),
            *(jnp.where(member == 0, a_first * own(0, t, g), behind[t]) for t in range(2)),
        )

    for side, g, temperature, salinity in two_steps(
        2,
        GROUPS,
        lambda side: strip_level,
        lambda side, g: strip_depth[side, rows_at(g), :],
        lambda side, g: (
            jnp.minimum(strip_depth[side, rows_at(g), :], strip_depth[side, rows_at(g + 1), :]),
            strip_face[side, rows_at(g), :],
        ),
        strip_flow,
        coef,
        q0,
        q1,
        first_row,
    ):
        rows = rows_at(g)
        q0[side, 0, rows, :] = temperature
        q0[side, 1, rows, :] = salinity
        strip_total[side, rows, :] = temperature - 0.8 * salinity
    for turn in (8, 16, 32, 64):
        values = {}
        for side in range(2):
            for g in GROUPS:
                value = strip_total[side, rows_at(g), :]
                values[side, g] = value + pltpu.roll(value, turn, 1)
        for (side, g), value in values.items():
            strip_total[side, rows_at(g), :] = value

    for tracer in range(2):
        high_values = {g: back_one(q0[1, tracer, rows_at(g), :]) for g in INNER}
        for g in INNER:
            rows = rows_at(g)
            from_strips[tracer, rows, :] = jnp.where(member >= 4, q0[0, tracer, rows, :], high_values[g])
    from_strip = (lane < 2) | (lane >= 126)

    def beside(low_value, high_value):
        return jnp.where(lane >= 64, pltpu.roll(low_value, 4, 1), pltpu.roll(high_value, 5, 1))

    def northward(main, side):
        a, b = ahead_one(main), ahead_one(side)
        return jnp.where(lane == 127, b, a), jnp.where(lane == 127, a, b)

    def southward(main, side):
        a, b = back_one(main), back_one(side)
        return jnp.where(lane == 0, b, a), jnp.where(lane == 0, a, b)

    for g in GROUPS:
        wall[rows_at(g), :] = early_total[rows_at(g), :] + late_total[rows_at(g), :]
    wall[PAD - 2 : PAD + 2, :] = ends_total[10:14, :]
    wall[PAD + SX - 2 : PAD + SX + 3, :] = ends_total[30:35, :]
    for g in GROUPS + OUTSIDE:
        rows = rows_at(g)
        grid[0, 0, rows, :] = depth[rows, :]
        grid[0, 1, rows, :] = beside(strip_depth[0, rows, :], strip_depth[1, rows, :])
    further_all = {g: northward(grid[0, 0, rows_at(g), :], grid[0, 1, rows_at(g), :]) for g in GROUPS}
    strip_sums = {
        g: (pltpu.roll(strip_total[0, rows_at(g), :], 4, 1), pltpu.roll(strip_total[1, rows_at(g), :], 5, 1))
        for g in GROUPS
    }
    for g in GROUPS:
        rows = rows_at(g)
        both = grid[0, 0, rows, :], grid[0, 1, rows, :]
        further = further_all[g]
        for part in range(2):
            grid[1, part, rows, :] = jnp.minimum(both[part], grid[0, part, rows_at(g + 1), :])
            grid[2, part, rows, :] = jnp.minimum(both[part], further[part])
        low_total, high_total = strip_sums[g]
        edge_total = jnp.where(lane < 64, low_total, high_total)
        total[0, rows, :] = jnp.where(from_strip, edge_total, wall[rows, :])
        total[1, rows, :] = jnp.where(lane >= 64, low_total, high_total)
    for part in range(2):
        grid[1, part, rows_at(LOW - 8), :] = blank
        for outside in OUTSIDE:
            for i in range(3):
                field[i, part, rows_at(outside), :] = blank
    scale = 1.0 / KL
    south_faces = {g: southward(grid[2, 0, rows_at(g), :], grid[2, 1, rows_at(g), :]) for g in GROUPS}
    for g in GROUPS:
        rows = rows_at(g)
        souths = south_faces[g]
        for part in range(2):
            grid[6, part, rows, :] = souths[part]
            here = grid[0, part, rows, :]
            own_part = ALPHA * scale * here + jnp.where(here == 0.0, 1.0, 0.0)
            faces = grid[1, part, rows, :] + grid[1, part, rows_at(g - 1), :] + grid[2, part, rows, :] + souths[part]
            diagonal = own_part + scale * faces
            inverse = 1.0 / diagonal
            grid[3, part, rows, :] = inverse
            grid[4, part, rows, :] = own_part
            grid[5, part, rows, :] = diagonal
            field[0, part, rows, :] = 0.25 * total[part, rows, :] * inverse

    moments = [blank] * 6
    for i in range(3):
        groups = GROUPS if i < 2 else INNER
        pairs = {g: (field[i, 0, rows_at(g), :], field[i, 1, rows_at(g), :]) for g in groups}
        all_norths = {g: northward(*pairs[g]) for g in groups}
        all_souths = {g: southward(*pairs[g]) for g in groups} if i < 2 else {}
        for g in groups:
            rows = rows_at(g)
            both = pairs[g]
            norths = all_norths[g]
            for part in range(2):
                if i == 2 and part == 1:
                    continue
                here = both[part]
                east_gap = here - field[i, part, rows_at(g + 1), :]
                north_gap = here - norths[part]
                east_face = scale * grid[1, part, rows, :]
                north_face = scale * grid[2, part, rows, :]
                own_part = grid[4, part, rows, :]
                if part == 0 and PAD <= g < PAD + SX:
                    moments[2 * i] += grid[5, 0, rows, :] * here * here
                    moments[2 * i + 1] += (
                        own_part * here * here + east_face * east_gap * east_gap + north_face * north_gap * north_gap
                    )
                if i < 2:
                    image = (
                        own_part * here
                        + east_face * east_gap
                        + scale * grid[1, part, rows_at(g - 1), :] * (here - field[i, part, rows_at(g - 1), :])
                        + north_face * north_gap
                        + scale * grid[6, part, rows, :] * (here - all_souths[g][part])
                    )
                    field[i + 1, part, rows, :] = image * grid[3, part, rows, :]
        fields[i] = field[i, 0, PAD : PAD + SX, :]
    sums_row = jnp.zeros((8, 128), F32)
    for i in range(6):
        value = jnp.sum(jnp.sum(moments[i], axis=0, keepdims=True), axis=1, keepdims=True)
        sums_row = jnp.where(lane == i, value, sums_row)
    for g in range(0, 128, 8):
        sums[rows_at(g), :] = sums_row


def operator(*arrays, count):
    tall = (ROWS, 128)
    scratch = (
        (),
        (2, 2),
        (2, 2),
        (2,),
        (2,),
        (2, 2),
        (2,),
        (2, 5),
        (),
        (2,),
        (3, 2),
        (7, 2),
    )
    return pl.pallas_call(
        functools.partial(operator_kernel, count=count),
        out_shape=[
            pltpu.VMEM((2,) + tall, F32),
            pltpu.VMEM((3, SX, SY), F32),
            jax.ShapeDtypeStruct((128, 128), F32),
        ],
        scratch_shapes=[pltpu.VMEM(s + tall, F32) for s in scratch],
        compiler_params=params(),
        name="operator",
    )(*arrays)


def place_kernel(early, late, ends_new, from_strips, new, staged, sem):
    lane = lanes()
    row = lax.broadcasted_iota(jnp.int32, (8, 128), 0)
    from_strip = (lane < 2) | (lane >= 126)
    for first_level in range(0, KL, PLACED):
        blocked, start = (early, 0) if first_level < EARLY else (late, EARLY)
        slots = [(t, first_level + c, g) for c in range(PLACED) for t in range(2) for g in range(0, SX, 8)]
        turned = {
            (t, k, g): pltpu.roll(from_strips[t, rows_at(g + PAD), :], 124 - 8 * k, 1) for t, k, g in slots
        }
        for t, k, g in slots:
            rows = rows_at(g)
            here = blocked[t, k - start, rows, :]
            if g == 0:
                here = jnp.where(row < 2, ends_new[t, k, rows_at(4), :], here)
            elif g == SX - 8:
                here = jnp.where(row >= 6, ends_new[t, k, rows_at(8), :], here)
            staged[t, k, rows, :] = jnp.where(from_strip, turned[t, k, g], here)
        at = slice(first_level, first_level + PLACED)
        for t in range(2):
            pltpu.make_async_copy(staged.at[t, at], new.at[t, at], sem).start()
    pltpu.make_async_copy(staged, new, sem).wait()


def place(*arrays):
    whole = (2, KL, SX, SY)
    return pl.pallas_call(
        place_kernel,
        out_shape=jax.ShapeDtypeStruct(whole, F32),
        out_specs=pl.BlockSpec(memory_space=pltpu.HBM),
        scratch_shapes=[pltpu.VMEM(whole, F32), pltpu.SemaphoreType.DMA(())],
        compiler_params=params(),
        cost_estimate=pl.CostEstimate(flops=2_000_000, bytes_accessed=6_000_000, transcendentals=0),
        name="place",
    )(*arrays)


def finish_kernel(sums, fields, out, sound):
    value = sums[0:8, :]
    for g in range(8, 128, 8):
        value = value + sums[rows_at(g), :]
    value = jnp.sum(value, axis=0, keepdims=True)
    lane = lanes((1, 128))
    m0, m1, m2, m3, m4, m5 = (
        jnp.sum(jnp.where(lane == i, value, 0.0), axis=1, keepdims=True) for i in range(6)
    )
    l10 = m2 / m1
    l20 = m3 / m1
    d1 = m3 - l10 * m2
    t = m4 - l20 * m2
    l21 = t / d1
    d2 = m5 - l20 * m3 - l21 * t
    enough = (d1 > 0.02 * m3) & (d2 > 0.002 * m5)
    sound[...] = jnp.broadcast_to(jnp.where(enough, 1.0, 0.0), (8, 128))
    y1 = m1 - l10 * m0
    y2 = m2 - l20 * m0 - l21 * y1
    c2 = y2 / d2
    c1 = y1 / d1 - l21 * c2
    c0 = m0 / m1 - l10 * c1 - l20 * c2
    for g in range(0, SX, 8):
        rows = rows_at(g)
        out[rows, :] = c0 * fields[0, rows, :] + c1 * fields[1, rows, :] + c2 * fields[2, rows, :]


def finish(sums, fields):
    return pl.pallas_call(
        finish_kernel,
        out_shape=[jax.ShapeDtypeStruct((SX, SY), F32), jax.ShapeDtypeStruct((8, 128), F32)],
        name="finish",
    )(*(pltpu.with_memory_space_constraint(x, pltpu.VMEM) for x in (sums, fields)))


def careful(levels, planes):
    def beside(field, axis, dim):
        count = lax.axis_size(axis)
        size = field.shape[dim]
        up = [(i, (i + 1) % count) for i in range(count)]
        before = lax.ppermute(lax.slice_in_dim(field, size - 1, size, axis=dim), axis, up)
        after = lax.ppermute(lax.slice_in_dim(field, 0, 1, axis=dim), axis, [(b, a) for a, b in up])
        whole = jnp.concatenate([before, field, after], axis=dim)
        return lax.slice_in_dim(whole, 0, size, axis=dim), lax.slice_in_dim(whole, 2, size + 2, axis=dim)

    def total(field):
        return lax.psum(jnp.sum(field), ("gx", "gy"))

    depth = levels.astype(F32) / KL
    at_first = (lax.axis_index("gy") == 0) & (lanes(depth.shape) == 0)
    at_last = (lax.axis_index("gy") == lax.axis_size("gy") - 1) & (lanes(depth.shape) == SY - 1)
    west, east = (jnp.minimum(depth, x) for x in beside(depth, "gx", 0))
    south, north = beside(depth, "gy", 1)
    south = jnp.where(at_first, 0.0, jnp.minimum(depth, south))
    north = jnp.where(at_last, 0.0, jnp.minimum(depth, north))
    diagonal = ALPHA * depth + jnp.where(levels == 0, 1.0, 0.0) + east + west + north + south
    residual = planes[0] * diagonal
    precond = direction = planes[0]
    solution = jnp.zeros_like(residual)
    now = total(residual * precond)
    for step in range(3):
        x_low, x_high = beside(direction, "gx", 0)
        y_low, y_high = beside(direction, "gy", 1)
        image = diagonal * direction - east * x_high - west * x_low - north * y_high - south * y_low
        alpha = now / total(direction * image)
        solution = solution + alpha * direction
        if step < 2:
            residual = residual - alpha * image
            precond = residual / diagonal
            later = total(residual * precond)
            direction = precond + later / now * direction
            now = later
    return solution


def first_pairs(array, axis):
    return lax.ppermute(array, axis, [(i, i ^ 1) for i in range(lax.axis_size(axis))])


def second_pairs(array, axis, around):
    count = lax.axis_size(axis)
    pairs = [] if around else [(0, 0), (count - 1, count - 1)]
    for i in range(1, count if around else count - 1, 2):
        pairs += [(i, (i + 1) % count), ((i + 1) % count, i)]
    return lax.ppermute(array, axis, pairs)


def on_device(tracers, east, north, levels):
    to_first, to_second = edges(tracers, east, north, levels)
    second = second_pairs(to_second, "gx", True)
    first = first_pairs(to_first, "gx")
    own_rows, one, two, early, early_total = block(tracers, east, north, levels, to_first)
    own_edges, one, two, low, high = pack_edges(first, second, one, two)
    second = second_pairs(two, "gy", False)
    first = first_pairs(one, "gy")
    late, late_total, ends_new, ends_total = late_levels(tracers, east, north, levels, low, high)
    from_strips, fields, sums = operator(
        levels, low, high, own_rows, own_edges, first, second, early_total, late_total, ends_total,
        count=lax.axis_size("gy"),
    )
    sums = lax.all_to_all(sums, ("gx", "gy"), split_axis=0, concat_axis=0, tiled=True)
    new = place(early, late, ends_new, from_strips)
    pressure, sound = finish(sums, fields)
    pressure = lax.cond(sound[0, 0] > 0.5, lambda: pressure, lambda: careful(levels, fields))
    return new, pressure


def solution(mesh):
    placed = (P(None, None, "gx", "gy"), P(None, "gx", "gy"), P(None, "gx", "gy"), P("gx", "gy"))
    return jax.shard_map(
        on_device,
        mesh=mesh,
        in_specs=placed,
        out_specs=(P(None, None, "gx", "gy"), P("gx", "gy")),
        check_vma=False,
    )
```

```python
import functools

import jax
import jax.numpy as jnp
from jax import lax
from jax.experimental import pallas as pl
from jax.experimental.pallas import tpu as pltpu
from jax.sharding import PartitionSpec as P

KAPPA = 0.08
ALPHA = 0.05
F32 = jnp.float32

SX = 128
SY = 128
KL = 16
EDGE = 8
PAD = 16
ROWS = SX + 2 * PAD
WIDE = SX + 2 * EDGE
LOW = PAD - EDGE
ARRAYS = 2 * KL + 2 * KL + 1
VMEM = 40 * 1024 * 1024
GROUPS = tuple(range(LOW, LOW + WIDE, 8))
OUTSIDE = (LOW - 8, LOW + WIDE)
INNER = GROUPS[1:-1]
END_GROUPS = (8, 24, 32)
END_ROWS = 48
SENT = 3


def params():
    return pltpu.CompilerParams(vmem_limit_bytes=VMEM)


def is_even(axis):
    return lax.rem(lax.axis_index(axis), 2) == 0


def rows_at(row):
    return slice(row, row + 8)


def lanes(shape=(8, 128)):
    return lax.broadcasted_iota(jnp.int32, shape, len(shape) - 1)


def ahead_one(value):
    return pltpu.roll(value, 127, 1)


def back_one(value):
    return pltpu.roll(value, 1, 1)


def offsets(counts):
    starts, at = [], 8
    for a in range(4):
        starts.append(at)
        at += KL * counts[a]
    return starts, at


NEXT = (4, 4, 4, 4)
BEFORE = (5, 5, 4, 4)
NEXT_AT, NEXT_ROWS = offsets(NEXT)
BEFORE_AT, BEFORE_ROWS = offsets(BEFORE)
BEFORE_ROWS += 8
assert NEXT_ROWS <= BEFORE_ROWS


def edges_kernel(t, e, n, d, first_pair, second_pair, tiles, flows, depths, sems):
    copies = []
    for side, at in enumerate((0, SX - 8)):
        at16 = 0 if side == 0 else SX - 16
        copies += [
            (t.at[0, :, at : at + 8, :], tiles.at[side, 0]),
            (t.at[1, :, at : at + 8, :], tiles.at[side, 1]),
            (e.at[:, at16 : at16 + 16, :], flows.at[side, 0]),
            (n.at[:, at16 : at16 + 16, :], flows.at[side, 1]),
            (d.at[at : at + 8, :], depths.at[side]),
        ]
    copies = [pltpu.make_async_copy(src, dst, sems.at[i]) for i, (src, dst) in enumerate(copies)]
    for copy in copies:
        copy.start()
    for copy in copies:
        copy.wait()

    def write(before, after):
        for side, (out, starts, counts) in enumerate(((before, BEFORE_AT, BEFORE), (after, NEXT_AT, NEXT))):
            out[0:8, :] = depths[side].astype(F32)
            for a in range(4):
                for k in range(KL):
                    value = tiles[side, a, k] if a < 2 else flows[side, a - 2, k].astype(F32)[8 * side : 8 * side + 8]
                    from_row = 0 if side == 0 else 8 - counts[a]
                    at = starts[a] + counts[a] * k
                    out[at : at + counts[a], :] = value[from_row : from_row + counts[a]]
        before[BEFORE_ROWS - 8 : BEFORE_ROWS, :] = jnp.zeros((8, 128), F32)
        after[NEXT_ROWS:BEFORE_ROWS, :] = jnp.zeros((BEFORE_ROWS - NEXT_ROWS, 128), F32)

    @pl.when(is_even("gx"))
    def _():
        write(second_pair, first_pair)

    @pl.when(~is_even("gx"))
    def _():
        write(first_pair, second_pair)


def edges(tracers, east, north, levels):
    return pl.pallas_call(
        edges_kernel,
        in_specs=[pl.BlockSpec(memory_space=pltpu.HBM)] * 4,
        out_shape=[pltpu.VMEM((BEFORE_ROWS, SY), F32)] * 2,
        scratch_shapes=[
            pltpu.VMEM((2, 2, KL, 8, SY), F32),
            pltpu.VMEM((2, 2, KL, 16, SY), jnp.bfloat16),
            pltpu.VMEM((2, 8, SY), jnp.int32),
            pltpu.SemaphoreType.DMA((10,)),
        ],
        compiler_params=params(),
        name="edges",
    )(*(pltpu.with_memory_space_constraint(x, pltpu.HBM) for x in (tracers, east, north, levels)))


def low_tile(ref, a, k):
    if a == 4:
        return ref[0:8, :]
    at = NEXT_AT[a] + NEXT[a] * (k + 1) - 8
    return ref[at : at + 8, :]


def high_tile(ref, a, k):
    if a == 4:
        return ref[0:8, :]
    at = BEFORE_AT[a] + BEFORE[a] * k
    return ref[at : at + 8, :]


def pack(source, rows, last):
    group = lanes((rows, 128)) // 8
    one = jnp.zeros((rows, 128), F32)
    beyond = jnp.zeros((rows, 128), F32)
    for k in range(KL):
        value = source(k)
        one = jnp.where(group == k, pltpu.roll(value, (8 * k - 124) % 128, 1), one)
        if last:
            beyond = jnp.where(group == k, pltpu.roll(value, (8 * k + 3) % 128, 1), beyond)
    two = pltpu.roll(one, 127, 1)
    if last:
        two = jnp.where(lanes((rows, 128)) % 8 == 7, beyond, two)
    return one, two


def pack_depth(sources):
    lane = lanes(sources[0].shape)
    values = [pltpu.roll(x, turn, 1) for turn in (4, 3) for x in sources]
    values = [jnp.where(lane < 8, x, 0.0) for x in values]
    for turn in (8, 16, 32, 64):
        values = [x + pltpu.roll(x, turn, 1) for x in values]
    return list(zip(values[: len(sources)], values[len(sources) :], strict=True))


def merge_one(t0, t1, e, n, d):
    member = lanes(t0.shape) % 8
    return (
        jnp.where(member < 4, t0, pltpu.roll(n, 4, 1)),
        jnp.where(member < 4, t1, pltpu.roll(e, 4, 1)),
        d,
    )


def split_one(a, b, c):
    return a, b, pltpu.roll(b, 124, 1), pltpu.roll(a, 124, 1), c


def merge_two(t0, t1, e, n, d):
    member = lanes(t0.shape) % 8
    return (
        jnp.where(member < 3, pltpu.roll(d, 125, 1), t0),
        jnp.where(member < 2, pltpu.roll(d, 122, 1), t1),
        jnp.where((member >= 3) & (member < 7), n, pltpu.roll(e, 4, 1)),
    )


def split_two(a, b, c):
    member = lanes(a.shape) % 8
    depth = jnp.where(member < 6, pltpu.roll(a, 3, 1), pltpu.roll(b, 6, 1))
    return a, b, pltpu.roll(c, 124, 1), c, depth


def pack_all(sources, depths, rows, own, own_rows, first_pair, second_pair, sent_rows):
    packed = [pack(source, rows, a < 2) for a, source in enumerate(sources)] + [depths]
    for which in range(2):
        for a in range(5):
            own[which, a, own_rows, :] = packed[a][which]
    even = is_even("gy")
    ones = merge_one(*(p[0] for p in packed))
    twos = merge_two(*(p[1] for p in packed))
    for a in range(SENT):
        first_pair[a, sent_rows, :] = jnp.where(even, ones[a], twos[a])
        second_pair[a, sent_rows, :] = jnp.where(even, twos[a], ones[a])


def pack_block(t, e, n, d, own, one, two):
    chunk = 32
    groups = range(0, SX, 8)
    for g, pair in zip(groups, pack_depth([d[rows_at(g), :].astype(F32) for g in groups]), strict=True):
        for which in range(2):
            own[which, 4, rows_at(g), :] = pair[which]

    def body(i, carry):
        rows = pl.ds(pl.multiple_of(i * chunk, chunk), chunk)
        sources = (
            lambda k: t[0, k, rows, :],
            lambda k: t[1, k, rows, :],
            lambda k: e[k, rows, :].astype(F32),
            lambda k: n[k, rows, :].astype(F32),
        )
        depths = own[0, 4, rows, :], own[1, 4, rows, :]
        pack_all(sources, depths, chunk, own, rows, one, two, rows)
        return carry

    lax.fori_loop(0, SX // chunk, body, 0)


def pack_edges_kernel(first_pair, second_pair, first_rows, second_rows, own, one, two, low, high, low_in, high_in):
    for g in range(0, SX, 8):
        for a in range(SENT):
            one[a, rows_at(g + EDGE), :] = first_rows[a, rows_at(g), :]
            two[a, rows_at(g + EDGE), :] = second_rows[a, rows_at(g), :]
    even = is_even("gx")
    for at in range(0, BEFORE_ROWS, 8):
        rows = rows_at(at)
        value, other = first_pair[rows, :], second_pair[rows, :]
        low_in[rows, :] = jnp.where(even, other, value)
        high_in[rows, :] = jnp.where(even, value, other)
    for a in range(5):
        for k in range(KL if a < 4 else 1):
            low[KL * a + k] = low_tile(low_in, a, k)
            high[KL * a + k] = high_tile(high_in, a, k)
    depths = pack_depth([low_tile(low_in, 4, 0), high_tile(high_in, 4, 0)])
    for side, (ref, tile) in enumerate(((low_in, low_tile), (high_in, high_tile))):
        sources = [functools.partial(tile, ref, a) for a in range(4)]
        at = 0 if side == 0 else WIDE - EDGE
        pack_all(sources, depths[side], 8, own, rows_at(8 * side), one, two, rows_at(at))


def pack_edges(first, second, first_rows, second_rows):
    sent = jax.ShapeDtypeStruct((SENT, WIDE, 128), F32)
    halo = jax.ShapeDtypeStruct((ARRAYS, EDGE, SY), F32)
    return pl.pallas_call(
        pack_edges_kernel,
        out_shape=[jax.ShapeDtypeStruct((2, 5, 2 * EDGE, 128), F32), sent, sent, halo, halo],
        scratch_shapes=[pltpu.VMEM((BEFORE_ROWS, SY), F32)] * 2,
        compiler_params=params(),
        name="pack_edges",
    )(first, second, first_rows, second_rows)


def face_weights(face, flow_value, threshold):
    is_open = face > threshold
    ahead = jnp.where(is_open, KAPPA + jnp.maximum(flow_value, 0.0), 0.0)
    back = jnp.where(is_open, KAPPA - jnp.minimum(flow_value, 0.0), 0.0)
    return ahead, back


def two_steps(copies, groups, threshold, depth_at, faces, flow, coef, q0, q1, first_row=None):
    parts = [(c, g) for c in range(copies) for g in groups]
    every = [(c, t, g) for c, g in parts for t in range(2)]
    for c, g in parts:
        rows = rows_at(g)
        east, north = faces(c, g)
        coef[c, 0, rows, :], coef[c, 1, rows, :] = face_weights(east, flow[c, 0, rows, :], threshold(c))
        coef[c, 3, rows, :], coef[c, 2, rows, :] = face_weights(north, flow[c, 1, rows, :], threshold(c))
    b_south = {(c, g): back_one(coef[c, 2, rows_at(g), :]) for c, g in parts}

    def shifted(source):
        ahead = {(c, t, g): ahead_one(source[c, t, rows_at(g), :]) for c, t, g in every}
        behind = {
            (c, t, g): back_one(coef[c, 3, rows_at(g), :] * source[c, t, rows_at(g), :]) for c, t, g in every
        }
        return ahead, behind

    def combine(source, c, t, g, ahead, behind):
        rows = rows_at(g)
        return (
            coef[c, 4, rows, :] * source[c, t, rows, :]
            + coef[c, 1, rows, :] * source[c, t, rows_at(g + 1), :]
            + coef[c, 0, rows_at(g - 1), :] * source[c, t, rows_at(g - 1), :]
            + coef[c, 2, rows, :] * ahead
            + behind
        )

    ahead, behind = shifted(q0)
    for c, g in parts:
        rows = rows_at(g)
        b_here = b_south[c, g]
        if first_row is not None:
            b_here, behind[c, 0, g], behind[c, 1, g] = first_row(c, g, b_here, behind[c, 0, g], behind[c, 1, g])
        leaving = coef[c, 0, rows, :] + coef[c, 3, rows, :] + coef[c, 1, rows_at(g - 1), :] + b_here
        coef[c, 4, rows, :] = jnp.where(depth_at(c, g) > threshold(c), 1.0 - leaving, 0.0)
        for t in range(2):
            q1[c, t, rows, :] = combine(q0, c, t, g, ahead[c, t, g], behind[c, t, g])
    ahead, behind = shifted(q1)
    for c, g in parts:
        yield c, g, *(combine(q1, c, t, g, ahead[c, t, g], behind[c, t, g]) for t in range(2))


def halo_depth(levels, low, high, depth):
    for g in GROUPS:
        r = g - LOW
        if r < EDGE:
            value = low[4 * KL]
        elif r >= WIDE - EDGE:
            value = high[4 * KL]
        else:
            value = levels[rows_at(r - EDGE), :].astype(F32)
        depth[rows_at(g), :] = value
    for outside in OUTSIDE:
        depth[rows_at(outside), :] = jnp.zeros((8, 128), F32)


LEVELS = 2
END_LEVELS = 4
PLACED = 8
EARLY = 8


def set_faces(groups, depth, face):
    lane = lanes()
    ahead = {g: ahead_one(depth[rows_at(g), :]) for g in groups}
    for g in groups:
        rows = rows_at(g)
        here = depth[rows, :]
        face[0, rows, :] = jnp.minimum(here, depth[rows_at(g + 1), :])
        face[1, rows, :] = jnp.where(lane == 127, 0.0, jnp.minimum(here, ahead[g]))


def inner_levels(from_level, to_level, tracers, east, north, levels, new, total, depth, face, q0, q1, flow, coef):
    blank = jnp.zeros((8, 128), F32)
    for g in INNER:
        depth[rows_at(g), :] = levels[rows_at(g - PAD), :].astype(F32)
        total[rows_at(g), :] = blank
    for g in (GROUPS[0], GROUPS[-1]):
        depth[rows_at(g), :] = blank
        total[rows_at(g), :] = blank
        for c in range(LEVELS):
            for i in range(2):
                coef[c, i, rows_at(g), :] = blank
                q0[c, i, rows_at(g), :] = blank
                q1[c, i, rows_at(g), :] = blank
    set_faces(INNER, depth, face)

    def some_levels(i, carry):
        for c in range(LEVELS):
            k = from_level + LEVELS * i + c
            for t in range(2):
                q0[c, t, PAD : PAD + SX, :] = tracers[t, k]
            flow[c, 0, PAD : PAD + SX, :] = east[k].astype(F32)
            flow[c, 1, PAD : PAD + SX, :] = north[k].astype(F32)
        for c, g, temperature, salinity in two_steps(
            LEVELS,
            INNER,
            lambda c: (from_level + LEVELS * i + c).astype(F32),
            lambda c, g: depth[rows_at(g), :],
            lambda c, g: (face[0, rows_at(g), :], face[1, rows_at(g), :]),
            flow,
            coef,
            q0,
            q1,
        ):
            new[0, LEVELS * i + c, rows_at(g - PAD), :] = temperature
            new[1, LEVELS * i + c, rows_at(g - PAD), :] = salinity
            total[rows_at(g), :] += temperature - 0.8 * salinity
        return carry

    lax.fori_loop(0, (to_level - from_level) // LEVELS, some_levels, 0)


def block_kernel(tracers, east, north, levels, after, own, first_pair, second_pair, *rest):
    del after
    pack_block(tracers, east, north, levels, own, first_pair, second_pair)
    inner_levels(0, EARLY, tracers, east, north, levels, *rest)


def level_scratch(rows, copies):
    shapes = ((), (2,), (copies, 2), (copies, 2), (copies, 2), (copies, 5))
    return [pltpu.VMEM(shape + (rows, 128), F32) for shape in shapes]


def block(tracers, east, north, levels, after):
    sent = pltpu.VMEM((SENT, SX, 128), F32)
    return pl.pallas_call(
        block_kernel,
        in_specs=[pl.BlockSpec(memory_space=pltpu.VMEM)] * 4 + [pl.BlockSpec(memory_space=pl.ANY)],
        out_shape=[
            pltpu.VMEM((2, 5, SX, 128), F32),
            sent,
            sent,
            pltpu.VMEM((2, EARLY, SX, SY), F32),
            pltpu.VMEM((ROWS, 128), F32),
        ],
        scratch_shapes=level_scratch(ROWS, LEVELS),
        compiler_params=params(),
        cost_estimate=pl.CostEstimate(flops=20_000_000, bytes_accessed=24_000_000, transcendentals=0),
        name="block",
    )(tracers, east, north, levels, after)


def late_kernel(tracers, east, north, levels, low, high, new, total, ends_new, ends_total, *scratch):
    ends(tracers, east, north, levels, low, high, ends_new, ends_total, *scratch[6:])
    inner_levels(EARLY, KL, tracers, east, north, levels, new, total, *scratch[:6])


def ends(tracers, east, north, levels, low, high, new, total, depth, face, q0, q1, flow, coef):
    blank = jnp.zeros((8, 128), F32)
    for g in range(0, END_ROWS, 8):
        rows = rows_at(g)
        depth[rows, :] = blank
        total[rows, :] = blank
        if g not in END_GROUPS:
            for c in range(END_LEVELS):
                for i in range(2):
                    coef[c, i, rows, :] = blank
                    q0[c, i, rows, :] = blank
                    q1[c, i, rows, :] = blank
    depth[8:12, :] = low[4 * KL, 4:8, :]
    depth[12:16, :] = levels[0:8, :].astype(F32)[0:4]
    depth[24:32, :] = levels[SX - 8 : SX, :].astype(F32)
    depth[32:40, :] = high[4 * KL]
    set_faces(END_GROUPS, depth, face)

    def some_levels(i, carry):
        for c in range(END_LEVELS):
            k = END_LEVELS * i + c
            for t in range(2):
                q0[c, t, 8:12, :] = low[KL * t + k, 4:8, :]
                q0[c, t, 12:16, :] = tracers[t, k, 0:4, :]
                q0[c, t, 24:32, :] = tracers[t, k, SX - 8 : SX, :]
                q0[c, t, 32:40, :] = high[KL * t + k]
            for t, field in enumerate((east, north)):
                flow[c, t, 8:12, :] = low[KL * (2 + t) + k, 4:8, :]
                flow[c, t, 12:16, :] = field[k, 0:16, :].astype(F32)[0:4]
                flow[c, t, 24:32, :] = field[k, SX - 16 : SX, :].astype(F32)[8:16]
                flow[c, t, 32:40, :] = high[KL * (2 + t) + k]
        for c, g, temperature, salinity in two_steps(
            END_LEVELS,
            END_GROUPS,
            lambda c: (END_LEVELS * i + c).astype(F32),
            lambda c, g: depth[rows_at(g), :],
            lambda c, g: (face[0, rows_at(g), :], face[1, rows_at(g), :]),
            flow,
            coef,
            q0,
            q1,
        ):
            if g < 32:
                rows = rows_at(0 if g == 8 else 8)
                new[0, END_LEVELS * i + c, rows, :] = temperature
                new[1, END_LEVELS * i + c, rows, :] = salinity
            total[rows_at(g), :] += temperature - 0.8 * salinity
        return carry

    lax.fori_loop(0, KL // END_LEVELS, some_levels, 0)


def late_levels(tracers, east, north, levels, low, high):
    return pl.pallas_call(
        late_kernel,
        out_shape=[
            pltpu.VMEM((2, KL - EARLY, SX, SY), F32),
            pltpu.VMEM((ROWS, 128), F32),
            pltpu.VMEM((2, KL, 16, SY), F32),
            pltpu.VMEM((END_ROWS, 128), F32),
        ],
        scratch_shapes=level_scratch(ROWS, LEVELS) + level_scratch(END_ROWS, END_LEVELS),
        compiler_params=params(),
        cost_estimate=pl.CostEstimate(flops=5_000_000, bytes_accessed=6_000_000, transcendentals=0),
        name="late_levels",
    )(tracers, east, north, levels, low, high)


def operator_kernel(
    levels, low, high, own_rows, own_edges, first_pair, second_pair, early_total, late_total, ends_total,
    from_strips, fields, sums,
    depth, q0, q1, strip_depth, strip_face, strip_flow, strip_total, coef, wall, total, field, grid, *, count,
):
    lane = lanes()
    member = lane % 8
    blank = jnp.zeros((8, 128), F32)
    strip_level = (lane // 8).astype(F32)
    first = lax.axis_index("gy") == 0
    last = lax.axis_index("gy") == count - 1

    def own(which, a, g):
        r = g - LOW
        if r < EDGE:
            return own_edges[which, a, rows_at(0), :]
        if r >= WIDE - EDGE:
            return own_edges[which, a, rows_at(8), :]
        return own_rows[which, a, rows_at(r - EDGE), :]

    even = is_even("gy")

    def sent(g):
        rows = rows_at(g - LOW)
        pairs = [(first_pair[a, rows, :], second_pair[a, rows, :]) for a in range(SENT)]
        return [jnp.where(even, b, a) for a, b in pairs], [jnp.where(even, a, b) for a, b in pairs]

    halo_depth(levels, low, high, depth)
    parts = {}
    for g in GROUPS:
        from_low, from_high = sent(g)
        parts[g] = list(split_one(*from_low)), list(split_two(*from_high))
    for g in GROUPS:
        rows = rows_at(g)
        from_low, from_high = parts[g]
        from_low[4] = jnp.where(first, 0.0, from_low[4])
        from_high[4] = jnp.where(last, 0.0, from_high[4])
        for a in range(5):
            low_strip = jnp.where(member < 4, from_low[a], own(0, a, g))
            high_strip = jnp.where(member >= 3, from_high[a], own(1, a, g))
            for side, value in enumerate((low_strip, high_strip)):
                if a < 2:
                    q0[side, a, rows, :] = value
                elif a < 4:
                    strip_flow[side, a - 2, rows, :] = value
                else:
                    strip_depth[side, rows, :] = value
    for outside in OUTSIDE:
        for side in range(2):
            strip_depth[side, rows_at(outside), :] = blank

    ahead = {
        (side, g): ahead_one(strip_depth[side, rows_at(g), :]) for side in range(2) for g in GROUPS
    }
    for (side, g), value in ahead.items():
        strip_face[side, rows_at(g), :] = jnp.minimum(strip_depth[side, rows_at(g), :], value)

    for side in range(2):
        for i in range(2):
            coef[side, i, rows_at(LOW - 8), :] = blank

    def first_row(side, g, b_south, *behind):
        if side == 0:
            return b_south, *behind
        face = jnp.minimum(own(0, 4, g), own(1, 4, g))
        a_first, b_first = face_weights(face, own(0, 3, g), strip_level)
        return (
            jnp.where(member == 0, b_first, b_south),
            *(jnp.where(member == 0, a_first * own(0, t, g), behind[t]) for t in range(2)),
        )

    for side, g, temperature, salinity in two_steps(
        2,
        GROUPS,
        lambda side: strip_level,
        lambda side, g: strip_depth[side, rows_at(g), :],
        lambda side, g: (
            jnp.minimum(strip_depth[side, rows_at(g), :], strip_depth[side, rows_at(g + 1), :]),
            strip_face[side, rows_at(g), :],
        ),
        strip_flow,
        coef,
        q0,
        q1,
        first_row,
    ):
        rows = rows_at(g)
        q0[side, 0, rows, :] = temperature
        q0[side, 1, rows, :] = salinity
        strip_total[side, rows, :] = temperature - 0.8 * salinity
    for turn in (8, 16, 32, 64):
        values = {}
        for side in range(2):
            for g in GROUPS:
                value = strip_total[side, rows_at(g), :]
                values[side, g] = value + pltpu.roll(value, turn, 1)
        for (side, g), value in values.items():
            strip_total[side, rows_at(g), :] = value

    for tracer in range(2):
        high_values = {g: back_one(q0[1, tracer, rows_at(g), :]) for g in INNER}
        for g in INNER:
            rows = rows_at(g)
            from_strips[tracer, rows, :] = jnp.where(member >= 4, q0[0, tracer, rows, :], high_values[g])
    from_strip = (lane < 2) | (lane >= 126)

    def beside(low_value, high_value):
        return jnp.where(lane >= 64, pltpu.roll(low_value, 4, 1), pltpu.roll(high_value, 5, 1))

    def northward(main, side):
        a, b = ahead_one(main), ahead_one(side)
        return jnp.where(lane == 127, b, a), jnp.where(lane == 127, a, b)

    def southward(main, side):
        a, b = back_one(main), back_one(side)
        return jnp.where(lane == 0, b, a), jnp.where(lane == 0, a, b)

    for g in GROUPS:
        wall[rows_at(g), :] = early_total[rows_at(g), :] + late_total[rows_at(g), :]
    wall[PAD - 2 : PAD + 2, :] = ends_total[10:14, :]
    wall[PAD + SX - 2 : PAD + SX + 3, :] = ends_total[30:35, :]
    for g in GROUPS + OUTSIDE:
        rows = rows_at(g)
        grid[0, 0, rows, :] = depth[rows, :]
        grid[0, 1, rows, :] = beside(strip_depth[0, rows, :], strip_depth[1, rows, :])
    further_all = {g: northward(grid[0, 0, rows_at(g), :], grid[0, 1, rows_at(g), :]) for g in GROUPS}
    strip_sums = {
        g: (pltpu.roll(strip_total[0, rows_at(g), :], 4, 1), pltpu.roll(strip_total[1, rows_at(g), :], 5, 1))
        for g in GROUPS
    }
    for g in GROUPS:
        rows = rows_at(g)
        both = grid[0, 0, rows, :], grid[0, 1, rows, :]
        further = further_all[g]
        for part in range(2):
            grid[1, part, rows, :] = jnp.minimum(both[part], grid[0, part, rows_at(g + 1), :])
            grid[2, part, rows, :] = jnp.minimum(both[part], further[part])
        low_total, high_total = strip_sums[g]
        edge_total = jnp.where(lane < 64, low_total, high_total)
        total[0, rows, :] = jnp.where(from_strip, edge_total, wall[rows, :])
        total[1, rows, :] = jnp.where(lane >= 64, low_total, high_total)
    for part in range(2):
        grid[1, part, rows_at(LOW - 8), :] = blank
        for outside in OUTSIDE:
            for i in range(3):
                field[i, part, rows_at(outside), :] = blank
    scale = 1.0 / KL
    south_faces = {g: southward(grid[2, 0, rows_at(g), :], grid[2, 1, rows_at(g), :]) for g in GROUPS}
    for g in GROUPS:
        rows = rows_at(g)
        souths = south_faces[g]
        for part in range(2):
            grid[6, part, rows, :] = souths[part]
            here = grid[0, part, rows, :]
            own_part = ALPHA * scale * here + jnp.where(here == 0.0, 1.0, 0.0)
            faces = grid[1, part, rows, :] + grid[1, part, rows_at(g - 1), :] + grid[2, part, rows, :] + souths[part]
            diagonal = own_part + scale * faces
            inverse = 1.0 / diagonal
            grid[3, part, rows, :] = inverse
            grid[4, part, rows, :] = own_part
            grid[5, part, rows, :] = diagonal
            field[0, part, rows, :] = 0.25 * total[part, rows, :] * inverse

    moments = [blank] * 6
    for i in range(3):
        groups = GROUPS if i < 2 else INNER
        pairs = {g: (field[i, 0, rows_at(g), :], field[i, 1, rows_at(g), :]) for g in groups}
        all_norths = {g: northward(*pairs[g]) for g in groups}
        all_souths = {g: southward(*pairs[g]) for g in groups} if i < 2 else {}
        for g in groups:
            rows = rows_at(g)
            both = pairs[g]
            norths = all_norths[g]
            for part in range(2):
                if i == 2 and part == 1:
                    continue
                here = both[part]
                east_gap = here - field[i, part, rows_at(g + 1), :]
                north_gap = here - norths[part]
                east_face = scale * grid[1, part, rows, :]
                north_face = scale * grid[2, part, rows, :]
                own_part = grid[4, part, rows, :]
                if part == 0 and PAD <= g < PAD + SX:
                    moments[2 * i] += grid[5, 0, rows, :] * here * here
                    moments[2 * i + 1] += (
                        own_part * here * here + east_face * east_gap * east_gap + north_face * north_gap * north_gap
                    )
                if i < 2:
                    image = (
                        own_part * here
                        + east_face * east_gap
                        + scale * grid[1, part, rows_at(g - 1), :] * (here - field[i, part, rows_at(g - 1), :])
                        + north_face * north_gap
                        + scale * grid[6, part, rows, :] * (here - all_souths[g][part])
                    )
                    field[i + 1, part, rows, :] = image * grid[3, part, rows, :]
        fields[i] = field[i, 0, PAD : PAD + SX, :]
    sums_row = jnp.zeros((8, 128), F32)
    for i in range(6):
        value = jnp.sum(jnp.sum(moments[i], axis=0, keepdims=True), axis=1, keepdims=True)
        sums_row = jnp.where(lane == i, value, sums_row)
    for g in range(0, 128, 8):
        sums[rows_at(g), :] = sums_row


def operator(*arrays, count):
    tall = (ROWS, 128)
    scratch = (
        (),
        (2, 2),
        (2, 2),
        (2,),
        (2,),
        (2, 2),
        (2,),
        (2, 5),
        (),
        (2,),
        (3, 2),
        (7, 2),
    )
    return pl.pallas_call(
        functools.partial(operator_kernel, count=count),
        out_shape=[
            pltpu.VMEM((2,) + tall, F32),
            pltpu.VMEM((3, SX, SY), F32),
            jax.ShapeDtypeStruct((128, 128), F32),
        ],
        scratch_shapes=[pltpu.VMEM(s + tall, F32) for s in scratch],
        compiler_params=params(),
        name="operator",
    )(*arrays)


def place_kernel(early, late, ends_new, from_strips, new, staged, sem):
    lane = lanes()
    row = lax.broadcasted_iota(jnp.int32, (8, 128), 0)
    from_strip = (lane < 2) | (lane >= 126)
    for first_level in range(0, KL, PLACED):
        blocked, start = (early, 0) if first_level < EARLY else (late, EARLY)
        slots = [(t, first_level + c, g) for c in range(PLACED) for t in range(2) for g in range(0, SX, 8)]
        turned = {
            (t, k, g): pltpu.roll(from_strips[t, rows_at(g + PAD), :], 124 - 8 * k, 1) for t, k, g in slots
        }
        for t, k, g in slots:
            rows = rows_at(g)
            here = blocked[t, k - start, rows, :]
            if g == 0:
                here = jnp.where(row < 2, ends_new[t, k, rows_at(4), :], here)
            elif g == SX - 8:
                here = jnp.where(row >= 6, ends_new[t, k, rows_at(8), :], here)
            staged[t, k, rows, :] = jnp.where(from_strip, turned[t, k, g], here)
        at = slice(first_level, first_level + PLACED)
        for t in range(2):
            pltpu.make_async_copy(staged.at[t, at], new.at[t, at], sem).start()
    pltpu.make_async_copy(staged, new, sem).wait()


def place(*arrays):
    whole = (2, KL, SX, SY)
    return pl.pallas_call(
        place_kernel,
        out_shape=jax.ShapeDtypeStruct(whole, F32),
        out_specs=pl.BlockSpec(memory_space=pltpu.HBM),
        scratch_shapes=[pltpu.VMEM(whole, F32), pltpu.SemaphoreType.DMA(())],
        compiler_params=params(),
        cost_estimate=pl.CostEstimate(flops=2_000_000, bytes_accessed=6_000_000, transcendentals=0),
        name="place",
    )(*arrays)


def finish_kernel(sums, fields, out, sound):
    value = sums[0:8, :]
    for g in range(8, 128, 8):
        value = value + sums[rows_at(g), :]
    value = jnp.sum(value, axis=0, keepdims=True)
    lane = lanes((1, 128))
    m0, m1, m2, m3, m4, m5 = (
        jnp.sum(jnp.where(lane == i, value, 0.0), axis=1, keepdims=True) for i in range(6)
    )
    l10 = m2 / m1
    l20 = m3 / m1
    d1 = m3 - l10 * m2
    t = m4 - l20 * m2
    l21 = t / d1
    d2 = m5 - l20 * m3 - l21 * t
    enough = (d1 > 0.02 * m3) & (d2 > 0.002 * m5)
    sound[0] = jnp.where(enough, 1.0, 0.0)[0, 0]
    y1 = m1 - l10 * m0
    y2 = m2 - l20 * m0 - l21 * y1
    c2 = y2 / d2
    c1 = y1 / d1 - l21 * c2
    c0 = m0 / m1 - l10 * c1 - l20 * c2
    for g in range(0, SX, 8):
        rows = rows_at(g)
        out[rows, :] = c0 * fields[0, rows, :] + c1 * fields[1, rows, :] + c2 * fields[2, rows, :]


def finish(sums, fields):
    return pl.pallas_call(
        finish_kernel,
        out_shape=[jax.ShapeDtypeStruct((SX, SY), F32), jax.ShapeDtypeStruct((1,), F32)],
        out_specs=[pl.BlockSpec(memory_space=pltpu.VMEM), pl.BlockSpec(memory_space=pltpu.SMEM)],
        name="finish",
    )(*(pltpu.with_memory_space_constraint(x, pltpu.VMEM) for x in (sums, fields)))


def careful(levels, planes):
    def beside(field, axis, dim):
        count = lax.axis_size(axis)
        size = field.shape[dim]
        up = [(i, (i + 1) % count) for i in range(count)]
        before = lax.ppermute(lax.slice_in_dim(field, size - 1, size, axis=dim), axis, up)
        after = lax.ppermute(lax.slice_in_dim(field, 0, 1, axis=dim), axis, [(b, a) for a, b in up])
        whole = jnp.concatenate([before, field, after], axis=dim)
        return lax.slice_in_dim(whole, 0, size, axis=dim), lax.slice_in_dim(whole, 2, size + 2, axis=dim)

    def total(field):
        return lax.psum(jnp.sum(field), ("gx", "gy"))

    depth = levels.astype(F32) / KL
    at_first = (lax.axis_index("gy") == 0) & (lanes(depth.shape) == 0)
    at_last = (lax.axis_index("gy") == lax.axis_size("gy") - 1) & (lanes(depth.shape) == SY - 1)
    west, east = (jnp.minimum(depth, x) for x in beside(depth, "gx", 0))
    south, north = beside(depth, "gy", 1)
    south = jnp.where(at_first, 0.0, jnp.minimum(depth, south))
    north = jnp.where(at_last, 0.0, jnp.minimum(depth, north))
    diagonal = ALPHA * depth + jnp.where(levels == 0, 1.0, 0.0) + east + west + north + south
    residual = planes[0] * diagonal
    precond = direction = planes[0]
    solution = jnp.zeros_like(residual)
    now = total(residual * precond)
    for step in range(3):
        x_low, x_high = beside(direction, "gx", 0)
        y_low, y_high = beside(direction, "gy", 1)
        image = diagonal * direction - east * x_high - west * x_low - north * y_high - south * y_low
        alpha = now / total(direction * image)
        solution = solution + alpha * direction
        if step < 2:
            residual = residual - alpha * image
            precond = residual / diagonal
            later = total(residual * precond)
            direction = precond + later / now * direction
            now = later
    return solution


def first_pairs(array, axis):
    return lax.ppermute(array, axis, [(i, i ^ 1) for i in range(lax.axis_size(axis))])


def second_pairs(array, axis, around):
    count = lax.axis_size(axis)
    pairs = [] if around else [(0, 0), (count - 1, count - 1)]
    for i in range(1, count if around else count - 1, 2):
        pairs += [(i, (i + 1) % count), ((i + 1) % count, i)]
    return lax.ppermute(array, axis, pairs)


def on_device(tracers, east, north, levels):
    to_first, to_second = edges(tracers, east, north, levels)
    second = second_pairs(to_second, "gx", True)
    first = first_pairs(to_first, "gx")
    own_rows, one, two, early, early_total = block(tracers, east, north, levels, to_first)
    own_edges, one, two, low, high = pack_edges(first, second, one, two)
    second = second_pairs(two, "gy", False)
    first = first_pairs(one, "gy")
    late, late_total, ends_new, ends_total = late_levels(tracers, east, north, levels, low, high)
    from_strips, fields, sums = operator(
        levels, low, high, own_rows, own_edges, first, second, early_total, late_total, ends_total,
        count=lax.axis_size("gy"),
    )
    sums = lax.all_to_all(sums, ("gx", "gy"), split_axis=0, concat_axis=0, tiled=True)
    new = place(early, late, ends_new, from_strips)
    pressure, sound = finish(sums, fields)
    pressure = lax.cond(sound[0] > 0.5, lambda: pressure, lambda: careful(levels, fields))
    return new, pressure


def solution(mesh):
    placed = (P(None, None, "gx", "gy"), P(None, "gx", "gy"), P(None, "gx", "gy"), P("gx", "gy"))
    return jax.shard_map(
        on_device,
        mesh=mesh,
        in_specs=placed,
        out_specs=(P(None, None, "gx", "gy"), P("gx", "gy")),
        check_vma=False,
    )
```
